32 devices in a mesh: section: 2 (over core), wide: 4 (over z), tensor: 4 (over y, x).
Axes of the slice: x: 2, y: 2, z: 4, core: 2. Of those that a mesh axis runs over, the one named last changes fastest.
Arguments:
- inputs: bfloat16 [2, 1, 4096, 768], P(None, None, 'wide'), may hold values from -6 to 6
- target: bfloat16 [2, 1, 4096, 768], P(None, None, 'wide'), may hold values from -1.1953125 to 1.1953125
- pad_mask: int32 [2, 1, 4096], replicated, may hold values from 0 to 1, as said below
- loss_mask: int32 [2, 1, 4096], replicated, may hold values from 0 to 1, as said below
- rand_blocks: int32 [2, 12, 64, 3], P('section', 'tensor'), may hold values from 0 to 63, as said below
- w_query: bfloat16 [2, 768, 768], P('section', None, 'tensor'), may hold values from -0.21875 to 0.21875
- b_query: bfloat16 [2, 768], P('section', 'tensor'), may hold values from -3 to 3
- w_key: bfloat16 [2, 768, 768], P('section', None, 'tensor'), may hold values from -0.21875 to 0.21875
- w_value: bfloat16 [2, 768, 768], P('section', None, 'tensor'), may hold values from -0.21875 to 0.21875
- b_value: bfloat16 [2, 768], P('section', 'tensor'), may hold values from -1.1953125 to 1.1953125
- w_out: bfloat16 [2, 768, 768], P('section', 'tensor'), may hold values from -0.875 to 0.875
- b_out: bfloat16 [2, 768], P('section'), may hold values from -3 to 3
- ln1_gain: bfloat16 [2, 768], P('section'), may hold values from 0.5 to 1.5
- ln1_bias: bfloat16 [2, 768], P('section'), may hold values from -1.796875 to 1.796875
- w_in: bfloat16 [2, 768, 3072], P('section', None, 'tensor'), may hold values from -0.21875 to 0.21875
- b_in: bfloat16 [2, 3072], P('section', 'tensor'), may hold values from -3 to 3
- w_ffn: bfloat16 [2, 3072, 768], P('section', 'tensor'), may hold values from -0.109375 to 0.109375
- b_ffn: bfloat16 [2, 768], P('section'), may hold values from -1.796875 to 1.796875
- ln2_gain: bfloat16 [2, 768], P('section'), may hold values from 0.5 to 1.5
- ln2_bias: bfloat16 [2, 768], P('section'), may hold values from -1.796875 to 1.796875
Outputs:
- layer_ends: bfloat16 [2, 2, 1, 4096, 768], P('section', None, None, 'wide')
- grad_w_query: float32 [2, 768, 768], P('section', None, 'tensor')
- grad_b_query: float32 [2, 768], P('section', 'tensor')
- grad_w_key: float32 [2, 768, 768], P('section', None, 'tensor')
- grad_w_value: float32 [2, 768, 768], P('section', None, 'tensor')
- grad_b_value: float32 [2, 768], P('section', 'tensor')
- grad_w_out: float32 [2, 768, 768], P('section', 'tensor')
- grad_b_out: float32 [2, 768], P('section')
- grad_ln1_gain: float32 [2, 768], P('section')
- grad_ln1_bias: float32 [2, 768], P('section')
- grad_w_in: float32 [2, 768, 3072], P('section', None, 'tensor')
- grad_b_in: float32 [2, 3072], P('section', 'tensor')
- grad_w_ffn: float32 [2, 3072, 768], P('section', 'tensor')
- grad_b_ffn: float32 [2, 768], P('section')
- grad_ln2_gain: float32 [2, 768], P('section')
- grad_ln2_bias: float32 [2, 768], P('section')
The draws below stay inside these ranges and needn't reach their ends.
Inputs may be any that keep to these rules, and one draw needn't show every extreme that they name: `pad_mask`: real tokens form a prefix of each sequence of at least 2048 tokens; at least one sequence of the run has no padding. `loss_mask`: the first token of every sequence is marked. `rand_blocks`: for every layer, every index i of wide (block rows i * 16 to (i + 1) * 16 - 1) and every group of 3 consecutive heads, at most 36 of those rows' random blocks lie in the blocks of any one index of wide (blocks j * 16 to (j + 1) * 16 - 1), and exactly 36 in some.
All inputs are finite; a program needn't handle non-finite values.
Results may differ from the reference program's by a relative error of at most 0.023.
Values may be sent and summed in bfloat16 or wider, within the bound.
A program may use at most 384 MiB of HBM per device.

```python
from functools import partial
import jax
import jax.numpy as jnp
from jax import lax

D = 768
HEADS = 12
HEAD_WIDTH = 64
FF = 3072
BLK = 64
RAND = 3
MB = 2
SEQS = 1
LAYERS = 2
H_DEV = 3
BLK_DEV = 16
NB = 64
SEQLEN = 4096
N_WIDE = 4


def draw_pad_mask(key, part):
    key = jax.random.fold_in(key, 3)
    key_len, key_full = jax.random.split(key)
    lengths = jax.random.randint(key_len, (MB, SEQS), SEQLEN // 2, SEQLEN + 1)
    full_pick = jax.random.randint(key_full, (), 0, MB * SEQS)
    flat_ids = jnp.arange(MB * SEQS).reshape(MB, SEQS)
    lengths = jnp.where(flat_ids == full_pick, SEQLEN, lengths)
    return (jnp.arange(SEQLEN)[None, None, :] < lengths[:, :, None]).astype(jnp.int32)


def draw_loss_mask(key, part):
    key = jax.random.fold_in(key, 5)
    position = jnp.arange(SEQLEN, dtype=jnp.int32)
    chance = 500 + 2000 * position // (SEQLEN - 1)
    rolled = jax.random.randint(key, (MB, SEQS, SEQLEN), 0, 10000)
    marked = (rolled < chance[None, None, :]) | (position == 0)[None, None, :]
    return marked.astype(jnp.int32)


def draw_rand_blocks(key, part):
    key = jax.random.fold_in(key, 7)
    groups = HEADS // H_DEV
    slot_count = H_DEV * BLK_DEV * RAND
    key_one, key_two, key_three = jax.random.split(key, 3)
    device_scores = jax.random.randint(key_one, (LAYERS, N_WIDE, groups, N_WIDE), 0, 1 << 20) * N_WIDE + jnp.arange(N_WIDE)
    device_order = jnp.argsort(device_scores, axis=-1).astype(jnp.int32)
    slot_scores = jax.random.randint(key_two, (LAYERS, N_WIDE, groups, slot_count), 0, 1 << 20) * slot_count + jnp.arange(slot_count)
    slot_order = jnp.argsort(slot_scores, axis=-1).astype(jnp.int32)
    position = slot_order % N_WIDE
    owners = jnp.take_along_axis(device_order, position, axis=-1)
    local_block = jax.random.randint(key_three, (LAYERS, N_WIDE, groups, slot_count), 0, BLK_DEV)
    block_id = owners * BLK_DEV + local_block
    shaped = block_id.reshape(LAYERS, N_WIDE, groups, H_DEV, BLK_DEV, RAND)
    return shaped.transpose(0, 2, 3, 1, 4, 5).reshape(LAYERS, HEADS, NB, RAND).astype(jnp.int32)


def levels(stream_key, dims, shards, least, largest):
    def one(dim, blocks):
        steps = jax.random.uniform(jax.random.fold_in(jax.random.fold_in(stream_key, 6), dim), (blocks,), jnp.float32, least / len(shards), largest / len(shards))
        return jnp.repeat(jnp.exp(steps), dims[dim] // blocks).reshape((-1,) + (1,) * (len(dims) - dim - 1))

    gain = one(*shards[0])
    for cut in shards[1:]:
        gain = gain * one(*cut)
    return gain


def bell_draw(stream_key, extent, width, most, cuts=(), kind=jnp.bfloat16):
    values = jax.random.normal(stream_key, extent, jnp.float32) * width
    if len(cuts) > 0:
        values = levels(stream_key, extent, cuts, -0.22, 0.18) * values
    return jnp.clip(values, min=-most, max=most).astype(kind)


def setup_inputs(seed: int = 0) -> dict:
    streams_of = jax.random.split(jax.random.key(seed), 21)
    inputs = bell_draw(streams_of[0], (MB, SEQS, SEQLEN, D), 1.0, 6.0, ((2, 4),))
    target = bell_draw(streams_of[1], (MB, SEQS, SEQLEN, D), 0.2, 1.1953125, ((2, 4),))
    pad_mask = draw_pad_mask(jax.random.fold_in(streams_of[20], 71), 0)
    loss_mask = draw_loss_mask(jax.random.fold_in(streams_of[20], 71), 0)
    rand_blocks = draw_rand_blocks(jax.random.fold_in(streams_of[20], 71), 0)
    w_query = bell_draw(streams_of[5], (LAYERS, D, D), D ** -0.5, 0.21875, ((0, 2), (2, 4)))
    b_query = bell_draw(streams_of[6], (LAYERS, D), 0.5, 3.0, ((0, 2), (1, 4)))
    w_key = bell_draw(streams_of[7], (LAYERS, D, D), D ** -0.5, 0.21875, ((0, 2), (2, 4)))
    w_value = bell_draw(streams_of[8], (LAYERS, D, D), D ** -0.5, 0.21875, ((0, 2), (2, 4)))
    b_value = bell_draw(streams_of[9], (LAYERS, D), 0.2, 1.1953125, ((0, 2), (1, 4)))
    w_out = bell_draw(streams_of[10], (LAYERS, D, D), (max(1, D // 16)) ** -0.5, 0.875, ((0, 2), (1, 4)))
    b_out = bell_draw(streams_of[11], (LAYERS, D), 0.5, 3.0, ((0, 2),))
    ln1_gain = jnp.clip(1.0 + 0.1 * jax.random.normal(streams_of[12], (LAYERS, D), jnp.float32), 0.5, 1.5).astype(jnp.bfloat16)
    ln1_bias = bell_draw(streams_of[13], (LAYERS, D), 0.3, 1.796875, ((0, 2),))
    w_in = bell_draw(streams_of[14], (LAYERS, D, FF), D ** -0.5, 0.21875, ((0, 2), (2, 4)))
    b_in = bell_draw(streams_of[15], (LAYERS, FF), 0.5, 3.0, ((0, 2), (1, 4)))
    w_ffn = bell_draw(streams_of[16], (LAYERS, FF, D), FF ** -0.5, 0.109375, ((0, 2), (1, 4)))
    b_ffn = bell_draw(streams_of[17], (LAYERS, D), 0.3, 1.796875, ((0, 2),))
    ln2_gain = jnp.clip(1.0 + 0.1 * jax.random.normal(streams_of[18], (LAYERS, D), jnp.float32), 0.5, 1.5).astype(jnp.bfloat16)
    ln2_bias = bell_draw(streams_of[19], (LAYERS, D), 0.3, 1.796875, ((0, 2),))
    return {"inputs": inputs, "target": target, "pad_mask": pad_mask, "loss_mask": loss_mask, "rand_blocks": rand_blocks, "w_query": w_query, "b_query": b_query, "w_key": w_key, "w_value": w_value, "b_value": b_value, "w_out": w_out, "b_out": b_out, "ln1_gain": ln1_gain, "ln1_bias": ln1_bias, "w_in": w_in, "b_in": b_in, "w_ffn": w_ffn, "b_ffn": b_ffn, "ln2_gain": ln2_gain, "ln2_bias": ln2_bias}


EPSILON = 1e-06
NEG_FILL = -1e+30
HIGH_PRECISION = lax.Precision.HIGHEST

@jax.custom_vjp
def low(v):
    return lax.optimization_barrier(v.astype(jnp.bfloat16)).astype(jnp.float32)

@jax.custom_vjp
def low_back(v):
    return v

def low_keep(v):
    return (low(v), None)

def low_pass(kept, grad):
    return (grad,)

def back_keep(v):
    return (v, None)

def back_low(kept, grad):
    return (low(grad),)
low.defvjp(low_keep, low_pass)
low_back.defvjp(back_keep, back_low)

def normalize(values, gain_vec, shift_vec):
    center = values - lax.optimization_barrier(jnp.mean(values, axis=-1, keepdims=True))
    variance = lax.optimization_barrier(jnp.mean(center * center, axis=-1, keepdims=True))
    return center * lax.rsqrt(variance + EPSILON) * gain_vec + shift_vec

def block_table(rand_rows, first_row, block_total):
    head_count, row_count, pick_count = rand_rows.shape
    row_ids = first_row + jnp.arange(row_count, dtype=jnp.int32)[:, None]
    fixed_ids = jnp.concatenate([row_ids - 1, row_ids, row_ids + 1, jnp.zeros_like(row_ids), jnp.ones_like(row_ids)], axis=1)
    block_ids = jnp.concatenate([jnp.broadcast_to(fixed_ids[None], (head_count, row_count, 5)), rand_rows], axis=2)
    slot_ids = jnp.arange(5 + pick_count)
    same_block = block_ids[..., :, None] == block_ids[..., None, :]
    earlier = slot_ids[:, None] > slot_ids[None, :]
    repeated = jnp.any(same_block & earlier, axis=-1)
    allowed = (block_ids >= 0) & (block_ids < block_total) & jnp.logical_not(repeated)
    return (jnp.clip(block_ids, 0, block_total - 1), allowed)

def softmax_rows(score_matrix):
    peak = lax.optimization_barrier(jnp.max(score_matrix, axis=-1, keepdims=True))
    log_total = peak + jnp.log(lax.optimization_barrier(jnp.sum(jnp.exp(score_matrix - peak), axis=-1, keepdims=True)))
    return jnp.exp(score_matrix - log_total)

def head_attention(packed, key_ok):
    queries, key_rows, value_rows, block_ids, allowed = packed
    block_total = block_ids.shape[0]
    sequence_length = queries.shape[0]
    logit_scale = HEAD_WIDTH ** (-0.5)
    query_block_tiles = queries.reshape(block_total, BLK, HEAD_WIDTH)
    key_block_tiles = key_rows.reshape(block_total, BLK, HEAD_WIDTH)[block_ids]
    value_block_tiles = value_rows.reshape(block_total, BLK, HEAD_WIDTH)[block_ids]
    ok_blocks = key_ok.reshape(block_total, BLK)[block_ids] & allowed[:, :, None]
    score_matrix = jnp.einsum('scw,sngw->scng', query_block_tiles, key_block_tiles, precision=HIGH_PRECISION) * logit_scale
    score_matrix = low_back(score_matrix)
    score_matrix = jnp.where(ok_blocks[:, None], score_matrix, NEG_FILL).reshape(block_total, BLK, -1)
    attention_weights = low(softmax_rows(score_matrix)).reshape(block_total, BLK, -1, BLK)
    sparse_output = jnp.einsum('sagn,sgnc->sac', attention_weights, value_block_tiles, precision=HIGH_PRECISION).reshape(sequence_length, HEAD_WIDTH)
    glob_rows = queries[:2 * BLK]
    glob_scores = jnp.dot(glob_rows, key_rows.T, precision=HIGH_PRECISION) * logit_scale
    glob_scores = jnp.where(key_ok[None, :], glob_scores, NEG_FILL)
    glob_out = jnp.dot(softmax_rows(glob_scores), value_rows, precision=HIGH_PRECISION)
    return jnp.concatenate([glob_out, sparse_output[2 * BLK:]], axis=0)

def one_layer(layer_in, layer_params, block_ids, allowed, key_ok):
    w_query, b_query, w_key, w_value, b_value, w_out, b_out, gain_one, bias_one, w_in, b_in, w_ffn, b_ffn, gain_two, bias_two = layer_params
    sequence_length = layer_in.shape[0]
    queries = low_back(low(jnp.dot(layer_in, w_query, precision=HIGH_PRECISION) + b_query))
    key_rows = low_back(low(jnp.dot(layer_in, w_key, precision=HIGH_PRECISION)))
    value_rows = low_back(low(jnp.dot(layer_in, w_value, precision=HIGH_PRECISION) + b_value))

    def split_heads(matrix):
        return matrix.reshape(sequence_length, HEADS, HEAD_WIDTH).transpose(1, 0, 2)
    head_fn = jax.checkpoint(partial(head_attention, key_ok=key_ok))
    per_head = lax.map(head_fn, (split_heads(queries), split_heads(key_rows), split_heads(value_rows), block_ids, allowed))
    attended = low_back(low(per_head.transpose(1, 0, 2).reshape(sequence_length, HEADS * HEAD_WIDTH)))
    branch = low_back(jnp.dot(attended, w_out, precision=HIGH_PRECISION))
    mixed = low(normalize(layer_in + branch + b_out, gain_one, bias_one))
    hidden = low_back(jnp.dot(mixed, w_in, precision=HIGH_PRECISION) + b_in)
    active = low(jax.nn.gelu(hidden, approximate=True))
    branch_two = low_back(jnp.dot(active, w_ffn, precision=HIGH_PRECISION))
    return normalize(mixed + branch_two + b_ffn, gain_two, bias_two)

def reference(inputs, target, pad_mask, loss_mask, rand_blocks, w_query, b_query, w_key, w_value, b_value, w_out, b_out, ln1_gain, ln1_bias, w_in, b_in, w_ffn, b_ffn, ln2_gain, ln2_bias):
    stacked = tuple((param.astype(jnp.float32) for param in (w_query, b_query, w_key, w_value, b_value, w_out, b_out, ln1_gain, ln1_bias, w_in, b_in, w_ffn, b_ffn, ln2_gain, ln2_bias)))
    key_ok = (pad_mask > 0).reshape(MB * SEQS, SEQLEN)
    table_one = block_table(rand_blocks[0], 0, NB)
    table_two = block_table(rand_blocks[1], 0, NB)

    def forward(x_all, *layer_params):
        first = tuple((param[0] for param in layer_params))
        second = tuple((param[1] for param in layer_params))

        def per_sequence(carry, packed):
            layer_in, ok_row = packed
            middle = low_back(low(one_layer(layer_in, first, table_one[0], table_one[1], ok_row)))
            return (carry, one_layer(middle, second, table_two[0], table_two[1], ok_row))
        carry_end, result = lax.scan(jax.checkpoint(per_sequence), jnp.zeros((), jnp.float32), (x_all, key_ok))
        return result
    x_all = inputs.astype(jnp.float32).reshape(MB * SEQS, SEQLEN, D)
    result, pullback = jax.vjp(forward, x_all, *stacked)
    weight_all = (loss_mask * pad_mask).astype(jnp.float32)
    counts = lax.optimization_barrier(jnp.sum(weight_all, axis=(1, 2)))
    factor = SEQS * SEQLEN / counts
    cotangent = (weight_all * factor[:, None, None])[..., None] * target.astype(jnp.float32)
    grads = pullback(cotangent.reshape(MB * SEQS, SEQLEN, D))
    layer_ends = jnp.stack([grads[0], result]).reshape(2, MB, SEQS, SEQLEN, D).astype(jnp.bfloat16)
    return (layer_ends, grads[1], grads[2], grads[3], grads[4], grads[5], grads[6], grads[7], grads[8], grads[9], grads[10], grads[11], grads[12], grads[13], grads[14], grads[15])
```

```python
import functools

import jax
import jax.numpy as jnp
from jax import lax
from jax.experimental import pallas as pl
from jax.experimental.pallas import tpu as pltpu
from jax.sharding import PartitionSpec as P

HW = 64
BLK = 64
EPS = 1e-06
NEG = -1e30
MESH = pl.DeviceIdType.MESH
F32 = jnp.float32
BF16 = jnp.bfloat16
VMEM_BYTES = 56 * 1024 * 1024
GELU_C = 0.7978845608
GELU_A = 0.044715
NT_DIMS = (((1,), (1,)), ((), ()))
TN_DIMS = (((0,), (0,)), ((), ()))
ORDER = (3, 1, 2)
PIECE = 144
LAG = 1


def dot(a, b):
    return jnp.dot(a, b, preferred_element_type=F32)


def dot_nt(a, b):
    return lax.dot_general(a, b, NT_DIMS, preferred_element_type=F32)


def dot_tn(a, b):
    return lax.dot_general(a, b, TN_DIMS, preferred_element_type=F32)


def vmem():
    return pl.BlockSpec(memory_space=pltpu.VMEM)


def anywhere():
    return pl.BlockSpec(memory_space=pl.ANY)


def whole(*shape):
    return pl.BlockSpec(shape, lambda i: (0,) * len(shape))


def of_layer(array, layer):
    return pl.BlockSpec((None,) + array.shape[1:], lambda i: (layer,) + (0,) * (array.ndim - 1))


def remote(src, dst, send_sem, recv_sem, device):
    return pltpu.make_async_remote_copy(
        src_ref=src,
        dst_ref=dst,
        send_sem=send_sem,
        recv_sem=recv_sem,
        device_id=device,
        device_id_type=MESH,
    )


def tensor_peer(me, offset):
    if offset == 1:
        return me + 1 - 2 * lax.rem(me, 2)
    if offset == 2:
        return lax.rem(me + 2, 4)
    return 3 - me


def tensor_barrier(me):
    barrier = pltpu.get_barrier_semaphore()
    for offset in (1, 2, 3):
        pl.semaphore_signal(
            barrier, inc=1, device_id={"tensor": tensor_peer(me, offset)}, device_id_type=MESH
        )
    return barrier


def params(collective_id=None):
    if collective_id is None:
        return pltpu.CompilerParams(vmem_limit_bytes=VMEM_BYTES)
    return pltpu.CompilerParams(
        vmem_limit_bytes=VMEM_BYTES, collective_id=collective_id, has_side_effects=True
    )


def key_blocks(ids_ref, layer, head, row, first, total):
    b = first + row
    start = jnp.clip(b - 1, 0, total - 3)
    window = [start, start + 1, start + 2]
    r = [ids_ref[layer, head, b * 3 + k] for k in range(3)]

    def far(block):
        return (block < b - 1) | (block > b + 1)

    fresh = [far(k) & (k >= 2) for k in r]
    allowed = [jnp.logical_not(far(k)) for k in window]
    allowed += [far(jnp.int32(0)), far(jnp.int32(1))]
    allowed += [fresh[0], fresh[1] & (r[1] != r[0]), fresh[2] & (r[2] != r[0]) & (r[2] != r[1])]
    return window + [jnp.int32(0), jnp.int32(1)] + r, allowed


def back_blocks(ids_ref, layer, head, b, total):
    blocks, allowed = key_blocks(ids_ref, layer, head, 0, b, total)
    window = [jnp.maximum(b - 1, 0), b, jnp.minimum(b + 1, total - 1)]
    return window + blocks[3:], [b >= 1, b >= 0, b + 1 < total] + allowed[3:]


def key_bias(blocks, allowed, length):
    lane = lax.broadcasted_iota(jnp.int32, (1, 8 * BLK), 1)
    slot = lane // BLK
    limit = jnp.zeros((1, 8 * BLK), jnp.int32)
    for s in range(8):
        tokens = jnp.where(allowed[s], jnp.clip(length - blocks[s] * BLK, 0, BLK), 0)
        limit = jnp.where(slot == s, tokens, limit)
    return jnp.where(lane - slot * BLK < limit, 0.0, NEG)


def gathered(kv_ref, blocks):
    window = kv_ref[pl.ds(blocks[0], 3)].reshape(3 * BLK, -1)
    ends = kv_ref[0:2].reshape(2 * BLK, -1)
    return jnp.concatenate([window, ends] + [kv_ref[k] for k in blocks[5:]], axis=0)


def grouping(rows_here):
    return max(u for u in (4, 3, 2, 1) if rows_here % u == 0)


def wide_barrier(me, count):
    barrier = pltpu.get_barrier_semaphore()
    for side in (1, count - 1):
        pl.semaphore_signal(
            barrier,
            inc=1,
            device_id={"wide": lax.rem(me + side, count)},
            device_id_type=MESH,
        )
    return barrier


def softmax_values(s, keys):
    peak = jnp.max(s, axis=-1, keepdims=True)
    e = jnp.exp(s - peak)
    mass = jnp.sum(e, axis=-1, keepdims=True)
    return dot(e.astype(BF16), keys) / mass, peak + jnp.log(mass)


def gather_attend(
    count, heads, layer, x_ref, wt_ref, bias, ids_ref, len_ref, outs, scratch, ready, finished
):
    q_ref, kv_ref, att_ref, lse_ref, top_ref = outs
    held, (save, send_r, recv_r, send_l, recv_l) = scratch[:heads], scratch[heads:]
    me = lax.axis_index("wide")
    tok = x_ref.shape[0]
    right, left = {"wide": lax.rem(me + 1, count)}, {"wide": lax.rem(me + count - 1, count)}
    pair = 2 * HW
    wide = heads * pair
    has_right, has_left = me < count - 1, me > 0
    length = len_ref[0]
    rows_here = tok // BLK
    total = held[0].shape[0]
    unit = grouping(rows_here)
    groups = rows_here // unit

    def rows(shard):
        return pl.ds(shard * rows_here, rows_here)

    kv = dot_nt(x_ref[...], wt_ref[wide:, :]) + bias[:, wide:]
    for h in range(heads):
        own = kv[:, h * pair : (h + 1) * pair].astype(BF16)
        held[h][rows(me)] = own.reshape(rows_here, BLK, pair)
    ready()

    def copy_r(h, shard, step):
        part = held[h].at[rows(shard)]
        return remote(part, part, send_r.at[h, step], recv_r.at[h, shard], right)

    def copy_l(h, shard, step):
        part = held[h].at[rows(shard)]
        return remote(part, part, send_l.at[h, step], recv_l.at[h, shard], left)

    for h in range(heads):

        @pl.when(has_right)
        def _():
            copy_r(h, me, 0).start()

        @pl.when(has_left)
        def _():
            copy_l(h, me, 0).start()

    q = dot_nt(x_ref[...], wt_ref[:wide, :]) + bias[:, :wide]
    q_ref[...] = q.astype(BF16)

    def forward(h, step):
        shard_r, shard_l = me - step, me + step

        @pl.when(shard_r >= 0)
        def _():
            copy_r(h, shard_r, step).wait_recv()

            @pl.when(has_right)
            def _():
                copy_r(h, shard_r, step).start()

        @pl.when(shard_l < count)
        def _():
            copy_l(h, shard_l, step).wait_recv()

            @pl.when(has_left)
            def _():
                copy_l(h, shard_l, step).start()

    def forward_from(h, first):
        def step(k, carry):
            forward(h, k)
            return carry

        lax.fori_loop(first, count, step, 0)

    forward_from(0, 1)
    for h in range(heads):
        pltpu.make_async_copy(held[h], kv_ref.at[h], save.at[h]).start()
        cols = slice(h * pair, (h + 1) * pair)

        def group(g, carry):
            for u in range(unit):
                row = g * unit + u
                here = pl.ds(pl.multiple_of(row * BLK, BLK), BLK)
                blocks, allowed = key_blocks(ids_ref, layer, h, row, me * rows_here, total)
                keys = gathered(held[h], blocks)
                s = dot_nt(q_ref[here, cols], keys) + key_bias(blocks, allowed, length)
                o, lse = softmax_values(s, keys)
                att_ref[here, cols] = o.astype(BF16)
                lse_ref[h, here, :] = lse
            if h + 1 < heads:

                @pl.when(g + 1 < count)
                def _():
                    forward(h + 1, g + 1)

            return carry

        lax.fori_loop(0, groups, group, 0)
        if h + 1 < heads:
            forward_from(h + 1, groups + 1)

        @pl.when(me == 0)
        def _():
            keys = held[h][...].reshape(total * BLK, pair)
            token = lax.broadcasted_iota(jnp.int32, (1, keys.shape[0]), 1)
            s = dot_nt(q_ref[0 : 2 * BLK, cols], keys) + jnp.where(token < length, 0.0, NEG)
            o, lse = softmax_values(s, keys)
            att_ref[0 : 2 * BLK, cols] = o.astype(BF16)
            lse_ref[h, 0 : 2 * BLK, :] = lse
            top_ref[h] = o

        @pl.when(me != 0)
        def _():
            top_ref[h] = jnp.zeros((2 * BLK, pair), F32)

    finished()

    def drain(step, carry):
        shard_r, shard_l = me - step, me + step
        for h in range(heads):

            @pl.when((shard_r >= 0) & has_right)
            def _():
                copy_r(h, shard_r, step).wait_send()

            @pl.when((shard_l < count) & has_left)
            def _():
                copy_l(h, shard_l, step).wait_send()

        return carry

    lax.fori_loop(0, count, drain, 0)
    for h in range(heads):
        pltpu.make_async_copy(held[h], kv_ref.at[h], save.at[h]).wait()


def attend_outs(count, heads, tok):
    pair = 2 * HW
    shapes = [
        jax.ShapeDtypeStruct((tok, heads * pair), BF16),
        jax.ShapeDtypeStruct((heads, count * tok // BLK, BLK, pair), BF16),
        jax.ShapeDtypeStruct((tok, heads * pair), BF16),
        jax.ShapeDtypeStruct((heads, tok, 1), F32),
        jax.ShapeDtypeStruct((heads, 2 * BLK, pair), F32),
    ]
    specs = [anywhere() if i == 1 else whole(*a.shape) for i, a in enumerate(shapes)]
    return shapes, specs


def gather_scratch(count, heads, tok):
    return (
        [pltpu.VMEM((count * tok // BLK, BLK, 2 * HW), BF16)] * heads
        + [pltpu.SemaphoreType.DMA((heads,))]
        + [pltpu.SemaphoreType.DMA((heads, count))] * 4
    )


def scalars():
    return pl.BlockSpec(memory_space=pltpu.SMEM)


def begin_kernel(
    count,
    heads,
    ids_ref,
    len_ref,
    inputs_ref,
    wq_ref,
    wk_ref,
    wv_ref,
    win_ref,
    wffn_ref,
    wout_ref,
    bq_ref,
    bv_ref,
    bout_ref,
    g1_ref,
    b1_ref,
    bin_ref,
    bffn_ref,
    g2_ref,
    b2_ref,
    x_ref,
    q_ref,
    kv_ref,
    att_ref,
    lse_ref,
    top_ref,
    wt_ref,
    vall_ref,
    win_all_ref,
    wffn_all_ref,
    wout_all_ref,
    turn,
    x_sem,
    keep,
    send,
    recv,
    *scratch,
):
    section = lax.axis_index("section")
    other = {"section": 1 - section}
    barrier = wide_barrier(lax.axis_index("wide"), count)
    pl.semaphore_signal(barrier, inc=1, device_id=other, device_id_type=MESH)
    load = pltpu.make_async_copy(inputs_ref.at[section, 0], x_ref, x_sem)
    load.start()
    wide = heads * 2 * HW
    scale = jnp.asarray(0.125, BF16)
    none = jnp.zeros((HW, x_ref.shape[1]), BF16)
    row = []
    for h in range(heads):
        at, cut = h * 2 * HW, slice(h * HW, (h + 1) * HW)
        wt_ref[section, at : at + HW, :] = wq_ref[cut, :] * scale
        wt_ref[section, at + HW : at + 2 * HW, :] = none
        wt_ref[section, wide + at : wide + at + HW, :] = wk_ref[cut, :]
        wt_ref[section, wide + at + HW : wide + at + 2 * HW, :] = wv_ref[cut, :]
        row += [bq_ref[:, cut].astype(F32) * 0.125, jnp.zeros((1, HW), F32)]
    for h in range(heads):
        row += [jnp.zeros((1, HW), F32), bv_ref[:, h * HW : (h + 1) * HW].astype(F32)]
    vall_ref[section, 0:1, :] = jnp.concatenate(row, axis=1)
    for i, ref in enumerate((bout_ref, g1_ref, b1_ref, bin_ref, bffn_ref, g2_ref, b2_ref)):
        vall_ref[section, i + 1 : i + 2, :] = ref[...].astype(F32)
    pl.semaphore_wait(barrier, 3)

    pairs = [
        (wt_ref.at[section], wt_ref.at[section]),
        (vall_ref.at[section], vall_ref.at[section]),
        (win_ref, win_all_ref.at[section]),
        (wffn_ref, wffn_all_ref.at[section]),
        (wout_ref, wout_all_ref.at[section]),
    ]
    swaps = [remote(src, dst, send.at[i], recv.at[i], other) for i, (src, dst) in enumerate(pairs)]
    keeps = [
        pltpu.make_async_copy(src, dst, keep.at[i]) for i, (src, dst) in enumerate(pairs[2:])
    ]
    for copy in swaps + keeps:
        copy.start()
    load.wait()

    @pl.when(section == 1)
    def _():
        swaps[0].wait_recv()
        swaps[1].wait_recv()

    def ready():
        @pl.when(section == 1)
        def _():
            pl.semaphore_wait(turn, 1)

    def finished():
        @pl.when(section == 0)
        def _():
            pl.semaphore_signal(turn, inc=1, device_id={"section": 1}, device_id_type=MESH)

    gather_attend(
        count,
        heads,
        0,
        x_ref,
        wt_ref.at[0],
        vall_ref[0, 0:1, :],
        ids_ref,
        len_ref,
        (q_ref, kv_ref, att_ref, lse_ref, top_ref),
        scratch,
        ready,
        finished,
    )

    @pl.when(section == 0)
    def _():
        swaps[0].wait_recv()
        swaps[1].wait_recv()

    for copy in swaps[2:]:
        copy.wait_recv()
    for copy in swaps:
        copy.wait_send()
    for copy in keeps:
        copy.wait()


def begin(ids, length, inputs, matrices, vectors, count, heads, collective_id):
    _, _, tok, width = inputs.shape
    wide = heads * 2 * HW
    narrow = heads * HW
    both = [(2, width, width), (2, width, width), (2, narrow, width)]
    shapes, specs = attend_outs(count, heads, tok)
    return pl.pallas_call(
        functools.partial(begin_kernel, count, heads),
        grid=(1,),
        out_shape=[jax.ShapeDtypeStruct((tok, width), BF16)]
        + shapes
        + [
            jax.ShapeDtypeStruct((2, 2 * wide, width), BF16),
            jax.ShapeDtypeStruct((2, 8, width), F32),
        ]
        + [jax.ShapeDtypeStruct(shape, BF16) for shape in both],
        in_specs=[scalars(), scalars(), anywhere()]
        + [whole(*m.shape) for m in matrices]
        + [whole(*v.shape) for v in vectors],
        out_specs=[whole(tok, width)]
        + specs
        + [whole(2, 2 * wide, width), whole(2, 8, width)]
        + [anywhere()] * 3,
        scratch_shapes=[
            pltpu.SemaphoreType.REGULAR,
            pltpu.SemaphoreType.DMA,
            pltpu.SemaphoreType.DMA((3,)),
            pltpu.SemaphoreType.DMA((5,)),
            pltpu.SemaphoreType.DMA((5,)),
        ]
        + gather_scratch(count, heads, tok),
        compiler_params=params(collective_id),
        name="begin",
    )(ids, length, inputs, *matrices, *vectors)


def project_kernel(count, heads, layer, ids_ref, len_ref, x_ref, wt_ref, v_ref, *refs):
    barrier = wide_barrier(lax.axis_index("wide"), count)
    gather_attend(
        count,
        heads,
        layer,
        x_ref,
        wt_ref,
        v_ref[0:1, :],
        ids_ref,
        len_ref,
        refs[:5],
        refs[5:],
        lambda: pl.semaphore_wait(barrier, 2),
        lambda: None,
    )


def project(ids, length, x, wt, vall, layer, count, heads, collective_id):
    tok, width = x.shape
    shapes, specs = attend_outs(count, heads, tok)
    return pl.pallas_call(
        functools.partial(project_kernel, count, heads, layer),
        grid=(1,),
        out_shape=shapes,
        in_specs=[scalars(), scalars(), whole(tok, width), of_layer(wt, layer), of_layer(vall, layer)],
        out_specs=specs,
        scratch_shapes=gather_scratch(count, heads, tok),
        compiler_params=params(collective_id),
        name="project",
    )(ids, length, x, wt, vall)


class Square:
    def __init__(self, me, own, width, blocks, send_buf, recv_buf, hold, send_sem, recv_sem):
        self.me = me
        self.x, self.y, self.d = (tensor_peer(me, k) for k in (1, 2, 3))
        self.own, self.sub, self.half = own, own // blocks, width // 2
        self.blocks = blocks
        self.send_buf, self.recv_buf, self.hold = send_buf, recv_buf, hold
        self.send_sem, self.recv_sem = send_sem, recv_sem
        self.used = []

    def rows(self, index, j, size=None):
        return pl.ds(pl.multiple_of(index * self.own + j * self.sub, 16), size or self.sub)

    def to(self, m):
        return {"tensor": self.x if m < 3 else self.y}

    def scatter(self, stage, j, m):
        slot = self.scatters.index(stage)
        return remote(
            self.send_buf.at[slot, j, m],
            self.recv_buf.at[slot, j, m],
            self.send_sem.at[stage, j, m],
            self.recv_sem.at[stage, j, m],
            self.to(m),
        )

    def put(self, stage, j, m, value):
        self.send_buf[self.scatters.index(stage), j, m] = value.astype(BF16)
        self.scatter(stage, j, m).start()
        self.used.append(self.scatter(stage, j, m))

    def got(self, stage, j, m):
        self.scatter(stage, j, m).wait_recv()
        return self.recv_buf[self.scatters.index(stage), j, m].astype(F32)

    def give_diagonal(self, stage, j, part):
        self.put(stage, j, 0, part[:, self.half :])
        self.put(stage, j, 3, part[:, : self.half])

    def give_x(self, stage, j, part):
        self.put(stage, j, 1, part[:, self.half :])
        self.hold[j, 0] = part[:, : self.half]

    def give_y(self, stage, j, part):
        self.put(stage, j, 4, part[:, : self.half])
        self.hold[j, 1] = part[:, self.half :]

    def relay_sum(self, stage, j):
        self.put(stage, j, 2, self.hold[j, 0] + self.got(stage, j, 3))
        self.put(stage, j, 5, self.hold[j, 1] + self.got(stage, j, 0))

    def total(self, stage, j, own):
        left = own[:, : self.half] + self.got(stage, j, 4) + self.got(stage, j, 2)
        right = own[:, self.half :] + self.got(stage, j, 1) + self.got(stage, j, 5)
        return jnp.concatenate([left, right], axis=1)

    def gather(self, stage, j, m, ref, index, first):
        cols = pl.ds(0 if first else self.half, self.half)
        return remote(
            ref.at[self.rows(index, j), cols],
            ref.at[self.rows(index, j), cols],
            self.send_sem.at[stage, j, m],
            self.recv_sem.at[stage, j, m],
            self.to(m),
        )

    def send(self, copy):
        copy.start()
        self.used.append(copy)

    def share(self, stage, j, ref):
        for m, first in ((0, True), (3, False), (1, False), (4, True)):
            self.send(self.gather(stage, j, m, ref, self.me, first))

    def relay_share(self, stage, j, ref):
        self.gather(stage, j, 0, ref, self.x, True).wait_recv()
        self.send(self.gather(stage, j, 5, ref, self.x, True))
        self.gather(stage, j, 3, ref, self.y, False).wait_recv()
        self.send(self.gather(stage, j, 2, ref, self.y, False))

    def have_x(self, stage, j, ref):
        self.gather(stage, j, 1, ref, self.x, False).wait_recv()

    def have_y(self, stage, j, ref):
        self.gather(stage, j, 4, ref, self.y, True).wait_recv()

    def have_diagonal(self, stage, j, ref):
        self.gather(stage, j, 5, ref, self.d, True).wait_recv()
        self.gather(stage, j, 2, ref, self.d, False).wait_recv()

    def have_all(self, stage, j, ref):
        self.have_x(stage, j, ref)
        self.have_y(stage, j, ref)
        self.have_diagonal(stage, j, ref)

    def close(self):
        for copy in self.used:
            copy.wait_send()


def square_barrier(me):
    barrier = pltpu.get_barrier_semaphore()
    for offset in (1, 2):
        pl.semaphore_signal(
            barrier, inc=1, device_id={"tensor": tensor_peer(me, offset)}, device_id_type=MESH
        )
    return barrier


def sub_blocks(own):
    return 2 if own % 32 == 0 else 1


def square_scratch(scatters, stages, own, width):
    blocks = sub_blocks(own)
    buf = pltpu.VMEM((scatters, blocks, 6, own // blocks, width // 2), BF16)
    return [
        buf,
        buf,
        pltpu.VMEM((blocks, 2, own // blocks, width // 2), F32),
        pltpu.SemaphoreType.DMA((stages, blocks, 6)),
        pltpu.SemaphoreType.DMA((stages, blocks, 6)),
    ]


def norm_parts(values):
    center = values - jnp.mean(values, axis=-1, keepdims=True)
    rstd = lax.rsqrt(jnp.mean(center * center, axis=-1, keepdims=True) + EPS)
    return center * rstd, rstd


def dense_kernel(
    last,
    layer,
    att_ref,
    x_ref,
    wout_ref,
    v_ref,
    win_any,
    wffn_any,
    mixed_any,
    active_any,
    slope_any,
    r1_ref,
    r2_ref,
    out_ref,
    wout_pad,
    win_ref,
    wffn_ref,
    mixed_ref,
    active_ref,
    slope_ref,
    sems,
    *scratch,
):
    me = lax.axis_index("tensor")
    own, width = x_ref.shape[0] // 4, x_ref.shape[1]
    blocks = sub_blocks(own)
    barrier = square_barrier(me)
    sq = Square(me, own, width, blocks, *scratch)
    pad_heads(wout_ref, wout_pad)
    sq.scatters = (0, 2)
    loads = [
        pltpu.make_async_copy(src.at[layer], dst, sems.at[i])
        for i, (src, dst) in enumerate(((win_any, win_ref), (wffn_any, wffn_ref)))
    ]
    for load in loads:
        load.start()
    stores = [
        pltpu.make_async_copy(src, dst, sems.at[2 + i])
        for i, (src, dst) in enumerate(
            ((mixed_ref, mixed_any), (active_ref, active_any), (slope_ref, slope_any))
        )
    ]

    def local(j):
        return slice(j * sq.sub, (j + 1) * sq.sub)

    def branch(index, j):
        return dot(att_ref[sq.rows(index, j), :], wout_pad[...])

    for j in range(blocks):
        part = branch(sq.d, j)
        if j == 0:
            pl.semaphore_wait(barrier, 2)
        sq.give_diagonal(0, j, part)
    for j in range(blocks):
        sq.give_x(0, j, branch(sq.x, j))
        sq.give_y(0, j, branch(sq.y, j))
    for j in range(blocks):
        r1_ref[local(j), :] = (
            branch(me, j) + x_ref[sq.rows(me, j), :].astype(F32) + v_ref[1:2, :]
        )
        sq.relay_sum(0, j)
    for j in range(blocks):
        total = sq.total(0, j, r1_ref[local(j), :])
        r1_ref[local(j), :] = total
        mixed = (norm_parts(total)[0] * v_ref[2:3, :] + v_ref[3:4, :]).astype(BF16)
        mixed_ref[sq.rows(me, j), :] = mixed
        sq.share(1, j, mixed_ref)

    for load in loads:
        load.wait()

    def feed(index, j):
        here = sq.rows(index, j)
        u = dot(mixed_ref[here, :], win_ref[...]) + v_ref[4:5, :]
        th = jnp.tanh(GELU_C * (u + GELU_A * u * u * u))
        half = 0.5 * (1.0 + th)
        slope = half + 0.5 * u * (1.0 - th * th) * (GELU_C * (1.0 + 3.0 * GELU_A * u * u))
        slope_ref[here, :] = slope.astype(BF16)
        active = (u * half).astype(BF16)
        active_ref[here, :] = active
        return dot(active, wffn_ref[...])

    for j in range(blocks):
        r2_ref[local(j), :] = (
            feed(me, j) + mixed_ref[sq.rows(me, j), :].astype(F32) + v_ref[5:6, :]
        )
        sq.relay_share(1, j, mixed_ref)
    for j in range(blocks):
        sq.have_x(1, j, mixed_ref)
        sq.give_x(2, j, feed(sq.x, j))
        sq.have_y(1, j, mixed_ref)
        sq.give_y(2, j, feed(sq.y, j))
        sq.have_diagonal(1, j, mixed_ref)
        sq.give_diagonal(2, j, feed(sq.d, j))
    for store in stores:
        store.start()
    for j in range(blocks):
        sq.relay_sum(2, j)
    for j in range(blocks):
        total = sq.total(2, j, r2_ref[local(j), :])
        r2_ref[local(j), :] = total
        result = (norm_parts(total)[0] * v_ref[6:7, :] + v_ref[7:8, :]).astype(BF16)
        if last:
            out_ref[local(j), :] = result
        else:
            out_ref[sq.rows(me, j), :] = result
            sq.share(3, j, out_ref)
    if not last:
        for j in range(blocks):
            sq.relay_share(3, j, out_ref)
        for j in range(blocks):
            sq.have_all(3, j, out_ref)
    sq.close()
    for store in stores:
        store.wait()


def pad_heads(rows_ref, padded_ref):
    for h in range(rows_ref.shape[0] // HW):
        at = h * 2 * HW
        padded_ref[at : at + HW, :] = jnp.zeros((HW, rows_ref.shape[1]), rows_ref.dtype)
        padded_ref[at + HW : at + 2 * HW, :] = rows_ref[h * HW : (h + 1) * HW, :]


def dense(att, x, wout, win, wffn, vall, layer, collective_id):
    tok, width = x.shape
    own = tok // 4
    wide = att.shape[1]
    last = layer == 1
    out_rows = own if last else tok
    return pl.pallas_call(
        functools.partial(dense_kernel, last, layer),
        out_shape=[jax.ShapeDtypeStruct((tok, width), BF16)] * 3
        + [jax.ShapeDtypeStruct((own, width), F32)] * 2
        + [jax.ShapeDtypeStruct((out_rows, width), BF16)],
        grid=(1,),
        in_specs=[whole(tok, wide), whole(tok, width)]
        + [of_layer(a, layer) for a in (wout, vall)]
        + [anywhere()] * 2,
        out_specs=[anywhere()] * 3 + [whole(own, width)] * 2 + [whole(out_rows, width)],
        scratch_shapes=[
            pltpu.VMEM((wide, width), BF16),
            pltpu.VMEM((width, width), BF16),
            pltpu.VMEM((width, width), BF16),
            pltpu.VMEM((tok, width), BF16),
            pltpu.VMEM((tok, width), BF16),
            pltpu.VMEM((tok, width), BF16),
            pltpu.SemaphoreType.DMA((5,)),
        ]
        + square_scratch(2, 4, own, width),
        compiler_params=params(collective_id),
        name="dense",
    )(att, x, wout, vall, win, wffn)


def norm_back(values, grad, gain):
    n, rstd = norm_parts(values)
    f = grad * gain
    back = (
        f - jnp.mean(f, axis=-1, keepdims=True) - n * jnp.mean(f * n, axis=-1, keepdims=True)
    ) * rstd
    return back, n


def dense_back_kernel(
    count,
    with_chain,
    g_ref,
    weight_ref,
    r2_ref,
    r1_ref,
    wout_ref,
    v_ref,
    *refs,
):
    late_any, refs = refs[:6], refs[6:]
    if with_chain:
        old_any, gqkv_ref, refs = refs[0], refs[1], refs[2:]
    gw_ref, gv_ref, do_ref, dr1_ref = refs[:4]
    refs = refs[4:]
    if with_chain:
        up_ref, gqkv_sum, refs = refs[0], refs[1], refs[2:]
    late, late_sems = refs[:6], refs[6]
    wffn_ref, slope_ref, win_ref, active_ref, mixed_ref, att_ref = late
    refs = refs[7:]
    layer = 0 if with_chain else 1
    loads = [
        pltpu.make_async_copy(src.at[layer] if i in (0, 2) else src, dst, late_sems.at[i])
        for i, (src, dst) in enumerate(zip(late_any, late))
    ]
    for load in loads:
        load.start()
    db2, dh, db1, wout_pad, g_buf, g_sem = refs[:6]
    refs = refs[3:]
    me = lax.axis_index("tensor")
    wide_at = lax.axis_index("wide")
    section = lax.axis_index("section")
    own, width = r1_ref.shape
    wide = att_ref.shape[1]
    blocks = sub_blocks(own)
    barrier = square_barrier(me)
    sq = Square(me, own, width, blocks, *refs[3:8])
    sq.scatters = (1,)
    refs = refs[8:]
    if with_chain:
        old, old_sem, sems, landed, hand_sems, ready = refs
        line = Line(count)
        rows = old.shape[0]
        half = gqkv_sum.shape[0]

        def half_of(core):
            return pl.ds(pl.multiple_of(core * half, 16), half)

        def swap():
            return remote(
                gqkv_ref.at[half_of(1 - section)],
                landed,
                hand_sems.at[0],
                hand_sems.at[1],
                {"section": 1 - section},
            )

        load_old = pltpu.make_async_copy(
            old_any.at[pl.ds(pl.multiple_of(section * rows, 16), rows)], old, old_sem
        )
        load_old.start()
        for side in (1, count - 1):
            pl.semaphore_signal(
                barrier,
                inc=1,
                device_id={"wide": lax.rem(wide_at + side, count)},
                device_id_type=MESH,
            )

        def inwards(source):
            return remote(source, up_ref, sems.at[0], sems.at[1], line.inward)

    def down(values):
        return jnp.sum(values, axis=0, keepdims=True)

    def local(j):
        return slice(j * sq.sub, (j + 1) * sq.sub)

    if with_chain:

        def gradient(j):
            return g_ref[local(j), :].astype(F32)

    else:
        load = pltpu.make_async_copy(g_ref.at[section, 0, sq.rows(me, 0, own)], g_buf, g_sem)
        load.start()
        weight = weight_ref[section]
        count_all = jnp.sum(jnp.sum(weight, axis=1, keepdims=True), axis=0, keepdims=True)
        factor = (weight.shape[0] * weight.shape[1]) / count_all
        here = weight_ref[section, pl.ds(wide_at * 4 + me, 1), :]
        equal = lax.broadcasted_iota(jnp.int32, (own, own), 0) == lax.broadcasted_iota(
            jnp.int32, (own, own), 1
        )
        column = jnp.sum(jnp.where(equal, here, 0.0), axis=1, keepdims=True) * factor
        load.wait()

        def gradient(j):
            return g_buf[local(j), :].astype(F32) * column[local(j), :]

    pad_heads(wout_ref, wout_pad)
    d_gain, d_shift, d_bias = 0.0, 0.0, 0.0
    for j in range(blocks):
        grad = gradient(j)
        d_two, n_two = norm_back(r2_ref[local(j), :], grad, v_ref[6:7, :])
        db2[sq.rows(me, j), :] = d_two.astype(BF16)
        dr1_ref[local(j), :] = d_two
        if j == 0:
            if with_chain:
                greet(barrier, section, 4)
                tell_ready(ready, section)
            else:
                pl.semaphore_wait(barrier, 2)
        sq.share(0, j, db2)
        d_gain += down(grad * n_two)
        d_shift += down(grad)
        d_bias += down(d_two)
    gv_ref[6:7, :] = d_gain
    gv_ref[7:8, :] = d_shift
    gv_ref[5:6, :] = d_bias

    def feed(index, j):
        here = sq.rows(index, j)
        back = dot_nt(db2[here, :], wffn_ref[...]) * slope_ref[here, :].astype(F32)
        low = back.astype(BF16)
        dh[here, :] = low
        return dot_nt(low, win_ref[...])

    if with_chain:
        load_old.wait()

        @pl.when(line.no_outer)
        def _():
            inwards(old).start()

        @pl.when(section == 1)
        def _():
            swap().start()

    for load in loads[:3]:
        load.wait()
    for j in range(blocks):
        dr1_ref[local(j), :] += feed(me, j)
        sq.relay_share(0, j, db2)
    for j in range(blocks):
        sq.have_x(0, j, db2)
        sq.give_x(1, j, feed(sq.x, j))
        sq.have_y(0, j, db2)
        sq.give_y(1, j, feed(sq.y, j))
        sq.have_diagonal(0, j, db2)
        sq.give_diagonal(1, j, feed(sq.d, j))
    for j in range(blocks):
        sq.relay_sum(1, j)
    for load in loads[3:]:
        load.wait()
    step = 256
    for i in range(width // step):
        cols = slice(i * step, (i + 1) * step)
        gw_ref[width + i * step : width + (i + 1) * step, :] = dot_tn(
            active_ref[:, cols], db2[...]
        ).astype(BF16)
        gw_ref[cols, :] = dot_tn(mixed_ref[:, cols], dh[...]).astype(BF16)
    gv_ref[4:5, :] = down(dh[...].astype(F32))
    d_gain, d_shift, d_bias = 0.0, 0.0, 0.0
    for j in range(blocks):
        total = sq.total(1, j, dr1_ref[local(j), :])
        d_one, n_one = norm_back(r1_ref[local(j), :], total, v_ref[2:3, :])
        db1[sq.rows(me, j), :] = d_one.astype(BF16)
        sq.share(2, j, db1)
        dr1_ref[local(j), :] = d_one
        d_gain += down(total * n_one)
        d_shift += down(total)
        d_bias += down(d_one)
    gv_ref[2:3, :] = d_gain
    gv_ref[3:4, :] = d_shift
    gv_ref[1:2, :] = d_bias
    gv_ref[0:1, :] = jnp.zeros((1, width), F32)

    def attended_back(index, j):
        here = sq.rows(index, j)
        do_ref[here, :] = dot_nt(db1[here, :], wout_pad[...]).astype(BF16)

    for j in range(blocks):
        attended_back(me, j)
        sq.relay_share(2, j, db1)
    for j in range(blocks):
        sq.have_x(2, j, db1)
        attended_back(sq.x, j)
        sq.have_y(2, j, db1)
        attended_back(sq.y, j)
        sq.have_diagonal(2, j, db1)
        attended_back(sq.d, j)
    for h in range(wide // (2 * HW)):
        cols = slice(h * 2 * HW, (h + 1) * 2 * HW)
        gw_ref[2 * width + h * HW : 2 * width + (h + 1) * HW, :] = dot_tn(
            att_ref[:, cols], db1[...]
        )[HW:].astype(BF16)
    sq.close()
    if with_chain:
        await_ready(ready, section)

        @pl.when(section == 0)
        def _():
            swap().start()

        @pl.when(line.has_outer)
        def _():
            inwards(old).wait_recv()

            def add(i, carry):
                span = pl.ds(pl.multiple_of(i * PIECE, 16), PIECE)
                up_ref[span, :] = (up_ref[span, :].astype(F32) + old[span, :].astype(F32)).astype(BF16)
                return carry

            lax.fori_loop(0, rows // PIECE, add, 0)

        @pl.when(line.has_outer & line.not_middle)
        def _():
            inwards(up_ref).start()

        @pl.when(line.not_middle)
        def _():
            inwards(old).wait_send()

        swap().wait()
        gqkv_sum[...] = (
            gqkv_ref[half_of(section), :].astype(F32) + landed[...].astype(F32)
        ).astype(BF16)


def dense_back(
    g, weight, r2, r1, slope, active, mixed, att, wout, win, wffn, vall, layer, count, collective_id, old
):
    own, width = r1.shape
    tok, wide = att.shape
    gw_rows = 2 * width + wide // 2
    extra_out, extra_scratch = [], []
    if old:
        half = (old[0].shape[0] // 2, width)
        small = (old[1].shape[0] // 2, width)
        extra_out = [half, small]
        extra_scratch = [
            pltpu.VMEM(half, BF16),
            pltpu.SemaphoreType.DMA,
            pltpu.SemaphoreType.DMA((2,)),
            pltpu.VMEM(small, BF16),
            pltpu.SemaphoreType.DMA((2,)),
            pltpu.SemaphoreType.REGULAR,
        ]
    return pl.pallas_call(
        functools.partial(dense_back_kernel, count, bool(old)),
        out_shape=[
            jax.ShapeDtypeStruct((gw_rows, width), BF16),
            jax.ShapeDtypeStruct((8, width), F32),
            jax.ShapeDtypeStruct((tok, wide), BF16),
            jax.ShapeDtypeStruct((own, width), F32),
        ]
        + [jax.ShapeDtypeStruct(shape, BF16) for shape in extra_out],
        grid=(1,),
        in_specs=[whole(own, width) if old else anywhere(), whole(*weight.shape)]
        + [whole(own, width)] * 2
        + [of_layer(a, layer) for a in (wout, vall)]
        + [anywhere()] * 6
        + ([anywhere(), whole(*old[1].shape)] if old else []),
        out_specs=[
            whole(gw_rows, width),
            whole(8, width),
            whole(tok, wide),
            whole(own, width),
        ]
        + [whole(*shape) for shape in extra_out],
        scratch_shapes=[
            pltpu.VMEM((width, width), BF16),
            pltpu.VMEM((tok, width), BF16),
            pltpu.VMEM((width, width), BF16),
            pltpu.VMEM((tok, width), BF16),
            pltpu.VMEM((tok, width), BF16),
            pltpu.VMEM((tok, wide), BF16),
            pltpu.SemaphoreType.DMA((6,)),
            pltpu.VMEM((tok, width), BF16),
            pltpu.VMEM((tok, width), BF16),
            pltpu.VMEM((tok, width), BF16),
            pltpu.VMEM((wide, width), BF16),
            pltpu.VMEM((own, width), BF16),
            pltpu.SemaphoreType.DMA,
        ]
        + square_scratch(1, 3, own, width)
        + extra_scratch,
        compiler_params=params(collective_id),
        name="dense_back",
    )(g, weight, r2, r1, wout, vall, wffn, slope, win, active, mixed, att, *old)


def attend_back(h, layer, total, scalars_, refs, hook):
    ids_ref, len_ref, perm_ref, start_ref = scalars_
    q_ref, kv_ref, do_ref, lse_ref, top_ref, joined, dkv, acc, rand, sums = refs
    me = lax.axis_index("wide")
    pair = 2 * HW
    rows_here = q_ref.shape[0] // BLK
    unit = grouping(rows_here)
    cols = slice(h * pair, (h + 1) * pair)
    length = len_ref[0]
    first = me * rows_here
    acc[...] = jnp.zeros_like(acc)

    def group(g, carry):
        for u in range(unit):
            row = g * unit + u
            b = first + row
            here = pl.ds(pl.multiple_of(row * BLK, BLK), BLK)
            blocks, allowed = back_blocks(ids_ref, layer, h, b, total)
            keys = jnp.concatenate([kv_ref[h, k] for k in blocks], axis=0)
            keep = jnp.where((me == 0) & (row < 2), 0.0, 1.0).astype(BF16)
            do_here = do_ref[here, cols] * keep
            both = jnp.concatenate([q_ref[here, cols], do_here], axis=0)
            s_dp = dot_nt(both, keys)
            p = jnp.exp(s_dp[:BLK] + key_bias(blocks, allowed, length) - lse_ref[h, here, :])
            p_dp = p * s_dp[BLK:]
            ds = (p_dp - p * jnp.sum(p_dp, axis=-1, keepdims=True)).astype(BF16)
            joined[here, cols] = dot(ds, keys).astype(BF16)
            d_keys = dot_tn(jnp.concatenate([ds, p.astype(BF16)], axis=0), both)
            d_keys = d_keys.reshape(8, BLK, pair)
            acc[pl.ds(b, 3)] += d_keys[:3]
            acc[1:3] += d_keys[3:5]
            rand[pl.ds(row * 3, 3)] = d_keys[5:]
        hook(g)
        return carry

    lax.fori_loop(0, rows_here // unit, group, 0)

    @pl.when(me == 0)
    def _():
        top = slice(0, 2 * BLK)
        q_here, do_here = q_ref[top, cols], do_ref[top, cols]
        both = jnp.concatenate([q_here, do_here], axis=0)
        lse = lse_ref[h, top, :]
        delta = jnp.sum(do_here.astype(F32) * top_ref[h], axis=-1, keepdims=True)
        span = max(d for d in (16, 12, 8, 2) if total % d == 0)
        step = span * BLK

        def part(i, dq):
            keys = kv_ref[h, pl.ds(i * span, span)].reshape(step, pair)
            s_dp = dot_nt(both, keys)
            token = i * step + lax.broadcasted_iota(jnp.int32, (1, step), 1)
            p = jnp.exp(s_dp[: 2 * BLK] + jnp.where(token < length, 0.0, NEG) - lse)
            ds = (p * (s_dp[2 * BLK :] - delta)).astype(BF16)
            d_keys = dot_tn(jnp.concatenate([ds, p.astype(BF16)], axis=0), both)
            acc[pl.ds(1 + i * span, span)] += d_keys.reshape(span, BLK, pair)
            return dq + dot(ds, keys)

        dq = lax.fori_loop(0, total // span, part, jnp.zeros((2 * BLK, pair), F32))
        joined[top, cols] = dq.astype(BF16)

    sums[0] = jnp.zeros((BLK, pair), F32)

    def prefix(k, carry):
        carry = carry + rand[perm_ref[layer, h, k]]
        sums[k + 1] = carry
        return carry

    lax.fori_loop(0, rows_here * 3, prefix, jnp.zeros((BLK, pair), F32))
    several = 4 if total % 4 == 0 else 1

    def settle(i, carry):
        for u in range(several):
            j = i * several + u
            low, high = start_ref[layer, h, j], start_ref[layer, h, j + 1]
            dkv[h, j] = (acc[j + 1] + (sums[high] - sums[low])).astype(BF16)
        return carry

    lax.fori_loop(0, total // several, settle, 0)


def project_back_kernel(
    count,
    heads,
    owner,
    ids_ref,
    len_ref,
    perm_ref,
    start_ref,
    q_ref,
    kv_ref,
    do_ref,
    lse_ref,
    top_ref,
    dr1_ref,
    x_any,
    w_any,
    dense_any,
    extra_ref,
    *refs,
):
    if owner == 0:
        small_ref, refs = refs[0], refs[1:]
    gw_ref, gv_ref, dx_ref, both_ref, out_ref = refs[:5]
    refs = refs[5:]
    if owner == 0:
        small_done, refs = refs[0], refs[1:]
    result_ref, all_ref, part_any, done_ref = extra_ref, out_ref, extra_ref, out_ref
    x_ref, w_ref, dense_ref, load_sems, dkv, acc, rand, sums = refs[:8]
    handed, slots, joined, send_wide, recv_wide = refs[8:13]
    sq_send, sq_recv, sq_hold, sq_send_sem, sq_recv_sem, hand_sems, ready = refs[13:20]
    me = lax.axis_index("wide")
    mine = lax.axis_index("tensor")
    section = lax.axis_index("section")
    tok, width = x_ref.shape
    own = tok // 4
    pair = 2 * HW
    wide = heads * pair
    total = dkv.shape[1]
    rows_here = tok // BLK
    right, left = {"wide": lax.rem(me + 1, count)}, {"wide": lax.rem(me + count - 1, count)}
    loads = [
        pltpu.make_async_copy(src, dst, load_sems.at[i])
        for i, (src, dst) in enumerate(
            ((dense_any, dense_ref), (w_any.at[owner], w_ref), (x_any, x_ref))
        )
    ]
    for load in loads:
        load.start()
    barrier = wide_barrier(me, count)
    for offset in (1, 2):
        pl.semaphore_signal(
            barrier, inc=1, device_id={"tensor": tensor_peer(mine, offset)}, device_id_type=MESH
        )
    greet(barrier, section, 4)
    blocks = sub_blocks(own)
    sq = Square(mine, own, width, blocks, sq_send, sq_recv, sq_hold, sq_send_sem, sq_recv_sem)
    sq.scatters = (0,)
    split = dense_ref.shape[0] // 2 if owner == 1 else dense_ref.shape[0]
    low, high = pl.ds(0, split), pl.ds(split, dense_ref.shape[0] - split)

    def hand_over(rows, to):
        return remote(
            dense_ref.at[rows], handed.at[rows], hand_sems.at[0], hand_sems.at[1], {"section": to}
        )

    if owner == 0:
        part, cross, small_up, small_cross, part_sems, small_sems = refs[20:]
        line = Line(count)

        def small_in(source):
            return remote(source, small_up, small_sems.at[0], small_sems.at[1], line.inward)

        def small_across():
            return remote(small_up, small_cross, small_sems.at[2], small_sems.at[3], line.inward)

        def small_out():
            return remote(small_done, small_done, small_sems.at[4], small_sems.at[5], line.outward)

        load_part = pltpu.make_async_copy(part_any, part, part_sems.at[0])
        load_part.start()

        def across():
            return remote(part, cross, part_sems.at[1], part_sems.at[2], line.inward)

        def outwards():
            return remote(done_ref, done_ref, part_sems.at[3], part_sems.at[4], line.outward)

        load_part.wait()

        @pl.when(line.is_middle)
        def _():
            across().start()

        @pl.when(line.no_outer)
        def _():
            small_in(small_ref).start()

    loads[0].wait()

    @pl.when(section == 1)
    def _():
        hand_over(low, 0).start()

    if owner == 1:
        tell_ready(ready, section)
        for j in range(blocks):
            all_ref[sq.rows(mine, j), :] = result_ref[j * sq.sub : (j + 1) * sq.sub, :]
            sq.share(1, j, all_ref)
    has_right, has_left = me < count - 1, me > 0

    def keys(shard):
        return pl.ds(shard * rows_here, rows_here)

    def hop(side, shard, h):
        return remote(
            slots.at[side, shard, h],
            slots.at[side, shard, h],
            send_wide.at[side, shard, h],
            recv_wide.at[side, shard, h],
            right if side == 0 else left,
        )

    def pass_on(side, shard, h, more):
        @pl.when(more)
        def _():
            hop(side, shard, h).wait_recv()
            slots[side, shard, h] = (
                slots[side, shard, h].astype(F32) + dkv[h, keys(shard)].astype(F32)
            ).astype(BF16)

        @pl.when(jnp.logical_not(more))
        def _():
            slots[side, shard, h] = dkv[h, keys(shard)]

        hop(side, shard, h).start()

    def step(h, k):
        shard_r, shard_l = count - 1 - k, k

        def rightwards():
            @pl.when(shard_r > me)
            def _():
                pass_on(0, shard_r, h, has_left)

        def leftwards():
            @pl.when(shard_l < me)
            def _():
                pass_on(1, shard_l, h, has_right)

        @pl.when(me < count // 2)
        def _():
            rightwards()
            leftwards()

        @pl.when(me >= count // 2)
        def _():
            leftwards()
            rightwards()

    def steps(h, first):
        def one(k, carry):
            step(h, k)
            return carry

        lax.fori_loop(first, count - 1, one, 0)

    groups = rows_here // grouping(rows_here)
    state = (q_ref, kv_ref, do_ref, lse_ref, top_ref, joined, dkv, acc, rand, sums)
    for h in range(heads):

        def hook(g):
            if h > 0:

                @pl.when(g < count - 1)
                def _():
                    step(h - 1, g)

        attend_back(h, owner, total, (ids_ref, len_ref, perm_ref, start_ref), state, hook)
        if h > 0:
            steps(h - 1, groups)
        if owner == 0 and h == 0:

            @pl.when(line.has_outer)
            def _():
                small_in(small_ref).wait_recv()
                small_up[...] = (
                    small_up[...].astype(F32) + small_ref[...].astype(F32)
                ).astype(BF16)

            @pl.when(line.has_outer & line.is_middle)
            def _():
                small_across().start()

            @pl.when(line.has_outer & line.not_middle)
            def _():
                small_in(small_up).start()

        if owner == 0 and h == heads - 2:

            @pl.when(line.is_middle)
            def _():
                small_across().wait_recv()
                small_done[...] = (
                    small_up[...].astype(F32) + small_cross[...].astype(F32)
                ).astype(BF16)
                across().wait_recv()

                def add(i, carry):
                    span = pl.ds(pl.multiple_of(i * PIECE, 16), PIECE)
                    done_ref[span, :] = (
                        part[span, :].astype(F32) + cross[span, :].astype(F32)
                    ).astype(BF16)
                    return carry

                lax.fori_loop(0, part.shape[0] // PIECE, add, 0)

            @pl.when(line.is_middle & line.has_outer)
            def _():
                small_out().start()
                outwards().start()

    if owner == 1:

        @pl.when(section == 0)
        def _():
            pl.semaphore_wait(ready, 1)
            hand_over(high, 1).start()

    steps(heads - 1, 0)
    for load in loads[1:]:
        load.wait()

    def add_up(first, last):
        def add(i, carry):
            span = pl.ds(pl.multiple_of(i * PIECE, 16), PIECE)
            both_ref[span, :] = (
                dense_ref[span, :].astype(F32) + handed[span, :].astype(F32)
            ).astype(BF16)
            return carry

        lax.fori_loop(first, last, add, 0)

    @pl.when(section == 0)
    def _():
        hand_over(low, 0).wait_recv()
        add_up(0, split // PIECE)

    if owner == 1:

        @pl.when(section == 1)
        def _():
            hand_over(high, 1).wait_recv()
            add_up(split // PIECE, dense_ref.shape[0] // PIECE)

    for h in range(heads):
        cols = slice(wide + h * pair, wide + (h + 1) * pair)

        @pl.when(has_left)
        def _():
            hop(0, me, h).wait_recv()

        @pl.when(has_right)
        def _():
            hop(1, me, h).wait_recv()

        here = dkv[h, keys(me)].astype(F32)
        from_left = jnp.where(has_left, slots[0, me, h].astype(F32), 0.0)
        from_right = jnp.where(has_right, slots[1, me, h].astype(F32), 0.0)
        joined[:, cols] = (here + from_left + from_right).astype(BF16).reshape(tok, pair)

    if owner == 1:
        for j in range(blocks):
            sq.relay_share(1, j, all_ref)

    def back(index, j):
        return dot(joined[sq.rows(index, j), :], w_ref[...])

    for j in range(blocks):
        sq.give_diagonal(0, j, back(sq.d, j))
    for j in range(blocks):
        sq.give_x(0, j, back(sq.x, j))
        sq.give_y(0, j, back(sq.y, j))
    for j in range(blocks):
        sq.relay_sum(0, j)
    for h in range(heads):
        at = h * 2 * HW
        gw_ref[h * HW : (h + 1) * HW, :] = dot_tn(joined[:, at : at + 2 * HW], x_ref[...])[
            :HW
        ].astype(BF16)
        gw_ref[heads * HW + at : heads * HW + at + 2 * HW, :] = dot_tn(
            joined[:, wide + at : wide + at + 2 * HW], x_ref[...]
        ).astype(BF16)
    gv_ref[...] = jnp.sum(joined[...].astype(F32), axis=0, keepdims=True)
    for j in range(blocks):
        rows = slice(j * sq.sub, (j + 1) * sq.sub)
        total = sq.total(0, j, back(mine, j) + dr1_ref[rows, :]).astype(BF16)
        dx_ref[rows, :] = total
    if owner == 1:
        for j in range(blocks):
            sq.have_all(1, j, all_ref)
    sq.close()

    @pl.when(section == 1)
    def _():
        hand_over(low, 0).wait_send()

    if owner == 1:

        @pl.when(section == 0)
        def _():
            hand_over(high, 1).wait_send()

    if owner == 0:

        @pl.when(line.is_middle)
        def _():
            small_across().wait_send()
            across().wait_send()

        @pl.when(line.not_middle)
        def _():
            small_in(small_ref).wait_send()
            small_out().wait_recv()
            outwards().wait_recv()

        @pl.when(line.not_middle & line.has_outer)
        def _():
            small_out().start()
            outwards().start()

        @pl.when(line.has_outer)
        def _():
            small_out().wait_send()
            outwards().wait_send()

    def drain(k, carry):
        shard_r, shard_l = count - 1 - k, k
        for h in range(heads):

            @pl.when(shard_r > me)
            def _():
                hop(0, shard_r, h).wait_send()

            @pl.when(shard_l < me)
            def _():
                hop(1, shard_l, h).wait_send()

        return carry

    lax.fori_loop(0, count - 1, drain, 0)


def project_back(
    scalars_, q, kv, do, lse, top, x, dr1, wt, gw, extra, small, layer, count, collective_id
):
    tok, width = x.shape
    heads, total, _, pair = kv.shape
    own = tok // 4
    wide = heads * pair
    rows_here = tok // BLK
    operands = [q, kv, do, lse, top, dr1]
    out = (tok, width) if layer == 1 else extra.shape
    parts = []
    if layer == 0:
        parts = [pltpu.VMEM(out, BF16)] * 2 + [pltpu.VMEM(small[0].shape, BF16)] * 2
        parts += [pltpu.SemaphoreType.DMA((5,)), pltpu.SemaphoreType.DMA((6,))]
    return pl.pallas_call(
        functools.partial(project_back_kernel, count, heads, layer),
        out_shape=[
            jax.ShapeDtypeStruct((wide + wide // 2, width), BF16),
            jax.ShapeDtypeStruct((1, 2 * wide), F32),
            jax.ShapeDtypeStruct((own, width), BF16),
            jax.ShapeDtypeStruct(gw.shape, BF16),
        ]
        + [jax.ShapeDtypeStruct(out, BF16)]
        + [jax.ShapeDtypeStruct(a.shape, BF16) for a in small],
        grid=(1,),
        in_specs=[scalars()] * 4
        + [whole(*a.shape) for a in operands]
        + [anywhere()] * 3
        + [whole(own, width) if layer == 1 else anywhere()]
        + [whole(*a.shape) for a in small],
        out_specs=[
            whole(wide + wide // 2, width),
            whole(1, 2 * wide),
            whole(own, width),
            whole(*gw.shape),
        ]
        + [whole(*out)]
        + [whole(*a.shape) for a in small],
        scratch_shapes=[
            pltpu.VMEM((tok, width), BF16),
            pltpu.VMEM((2 * wide, width), BF16),
            pltpu.VMEM(gw.shape, BF16),
            pltpu.SemaphoreType.DMA((3,)),
            pltpu.VMEM((heads, total, BLK, pair), BF16),
            pltpu.VMEM((total + 2, BLK, pair), F32),
            pltpu.VMEM((rows_here * 3, BLK, pair), F32),
            pltpu.VMEM((rows_here * 3 + 1, BLK, pair), F32),
            pltpu.VMEM(gw.shape, BF16),
            pltpu.VMEM((2, count, heads, rows_here, BLK, pair), BF16),
            pltpu.VMEM((tok, 2 * wide), BF16),
            pltpu.SemaphoreType.DMA((2, count, heads)),
            pltpu.SemaphoreType.DMA((2, count, heads)),
        ]
        + square_scratch(1, 2, own, width)
        + [pltpu.SemaphoreType.DMA((2,)), pltpu.SemaphoreType.REGULAR]
        + parts,
        compiler_params=params(collective_id),
        name="project_back",
    )(*scalars_, *operands, x, wt, gw, extra, *small)


def greet(barrier, section, expected):
    @pl.when(section == 0)
    def _():
        pl.semaphore_signal(barrier, inc=1, device_id={"section": 1}, device_id_type=MESH)

    pl.semaphore_wait(barrier, expected + section)


def tell_ready(ready, section):
    @pl.when(section == 1)
    def _():
        pl.semaphore_signal(ready, inc=1, device_id={"section": 0}, device_id_type=MESH)


def await_ready(ready, section):
    @pl.when(section == 0)
    def _():
        pl.semaphore_wait(ready, 1)


class Line:
    def __init__(self, count):
        w = lax.axis_index("wide")
        middle = count // 2
        low = w < middle
        self.inward = {"wide": jnp.where(low, w + 1, w - 1)}
        self.outward = {"wide": lax.rem(jnp.where(low, w + count - 1, w + 1), count)}
        self.has_outer = (w > 0) & (w < count - 1)
        self.no_outer = (w == 0) | (w == count - 1)
        self.is_middle = (w == middle - 1) | (w == middle)
        self.not_middle = (w < middle - 1) | (w > middle)


class Chain:
    def __init__(self, count, section, owner, sect, up, done, sems, segments):
        self.sect, self.up, self.done = sect, up, done
        self.r_sect, self.s_in, self.r_up, self.r_done, self.s_out, self.s_sect = sems
        self.segments = segments
        w = lax.axis_index("wide")
        middle = count // 2
        low = w < middle
        self.inward = {"wide": jnp.where(low, w + 1, w - 1)}
        self.outward = {"wide": lax.rem(jnp.where(low, w + count - 1, w + 1), count)}
        self.has_outer = (w > 0) & (w < count - 1)
        self.no_outer = (w == 0) | (w == count - 1)
        self.is_middle = (w == middle - 1) | (w == middle)
        self.not_middle = (w < middle - 1) | (w > middle)
        self.owner, self.mine = owner, section == owner
        self.other = {"section": 1 - section}

    def span(self, i, base):
        return pl.ds(pl.multiple_of((i - base) * PIECE, 16), PIECE)

    def size(self):
        return sum(size for _, _, _, size, _ in self.segments)

    def first(self):
        return min(start for _, _, start, _, _ in self.segments)

    def handed(self, ref, i, base):
        return remote(
            ref.at[self.span(i, base)],
            self.sect.at[i],
            self.s_sect.at[i],
            self.r_sect.at[i],
            self.other,
        )

    def to_up(self, i):
        return remote(self.sect.at[i], self.up.at[i], self.s_in.at[i], self.r_up.at[i], self.inward)

    def to_middle(self, i):
        return remote(
            self.sect.at[i], self.done.at[i], self.s_in.at[i], self.r_done.at[i], self.inward
        )

    def to_outer(self, i):
        return remote(
            self.done.at[i], self.done.at[i], self.s_out.at[i], self.r_done.at[i], self.outward
        )

    def pieces(self, lo, hi, body):
        for ref, base, start, size, shared in self.segments:
            first, last = max(lo, start), min(hi, start + size)
            if first < last:

                def step(i, carry, ref=ref, base=base, shared=shared):
                    body(i, ref, base, shared)
                    return carry

                lax.fori_loop(first, last, step, 0)

    def hand_over(self):
        @pl.when(jnp.logical_not(self.mine))
        def _():
            def step(i, ref, base, shared):
                if shared:
                    self.handed(ref, i, base).start()

            self.pieces(0, 1 << 20, step)

    def add(self, i, ref, base, shared):
        value = ref[self.span(i, base), :].astype(F32)
        if shared:
            self.handed(ref, i, base).wait_recv()
            value += self.sect[i].astype(F32)
        return value

    def send_in(self, i):
        @pl.when(self.is_middle)
        def _():
            self.to_middle(i).start()

        @pl.when(self.not_middle)
        def _():
            self.to_up(i).start()

    def give(self, i, ref, base, shared):
        self.sect[i] = self.add(i, ref, base, shared).astype(BF16)
        self.send_in(i)

    def relay(self, i, ref, base, shared):
        value = self.add(i, ref, base, shared)
        self.to_up(i).wait_recv()
        self.sect[i] = (value + self.up[i].astype(F32)).astype(BF16)
        self.send_in(i)

    def settle(self, i, ref, base, shared):
        self.to_middle(i).wait_recv()

        @pl.when(self.is_middle)
        def _():
            self.done[i] = (self.sect[i].astype(F32) + self.done[i].astype(F32)).astype(BF16)

        @pl.when(self.has_outer)
        def _():
            self.to_outer(i).start()

    def inwards(self, lo, hi):
        @pl.when(self.mine & self.no_outer)
        def _():
            self.pieces(lo, hi, self.give)

        @pl.when(self.mine & self.has_outer)
        def _():
            for i in range(lo, hi):
                self.pieces(i, i + 1, self.relay)
                self.pieces(i - LAG, i - LAG + 1, self.settle)

    def rest(self):
        end = self.first() + self.size()

        @pl.when(self.mine & self.no_outer)
        def _():
            self.pieces(0, end, self.settle)

        @pl.when(self.mine & self.has_outer)
        def _():
            self.pieces(end - LAG, end, self.settle)

    def close(self):
        @pl.when(self.mine)
        def _():
            self.pieces(0, 1 << 20, lambda i, ref, base, shared: self.to_up(i).wait_send())

        @pl.when(self.mine & self.has_outer)
        def _():
            self.pieces(0, 1 << 20, lambda i, ref, base, shared: self.to_outer(i).wait_send())

        @pl.when(jnp.logical_not(self.mine))
        def _():
            def step(i, ref, base, shared):
                if shared:
                    self.handed(ref, i, base).wait_send()

            self.pieces(0, 1 << 20, step)


def chain_scratch(pieces, width):
    return [pltpu.VMEM((pieces, PIECE, width), BF16)] * 2 + [
        pltpu.SemaphoreType.DMA((pieces,))
    ] * 6


def finish_kernel(
    count,
    gqkv_ref,
    gw_ref,
    gvq0_ref,
    gv0_ref,
    gvq1_ref,
    gv1_ref,
    result_ref,
    dx_ref,
    old_ref,
    small_ref,
    done_ref,
    vout_ref,
    far_ref,
    all_ref,
    got_ref,
    got_small,
    vec_ref,
    sect,
    up,
    c0,
    c1,
    c2,
    c3,
    c4,
    c5,
    vsect,
    vtens,
    vup,
    vpart,
    vfin_in,
    vfin,
    vs,
    vr,
    ts,
    tr,
    far_sems,
    ready,
    *square,
):
    section = lax.axis_index("section")
    w = lax.axis_index("wide")
    t = lax.axis_index("tensor")
    barrier = wide_barrier(w, count)
    for offset in (1, 2, 3):
        pl.semaphore_signal(
            barrier, inc=1, device_id={"tensor": tensor_peer(t, offset)}, device_id_type=MESH
        )
    greet(barrier, section, 5)
    tell_ready(ready, section)
    own, width = dx_ref.shape
    blocks = sub_blocks(own)
    sq = Square(t, own, width, blocks, *square)
    sq.scatters = ()
    for at, gvq, gv in ((0, gvq0_ref, gv0_ref), (8, gvq1_ref, gv1_ref)):
        vec_ref[at : at + 1, :] = gvq[...]
        vec_ref[at + 1 : at + 8, :] = gv[1:8, :]
    gw_pieces = gw_ref.shape[0] // PIECE
    qkv_pieces = gqkv_ref.shape[0] // PIECE
    total = gw_pieces + qkv_pieces
    sems = (c0, c1, c2, c3, c4, c5)
    chain = Chain(
        count,
        section,
        0,
        sect,
        up,
        done_ref,
        sems,
        [(gw_ref, 0, 0, gw_pieces, False), (gqkv_ref, gw_pieces, gw_pieces, qkv_pieces, True)],
    )
    inward, outward, other = chain.inward, chain.outward, chain.other
    mine = pl.ds(pl.multiple_of(section * 8, 8), 8)
    theirs = pl.ds(pl.multiple_of(8 - section * 8, 8), 8)

    def v_other():
        return remote(vec_ref.at[theirs], vsect, vs.at[0], vr.at[0], other)

    def v_peer(offset, slot):
        return remote(
            vtens.at[t],
            vtens.at[slot],
            ts.at[offset - 1],
            tr.at[offset - 1],
            {"tensor": tensor_peer(t, offset)},
        )

    def v_up():
        return remote(vpart, vup, vs.at[1], vr.at[1], inward)

    def v_middle():
        return remote(vpart, vfin_in, vs.at[1], vr.at[2], inward)

    def v_outer():
        return remote(vfin, vfin_in, vs.at[2], vr.at[2], outward)

    chain.hand_over()

    def far(ref):
        return remote(ref, far_ref, far_sems.at[0], far_sems.at[1], other)

    def hand_small():
        return remote(small_ref, got_small, far_sems.at[4], far_sems.at[5], other)

    def hand_done():
        return remote(
            old_ref, got_ref, far_sems.at[2], far_sems.at[3], other
        )

    for j in range(blocks):
        all_ref[sq.rows(t, j), :] = dx_ref[j * sq.sub : (j + 1) * sq.sub, :]
        sq.share(0, j, all_ref)
    for j in range(blocks):
        sq.relay_share(0, j, all_ref)
    chain.inwards(0, gw_pieces)
    await_ready(ready, section)
    v_other().start()

    @pl.when(section == 0)
    def _():
        far(result_ref).start()
        hand_small().start()
        hand_done().start()

    v_other().wait_recv()
    vtens[t] = vec_ref[mine, :] + vsect[...]
    for offset in (1, 2, 3):
        v_peer(offset, t).start()
    chain.inwards(gw_pieces, total)
    for j in range(blocks):
        sq.have_all(0, j, all_ref)

    @pl.when(section == 1)
    def _():
        far(all_ref).start()

    for offset in (1, 2, 3):
        v_peer(offset, tensor_peer(t, offset)).wait_recv()
    shared = vtens[0] + vtens[1] + vtens[2] + vtens[3]
    row = lax.broadcasted_iota(jnp.int32, shared.shape, 0)
    value = jnp.where((row == 0) | (row == 4), vtens[t], shared)

    @pl.when(chain.has_outer)
    def _():
        v_up().wait_recv()
        vpart[...] = value + vup[...]

    @pl.when(chain.no_outer)
    def _():
        vpart[...] = value

    @pl.when(chain.is_middle)
    def _():
        v_middle().start()

    @pl.when(chain.not_middle)
    def _():
        v_up().start()

    chain.rest()
    v_middle().wait_recv()

    @pl.when(chain.is_middle)
    def _():
        vfin[...] = vpart[...] + vfin_in[...]

    @pl.when(chain.not_middle)
    def _():
        vfin[...] = vfin_in[...]

    @pl.when(chain.has_outer)
    def _():
        v_outer().start()

    vout_ref[...] = vfin[...]
    chain.close()
    sq.close()
    far(all_ref).wait()

    @pl.when(section == 0)
    def _():
        hand_small().wait_send()
        hand_done().wait_send()

    @pl.when(section == 1)
    def _():
        hand_small().wait_recv()
        hand_done().wait_recv()

    v_other().wait_send()
    v_up().wait_send()
    for offset in (1, 2, 3):
        v_peer(offset, t).wait_send()

    @pl.when(chain.has_outer)
    def _():
        v_outer().wait_send()


def finish(gqkv, gw, vectors, result, dx, old, small_old, count, collective_id):
    own, width = dx.shape
    tok = own * 4
    pieces = (gqkv.shape[0] + gw.shape[0]) // PIECE
    small = pltpu.VMEM((8, width), F32)
    operands = [gqkv, gw, *vectors, result, dx, old, small_old]
    return pl.pallas_call(
        functools.partial(finish_kernel, count),
        out_shape=[
            jax.ShapeDtypeStruct((pieces, PIECE, width), BF16),
            jax.ShapeDtypeStruct((8, width), F32),
            jax.ShapeDtypeStruct((tok, width), BF16),
            jax.ShapeDtypeStruct((tok, width), BF16),
            jax.ShapeDtypeStruct(old.shape, BF16),
            jax.ShapeDtypeStruct(small_old.shape, BF16),
        ],
        grid=(1,),
        in_specs=[whole(*a.shape) for a in operands],
        out_specs=[whole(pieces, PIECE, width), whole(8, width)]
        + [whole(tok, width)] * 2
        + [whole(*old.shape), whole(*small_old.shape)],
        scratch_shapes=[pltpu.VMEM((16, width), F32)]
        + chain_scratch(pieces, width)
        + [small, pltpu.VMEM((4, 8, width), F32)]
        + [small] * 4
        + [pltpu.SemaphoreType.DMA((3,))] * 4
        + [pltpu.SemaphoreType.DMA((6,)), pltpu.SemaphoreType.REGULAR]
        + square_scratch(1, 1, own, width),
        compiler_params=params(collective_id),
        name="finish",
    )(*operands)


def unpack_kernel(
    heads,
    sums_ref,
    low_ref,
    high_ref,
    low_small,
    high_small,
    dx_ref,
    result_ref,
    far_ref,
    vec_ref,
    ends_ref,
    gq_ref,
    gbq_ref,
    gk_ref,
    gv_ref,
    gbv_ref,
    go_ref,
    gbo_ref,
    g1_ref,
    b1_ref,
    gi_ref,
    gbi_ref,
    gf_ref,
    gbf_ref,
    g2_ref,
    b2_ref,
    buf,
    sems,
):
    section = lax.axis_index("section")
    width = gi_ref.shape[1]
    narrow = heads * HW
    wide = heads * 2 * HW
    half = low_ref.shape[0]
    low, high = pl.ds(0, half), pl.ds(half, half)
    few = low_small.shape[0]
    spans = (low, high, pl.ds(2 * half, few), pl.ds(2 * half + few, few))
    targets = tuple(buf.at[span] for span in spans)
    targets += (ends_ref.at[0, 0, 0], ends_ref.at[0, 1, 0])

    def copy(i, source):
        return pltpu.make_async_copy(source, targets[i], sems.at[i])

    @pl.when(section == 0)
    def _():
        for i, source in enumerate(
            tuple(sums_ref.at[span] for span in spans) + (dx_ref, far_ref)
        ):
            copy(i, source).start()

    @pl.when(section != 0)
    def _():
        for i, source in enumerate(
            (low_ref, high_ref, low_small, high_small, far_ref, result_ref)
        ):
            copy(i, source).start()

    for i, ref in (
        (1, gbo_ref),
        (2, g1_ref),
        (3, b1_ref),
        (4, gbi_ref),
        (5, gbf_ref),
        (6, g2_ref),
        (7, b2_ref),
    ):
        ref[...] = vec_ref[i : i + 1, :]
    row = vec_ref[0:1, :]
    cuts = [(h * 2 * HW, wide + h * 2 * HW + HW) for h in range(heads)]
    gbq_ref[...] = 0.125 * jnp.concatenate([row[:, q : q + HW] for q, _ in cuts], axis=1)
    gbv_ref[...] = jnp.concatenate([row[:, v : v + HW] for _, v in cuts], axis=1)
    for i, source in enumerate((low_ref, high_ref, low_small, high_small)):
        copy(i, source).wait()

    def take(out, scale, source, size):
        value = buf[source : source + size, :].astype(F32)
        out(0, size, value if scale is None else scale * value)

    def into(ref, first=0):
        def put(at, span, value):
            ref[0, first + at : first + at + span, :] = value

        return put

    take(into(gi_ref), None, 0, width)
    take(into(gf_ref), None, width, width)
    take(into(go_ref), None, 2 * width, narrow)
    take(into(gq_ref), 0.125, 2 * width + narrow, narrow)
    for h in range(heads):
        source = 2 * width + 2 * narrow + h * 2 * HW
        take(into(gk_ref, h * HW), None, source, HW)
        take(into(gv_ref, h * HW), None, source + HW, HW)
    for i in (4, 5):
        copy(i, far_ref).wait()


def unpack(sums, low, high, low_small, high_small, dx, result, far, vec, heads):
    rows, width = sums.shape
    narrow = heads * HW
    ends = jax.ShapeDtypeStruct((1, 2, 1) + dx.shape, BF16)
    slim = jax.ShapeDtypeStruct((1, narrow, width), F32)
    full = jax.ShapeDtypeStruct((1, width, width), F32)
    line = jax.ShapeDtypeStruct((1, width), F32)
    short = jax.ShapeDtypeStruct((1, narrow), F32)
    shapes = [ends, slim, short, slim, slim, short, slim, line, line, line]
    shapes += [full, line, full, line, line, line]
    return pl.pallas_call(
        functools.partial(unpack_kernel, heads),
        out_shape=shapes,
        grid=(1,),
        in_specs=[anywhere()] * 8 + [whole(*vec.shape)],
        out_specs=[whole(*a.shape) for a in shapes],
        scratch_shapes=[pltpu.VMEM((rows, width), BF16), pltpu.SemaphoreType.DMA((6,))],
        compiler_params=params(),
        name="unpack",
    )(sums, low, high, low_small, high_small, dx, result, far, vec)


def body(
    inputs,
    target,
    pad_mask,
    loss_mask,
    rand_blocks,
    w_query,
    b_query,
    w_key,
    w_value,
    b_value,
    w_out,
    b_out,
    ln1_gain,
    ln1_bias,
    w_in,
    b_in,
    w_ffn,
    b_ffn,
    ln2_gain,
    ln2_bias,
):
    section = lax.axis_index("section")
    count = lax.axis_size("wide")
    micro, _, tok, width = inputs.shape
    total = pad_mask.shape[2] // BLK
    heads = w_query.shape[2] // HW
    wide = heads * 2 * HW

    rand = rand_blocks[0].reshape(heads, -1)
    far_rand = lax.ppermute(rand, "section", [(0, 1), (1, 0)])
    ids = jnp.where(section == 0, jnp.stack([rand, far_rand]), jnp.stack([far_rand, rand]))
    here = lax.dynamic_slice_in_dim(ids, lax.axis_index("wide") * (tok // BLK * 3), tok // BLK * 3, 2)
    slot = jnp.arange(here.shape[2], dtype=jnp.int32)
    order = here * here.shape[2] + slot
    rank = jnp.sum((order[..., None, :] < order[..., :, None]).astype(jnp.int32), axis=-1)
    perm = jnp.sum(jnp.where(rank[..., None, :] == slot[:, None], slot, 0), axis=-1)
    block = jnp.arange(total + 1, dtype=jnp.int32)
    starts = jnp.sum((here[..., None, :] < block[:, None]).astype(jnp.int32), axis=-1)
    weight = (loss_mask * pad_mask).astype(F32).reshape(micro, -1, tok // 4)
    length = jnp.sum(lax.dynamic_index_in_dim(pad_mask, section, 0), axis=(0, 1, 2))[None]
    matrices = [jnp.swapaxes(m, 1, 2)[0] for m in (w_query, w_key, w_value)]
    matrices += [w_in[0], w_ffn[0], w_out[0]]
    vectors = [b_query, b_value, b_out, ln1_gain, ln1_bias, b_in, b_ffn, ln2_gain, ln2_bias]
    x, q, kv, att, lse, top, wt, vall, win, wffn, wout = begin(
        ids, length, inputs, matrices, vectors, count, heads, 2
    )

    saved = []
    for layer in range(2):
        if layer == 1:
            q, kv, att, lse, top = project(ids, length, x, wt, vall, layer, count, heads, 3)
        mixed, active, slope, r1, r2, x_next = dense(
            att, x, wout, win, wffn, vall, layer, 4 + layer
        )
        saved.append((x, q, kv, att, lse, top, mixed, active, slope, r1, r2))
        x = x_next
    result, grad, handed, vector_grads = x, target, (), [None, None]
    for layer in (1, 0):
        x, q, kv, att, lse, top, mixed, active, slope, r1, r2 = saved[layer]
        gw, gv, do, dr1, *middle = dense_back(
            grad,
            weight,
            r2,
            r1,
            slope,
            active,
            mixed,
            att,
            wout,
            win,
            wffn,
            vall,
            layer,
            count,
            6 + layer,
            handed,
        )
        scalars_ = (ids, length, perm, starts)
        extra, small = (result, []) if layer == 1 else (middle[0], [middle[1]])
        gqkv, gvq, grad, gw_both, out, *small_done = project_back(
            scalars_, q, kv, do, lse, top, x, dr1, wt, gw, extra, small, layer, count, 8 + layer
        )
        vector_grads[layer] = [gvq, gv]
        if layer == 1:
            handed, result = (gw_both, gqkv), out

    vectors = vector_grads[0] + vector_grads[1]
    sums, vec, far, dx, low, low_small = finish(
        gqkv, gw_both, vectors, result, grad, out, small_done[0], count, 10
    )
    ends, gq, gbq, gk, gvalue, gbv, gout, *rest = unpack(
        sums.reshape(-1, width), low, out, low_small, small_done[0], dx, result, far, vec, heads
    )
    return (
        ends,
        jnp.swapaxes(gq, 1, 2),
        gbq,
        jnp.swapaxes(gk, 1, 2),
        jnp.swapaxes(gvalue, 1, 2),
        gbv,
        gout,
        *rest,
    )


def solution(mesh):
    matrix = P("section", None, "tensor")
    rowwise = P("section", "tensor", None)
    cut = P("section", "tensor")
    plain = P("section", None)
    return jax.shard_map(
        body,
        mesh=mesh,
        in_specs=(
            P(None, None, "wide", None),
            P(None, None, "wide", None),
            P(),
            P(),
            P("section", "tensor", None, None),
            matrix,
            cut,
            matrix,
            matrix,
            cut,
            rowwise,
            plain,
            plain,
            plain,
            matrix,
            cut,
            rowwise,
            plain,
            plain,
            plain,
        ),
        out_specs=(
            P("section", None, None, "wide", None),
            matrix,
            cut,
            matrix,
            matrix,
            cut,
            rowwise,
            plain,
            plain,
            plain,
            matrix,
            cut,
            rowwise,
            plain,
            plain,
            plain,
        ),
        check_vma=False,
    )
```

```python
import functools

import jax
import jax.numpy as jnp
from jax import lax
from jax.experimental import pallas as pl
from jax.experimental.pallas import tpu as pltpu
from jax.sharding import PartitionSpec as P

HW = 64
BLK = 64
EPS = 1e-06
NEG = -1e30
MESH = pl.DeviceIdType.MESH
F32 = jnp.float32
BF16 = jnp.bfloat16
VMEM_BYTES = 56 * 1024 * 1024
GELU_C = 0.7978845608
GELU_A = 0.044715
NT_DIMS = (((1,), (1,)), ((), ()))
TN_DIMS = (((0,), (0,)), ((), ()))
ORDER = (3, 1, 2)
PIECE = 288
LAG = 1


def dot(a, b):
    return jnp.dot(a, b, preferred_element_type=F32)


def dot_nt(a, b):
    return lax.dot_general(a, b, NT_DIMS, preferred_element_type=F32)


def dot_tn(a, b):
    return lax.dot_general(a, b, TN_DIMS, preferred_element_type=F32)


def vmem():
    return pl.BlockSpec(memory_space=pltpu.VMEM)


def anywhere():
    return pl.BlockSpec(memory_space=pl.ANY)


def whole(*shape):
    return pl.BlockSpec(shape, lambda i: (0,) * len(shape))


def of_layer(array, layer):
    return pl.BlockSpec((None,) + array.shape[1:], lambda i: (layer,) + (0,) * (array.ndim - 1))


def remote(src, dst, send_sem, recv_sem, device):
    return pltpu.make_async_remote_copy(
        src_ref=src,
        dst_ref=dst,
        send_sem=send_sem,
        recv_sem=recv_sem,
        device_id=device,
        device_id_type=MESH,
    )


def tensor_peer(me, offset):
    if offset == 1:
        return me + 1 - 2 * lax.rem(me, 2)
    if offset == 2:
        return lax.rem(me + 2, 4)
    return 3 - me


def tensor_barrier(me):
    barrier = pltpu.get_barrier_semaphore()
    for offset in (1, 2, 3):
        pl.semaphore_signal(
            barrier, inc=1, device_id={"tensor": tensor_peer(me, offset)}, device_id_type=MESH
        )
    return barrier


def params(collective_id=None):
    if collective_id is None:
        return pltpu.CompilerParams(vmem_limit_bytes=VMEM_BYTES)
    return pltpu.CompilerParams(
        vmem_limit_bytes=VMEM_BYTES, collective_id=collective_id, has_side_effects=True
    )


def key_blocks(ids_ref, layer, head, row, first, total):
    b = first + row
    start = jnp.clip(b - 1, 0, total - 3)
    window = [start, start + 1, start + 2]
    r = [ids_ref[layer, head, b * 3 + k] for k in range(3)]

    def far(block):
        return (block < b - 1) | (block > b + 1)

    fresh = [far(k) & (k >= 2) for k in r]
    allowed = [jnp.logical_not(far(k)) for k in window]
    allowed += [far(jnp.int32(0)), far(jnp.int32(1))]
    allowed += [fresh[0], fresh[1] & (r[1] != r[0]), fresh[2] & (r[2] != r[0]) & (r[2] != r[1])]
    return window + [jnp.int32(0), jnp.int32(1)] + r, allowed


def back_blocks(ids_ref, layer, head, b, total):
    blocks, allowed = key_blocks(ids_ref, layer, head, 0, b, total)
    window = [jnp.maximum(b - 1, 0), b, jnp.minimum(b + 1, total - 1)]
    return window + blocks[3:], [b >= 1, b >= 0, b + 1 < total] + allowed[3:]


def key_bias(blocks, allowed, length):
    lane = lax.broadcasted_iota(jnp.int32, (1, 8 * BLK), 1)
    slot = lane // BLK
    limit = jnp.zeros((1, 8 * BLK), jnp.int32)
    for s in range(8):
        tokens = jnp.where(allowed[s], jnp.clip(length - blocks[s] * BLK, 0, BLK), 0)
        limit = jnp.where(slot == s, tokens, limit)
    return jnp.where(lane - slot * BLK < limit, 0.0, NEG)


def gathered(kv_ref, blocks):
    window = kv_ref[pl.ds(blocks[0], 3)].reshape(3 * BLK, -1)
    ends = kv_ref[0:2].reshape(2 * BLK, -1)
    return jnp.concatenate([window, ends] + [kv_ref[k] for k in blocks[5:]], axis=0)


def grouping(rows_here):
    return max(u for u in (4, 3, 2, 1) if rows_here % u == 0)


def wide_barrier(me, count):
    barrier = pltpu.get_barrier_semaphore()
    for side in (1, count - 1):
        pl.semaphore_signal(
            barrier,
            inc=1,
            device_id={"wide": lax.rem(me + side, count)},
            device_id_type=MESH,
        )
    return barrier


def softmax_values(s, keys):
    peak = jnp.max(s, axis=-1, keepdims=True)
    e = jnp.exp(s - peak)
    mass = jnp.sum(e, axis=-1, keepdims=True)
    return dot(e.astype(BF16), keys) / mass, peak + jnp.log(mass)


def gather_attend(
    count, heads, layer, x_ref, wt_ref, bias, ids_ref, len_ref, outs, scratch, ready, finished
):
    q_ref, kv_ref, att_ref, lse_ref, top_ref = outs
    held, (save, send_r, recv_r, send_l, recv_l) = scratch[:heads], scratch[heads:]
    me = lax.axis_index("wide")
    tok = x_ref.shape[0]
    right, left = {"wide": lax.rem(me + 1, count)}, {"wide": lax.rem(me + count - 1, count)}
    pair = 2 * HW
    wide = heads * pair
    has_right, has_left = me < count - 1, me > 0
    length = len_ref[0]
    rows_here = tok // BLK
    total = held[0].shape[0]
    unit = grouping(rows_here)
    groups = rows_here // unit

    def rows(shard):
        return pl.ds(shard * rows_here, rows_here)

    kv = dot_nt(x_ref[...], wt_ref[wide:, :]) + bias[:, wide:]
    for h in range(heads):
        own = kv[:, h * pair : (h + 1) * pair].astype(BF16)
        held[h][rows(me)] = own.reshape(rows_here, BLK, pair)
    ready()

    def copy_r(h, shard, step):
        part = held[h].at[rows(shard)]
        return remote(part, part, send_r.at[h, step], recv_r.at[h, shard], right)

    def copy_l(h, shard, step):
        part = held[h].at[rows(shard)]
        return remote(part, part, send_l.at[h, step], recv_l.at[h, shard], left)

    for h in range(heads):

        @pl.when(has_right)
        def _():
            copy_r(h, me, 0).start()

        @pl.when(has_left)
        def _():
            copy_l(h, me, 0).start()

    q = dot_nt(x_ref[...], wt_ref[:wide, :]) + bias[:, :wide]
    q_ref[...] = q.astype(BF16)

    def forward(h, step):
        shard_r, shard_l = me - step, me + step

        @pl.when(shard_r >= 0)
        def _():
            copy_r(h, shard_r, step).wait_recv()

            @pl.when(has_right)
            def _():
                copy_r(h, shard_r, step).start()

        @pl.when(shard_l < count)
        def _():
            copy_l(h, shard_l, step).wait_recv()

            @pl.when(has_left)
            def _():
                copy_l(h, shard_l, step).start()

    def forward_from(h, first):
        def step(k, carry):
            forward(h, k)
            return carry

        lax.fori_loop(first, count, step, 0)

    forward_from(0, 1)
    for h in range(heads):
        pltpu.make_async_copy(held[h], kv_ref.at[h], save.at[h]).start()
        cols = slice(h * pair, (h + 1) * pair)

        def group(g, carry):
            for u in range(unit):
                row = g * unit + u
                here = pl.ds(pl.multiple_of(row * BLK, BLK), BLK)
                blocks, allowed = key_blocks(ids_ref, layer, h, row, me * rows_here, total)
                keys = gathered(held[h], blocks)
                s = dot_nt(q_ref[here, cols], keys) + key_bias(blocks, allowed, length)
                o, lse = softmax_values(s, keys)
                att_ref[here, cols] = o.astype(BF16)
                lse_ref[h, here, :] = lse
            if h + 1 < heads:

                @pl.when(g + 1 < count)
                def _():
                    forward(h + 1, g + 1)

            return carry

        lax.fori_loop(0, groups, group, 0)
        if h + 1 < heads:
            forward_from(h + 1, groups + 1)

        @pl.when(me == 0)
        def _():
            keys = held[h][...].reshape(total * BLK, pair)
            token = lax.broadcasted_iota(jnp.int32, (1, keys.shape[0]), 1)
            s = dot_nt(q_ref[0 : 2 * BLK, cols], keys) + jnp.where(token < length, 0.0, NEG)
            o, lse = softmax_values(s, keys)
            att_ref[0 : 2 * BLK, cols] = o.astype(BF16)
            lse_ref[h, 0 : 2 * BLK, :] = lse
            top_ref[h] = o

        @pl.when(me != 0)
        def _():
            top_ref[h] = jnp.zeros((2 * BLK, pair), F32)

    finished()

    def drain(step, carry):
        shard_r, shard_l = me - step, me + step
        for h in range(heads):

            @pl.when((shard_r >= 0) & has_right)
            def _():
                copy_r(h, shard_r, step).wait_send()

            @pl.when((shard_l < count) & has_left)
            def _():
                copy_l(h, shard_l, step).wait_send()

        return carry

    lax.fori_loop(0, count, drain, 0)
    for h in range(heads):
        pltpu.make_async_copy(held[h], kv_ref.at[h], save.at[h]).wait()


def attend_outs(count, heads, tok):
    pair = 2 * HW
    shapes = [
        jax.ShapeDtypeStruct((tok, heads * pair), BF16),
        jax.ShapeDtypeStruct((heads, count * tok // BLK, BLK, pair), BF16),
        jax.ShapeDtypeStruct((tok, heads * pair), BF16),
        jax.ShapeDtypeStruct((heads, tok, 1), F32),
        jax.ShapeDtypeStruct((heads, 2 * BLK, pair), F32),
    ]
    specs = [anywhere() if i == 1 else whole(*a.shape) for i, a in enumerate(shapes)]
    return shapes, specs


def gather_scratch(count, heads, tok):
    return (
        [pltpu.VMEM((count * tok // BLK, BLK, 2 * HW), BF16)] * heads
        + [pltpu.SemaphoreType.DMA((heads,))]
        + [pltpu.SemaphoreType.DMA((heads, count))] * 4
    )


def scalars():
    return pl.BlockSpec(memory_space=pltpu.SMEM)


def begin_kernel(
    count,
    heads,
    ids_ref,
    len_ref,
    inputs_ref,
    wq_ref,
    wk_ref,
    wv_ref,
    win_ref,
    wffn_ref,
    wout_ref,
    bq_ref,
    bv_ref,
    bout_ref,
    g1_ref,
    b1_ref,
    bin_ref,
    bffn_ref,
    g2_ref,
    b2_ref,
    x_ref,
    q_ref,
    kv_ref,
    att_ref,
    lse_ref,
    top_ref,
    wt_ref,
    vall_ref,
    win_all_ref,
    wffn_all_ref,
    wout_all_ref,
    turn,
    x_sem,
    keep,
    send,
    recv,
    *scratch,
):
    section = lax.axis_index("section")
    other = {"section": 1 - section}
    barrier = wide_barrier(lax.axis_index("wide"), count)
    pl.semaphore_signal(barrier, inc=1, device_id=other, device_id_type=MESH)
    load = pltpu.make_async_copy(inputs_ref.at[section, 0], x_ref, x_sem)
    load.start()
    wide = heads * 2 * HW
    scale = jnp.asarray(0.125, BF16)
    none = jnp.zeros((HW, x_ref.shape[1]), BF16)
    row = []
    for h in range(heads):
        at, cut = h * 2 * HW, slice(h * HW, (h + 1) * HW)
        wt_ref[section, at : at + HW, :] = wq_ref[cut, :] * scale
        wt_ref[section, at + HW : at + 2 * HW, :] = none
        wt_ref[section, wide + at : wide + at + HW, :] = wk_ref[cut, :]
        wt_ref[section, wide + at + HW : wide + at + 2 * HW, :] = wv_ref[cut, :]
        row += [bq_ref[:, cut].astype(F32) * 0.125, jnp.zeros((1, HW), F32)]
    for h in range(heads):
        row += [jnp.zeros((1, HW), F32), bv_ref[:, h * HW : (h + 1) * HW].astype(F32)]
    vall_ref[section, 0:1, :] = jnp.concatenate(row, axis=1)
    for i, ref in enumerate((bout_ref, g1_ref, b1_ref, bin_ref, bffn_ref, g2_ref, b2_ref)):
        vall_ref[section, i + 1 : i + 2, :] = ref[...].astype(F32)
    pl.semaphore_wait(barrier, 3)

    pairs = [
        (wt_ref.at[section], wt_ref.at[section]),
        (vall_ref.at[section], vall_ref.at[section]),
        (win_ref, win_all_ref.at[section]),
        (wffn_ref, wffn_all_ref.at[section]),
        (wout_ref, wout_all_ref.at[section]),
    ]
    swaps = [remote(src, dst, send.at[i], recv.at[i], other) for i, (src, dst) in enumerate(pairs)]
    keeps = [
        pltpu.make_async_copy(src, dst, keep.at[i]) for i, (src, dst) in enumerate(pairs[2:])
    ]
    for copy in swaps + keeps:
        copy.start()
    load.wait()

    @pl.when(section == 1)
    def _():
        swaps[0].wait_recv()
        swaps[1].wait_recv()

    def ready():
        @pl.when(section == 1)
        def _():
            pl.semaphore_wait(turn, 1)

    def finished():
        @pl.when(section == 0)
        def _():
            pl.semaphore_signal(turn, inc=1, device_id={"section": 1}, device_id_type=MESH)

    gather_attend(
        count,
        heads,
        0,
        x_ref,
        wt_ref.at[0],
        vall_ref[0, 0:1, :],
        ids_ref,
        len_ref,
        (q_ref, kv_ref, att_ref, lse_ref, top_ref),
        scratch,
        ready,
        finished,
    )

    @pl.when(section == 0)
    def _():
        swaps[0].wait_recv()
        swaps[1].wait_recv()

    for copy in swaps[2:]:
        copy.wait_recv()
    for copy in swaps:
        copy.wait_send()
    for copy in keeps:
        copy.wait()


def begin(ids, length, inputs, matrices, vectors, count, heads, collective_id):
    _, _, tok, width = inputs.shape
    wide = heads * 2 * HW
    narrow = heads * HW
    both = [(2, width, width), (2, width, width), (2, narrow, width)]
    shapes, specs = attend_outs(count, heads, tok)
    return pl.pallas_call(
        functools.partial(begin_kernel, count, heads),
        grid=(1,),
        out_shape=[jax.ShapeDtypeStruct((tok, width), BF16)]
        + shapes
        + [
            jax.ShapeDtypeStruct((2, 2 * wide, width), BF16),
            jax.ShapeDtypeStruct((2, 8, width), F32),
        ]
        + [jax.ShapeDtypeStruct(shape, BF16) for shape in both],
        in_specs=[scalars(), scalars(), anywhere()]
        + [whole(*m.shape) for m in matrices]
        + [whole(*v.shape) for v in vectors],
        out_specs=[whole(tok, width)]
        + specs
        + [whole(2, 2 * wide, width), whole(2, 8, width)]
        + [anywhere()] * 3,
        scratch_shapes=[
            pltpu.SemaphoreType.REGULAR,
            pltpu.SemaphoreType.DMA,
            pltpu.SemaphoreType.DMA((3,)),
            pltpu.SemaphoreType.DMA((5,)),
            pltpu.SemaphoreType.DMA((5,)),
        ]
        + gather_scratch(count, heads, tok),
        compiler_params=params(collective_id),
        name="begin",
    )(ids, length, inputs, *matrices, *vectors)


def project_kernel(count, heads, layer, ids_ref, len_ref, x_ref, wt_ref, v_ref, *refs):
    barrier = wide_barrier(lax.axis_index("wide"), count)
    gather_attend(
        count,
        heads,
        layer,
        x_ref,
        wt_ref,
        v_ref[0:1, :],
        ids_ref,
        len_ref,
        refs[:5],
        refs[5:],
        lambda: pl.semaphore_wait(barrier, 2),
        lambda: None,
    )


def project(ids, length, x, wt, vall, layer, count, heads, collective_id):
    tok, width = x.shape
    shapes, specs = attend_outs(count, heads, tok)
    return pl.pallas_call(
        functools.partial(project_kernel, count, heads, layer),
        grid=(1,),
        out_shape=shapes,
        in_specs=[scalars(), scalars(), whole(tok, width), of_layer(wt, layer), of_layer(vall, layer)],
        out_specs=specs,
        scratch_shapes=gather_scratch(count, heads, tok),
        compiler_params=params(collective_id),
        name="project",
    )(ids, length, x, wt, vall)


class Square:
    def __init__(self, me, own, width, blocks, send_buf, recv_buf, hold, send_sem, recv_sem):
        self.me = me
        self.x, self.y, self.d = (tensor_peer(me, k) for k in (1, 2, 3))
        self.own, self.sub, self.half = own, own // blocks, width // 2
        self.blocks = blocks
        self.send_buf, self.recv_buf, self.hold = send_buf, recv_buf, hold
        self.send_sem, self.recv_sem = send_sem, recv_sem
        self.used = []

    def rows(self, index, j, size=None):
        return pl.ds(pl.multiple_of(index * self.own + j * self.sub, 16), size or self.sub)

    def to(self, m):
        return {"tensor": self.x if m < 3 else self.y}

    def scatter(self, stage, j, m):
        slot = self.scatters.index(stage)
        return remote(
            self.send_buf.at[slot, j, m],
            self.recv_buf.at[slot, j, m],
            self.send_sem.at[stage, j, m],
            self.recv_sem.at[stage, j, m],
            self.to(m),
        )

    def put(self, stage, j, m, value):
        self.send_buf[self.scatters.index(stage), j, m] = value.astype(BF16)
        self.scatter(stage, j, m).start()
        self.used.append(self.scatter(stage, j, m))

    def got(self, stage, j, m):
        self.scatter(stage, j, m).wait_recv()
        return self.recv_buf[self.scatters.index(stage), j, m].astype(F32)

    def give_diagonal(self, stage, j, part):
        self.put(stage, j, 0, part[:, self.half :])
        self.put(stage, j, 3, part[:, : self.half])

    def give_x(self, stage, j, part):
        self.put(stage, j, 1, part[:, self.half :])
        self.hold[j, 0] = part[:, : self.half]

    def give_y(self, stage, j, part):
        self.put(stage, j, 4, part[:, : self.half])
        self.hold[j, 1] = part[:, self.half :]

    def relay_sum(self, stage, j):
        self.put(stage, j, 2, self.hold[j, 0] + self.got(stage, j, 3))
        self.put(stage, j, 5, self.hold[j, 1] + self.got(stage, j, 0))

    def total(self, stage, j, own):
        left = own[:, : self.half] + self.got(stage, j, 4) + self.got(stage, j, 2)
        right = own[:, self.half :] + self.got(stage, j, 1) + self.got(stage, j, 5)
        return jnp.concatenate([left, right], axis=1)

    def gather(self, stage, j, m, ref, index, first):
        cols = pl.ds(0 if first else self.half, self.half)
        return remote(
            ref.at[self.rows(index, j), cols],
            ref.at[self.rows(index, j), cols],
            self.send_sem.at[stage, j, m],
            self.recv_sem.at[stage, j, m],
            self.to(m),
        )

    def send(self, copy):
        copy.start()
        self.used.append(copy)

    def share(self, stage, j, ref):
        for m, first in ((0, True), (3, False), (1, False), (4, True)):
            self.send(self.gather(stage, j, m, ref, self.me, first))

    def relay_share(self, stage, j, ref):
        self.gather(stage, j, 0, ref, self.x, True).wait_recv()
        self.send(self.gather(stage, j, 5, ref, self.x, True))
        self.gather(stage, j, 3, ref, self.y, False).wait_recv()
        self.send(self.gather(stage, j, 2, ref, self.y, False))

    def have_x(self, stage, j, ref):
        self.gather(stage, j, 1, ref, self.x, False).wait_recv()

    def have_y(self, stage, j, ref):
        self.gather(stage, j, 4, ref, self.y, True).wait_recv()

    def have_diagonal(self, stage, j, ref):
        self.gather(stage, j, 5, ref, self.d, True).wait_recv()
        self.gather(stage, j, 2, ref, self.d, False).wait_recv()

    def have_all(self, stage, j, ref):
        self.have_x(stage, j, ref)
        self.have_y(stage, j, ref)
        self.have_diagonal(stage, j, ref)

    def close(self):
        for copy in self.used:
            copy.wait_send()


def square_barrier(me):
    barrier = pltpu.get_barrier_semaphore()
    for offset in (1, 2):
        pl.semaphore_signal(
            barrier, inc=1, device_id={"tensor": tensor_peer(me, offset)}, device_id_type=MESH
        )
    return barrier


def sub_blocks(own):
    return 2 if own % 32 == 0 else 1


def square_scratch(scatters, stages, own, width):
    blocks = sub_blocks(own)
    buf = pltpu.VMEM((scatters, blocks, 6, own // blocks, width // 2), BF16)
    return [
        buf,
        buf,
        pltpu.VMEM((blocks, 2, own // blocks, width // 2), F32),
        pltpu.SemaphoreType.DMA((stages, blocks, 6)),
        pltpu.SemaphoreType.DMA((stages, blocks, 6)),
    ]


def norm_parts(values):
    center = values - jnp.mean(values, axis=-1, keepdims=True)
    rstd = lax.rsqrt(jnp.mean(center * center, axis=-1, keepdims=True) + EPS)
    return center * rstd, rstd


def dense_kernel(
    last,
    layer,
    att_ref,
    x_ref,
    wout_ref,
    v_ref,
    win_any,
    wffn_any,
    mixed_any,
    active_any,
    slope_any,
    r1_ref,
    r2_ref,
    out_ref,
    wout_pad,
    win_ref,
    wffn_ref,
    mixed_ref,
    active_ref,
    slope_ref,
    sems,
    *scratch,
):
    me = lax.axis_index("tensor")
    own, width = x_ref.shape[0] // 4, x_ref.shape[1]
    blocks = sub_blocks(own)
    barrier = square_barrier(me)
    sq = Square(me, own, width, blocks, *scratch)
    pad_heads(wout_ref, wout_pad)
    sq.scatters = (0, 2)
    loads = [
        pltpu.make_async_copy(src.at[layer], dst, sems.at[i])
        for i, (src, dst) in enumerate(((win_any, win_ref), (wffn_any, wffn_ref)))
    ]
    for load in loads:
        load.start()
    stores = [
        pltpu.make_async_copy(src, dst, sems.at[2 + i])
        for i, (src, dst) in enumerate(
            ((mixed_ref, mixed_any), (active_ref, active_any), (slope_ref, slope_any))
        )
    ]

    def local(j):
        return slice(j * sq.sub, (j + 1) * sq.sub)

    def branch(index, j):
        return dot(att_ref[sq.rows(index, j), :], wout_pad[...])

    for j in range(blocks):
        part = branch(sq.d, j)
        if j == 0:
            pl.semaphore_wait(barrier, 2)
        sq.give_diagonal(0, j, part)
    for j in range(blocks):
        sq.give_x(0, j, branch(sq.x, j))
        sq.give_y(0, j, branch(sq.y, j))
    for j in range(blocks):
        r1_ref[local(j), :] = (
            branch(me, j) + x_ref[sq.rows(me, j), :].astype(F32) + v_ref[1:2, :]
        )
        sq.relay_sum(0, j)
    for j in range(blocks):
        total = sq.total(0, j, r1_ref[local(j), :])
        r1_ref[local(j), :] = total
        mixed = (norm_parts(total)[0] * v_ref[2:3, :] + v_ref[3:4, :]).astype(BF16)
        mixed_ref[sq.rows(me, j), :] = mixed
        sq.share(1, j, mixed_ref)

    for load in loads:
        load.wait()

    def feed(index, j):
        here = sq.rows(index, j)
        u = dot(mixed_ref[here, :], win_ref[...]) + v_ref[4:5, :]
        th = jnp.tanh(GELU_C * (u + GELU_A * u * u * u))
        half = 0.5 * (1.0 + th)
        slope = half + 0.5 * u * (1.0 - th * th) * (GELU_C * (1.0 + 3.0 * GELU_A * u * u))
        slope_ref[here, :] = slope.astype(BF16)
        active = (u * half).astype(BF16)
        active_ref[here, :] = active
        return dot(active, wffn_ref[...])

    for j in range(blocks):
        r2_ref[local(j), :] = (
            feed(me, j) + mixed_ref[sq.rows(me, j), :].astype(F32) + v_ref[5:6, :]
        )
        sq.relay_share(1, j, mixed_ref)
    for j in range(blocks):
        sq.have_x(1, j, mixed_ref)
        sq.give_x(2, j, feed(sq.x, j))
        sq.have_y(1, j, mixed_ref)
        sq.give_y(2, j, feed(sq.y, j))
        sq.have_diagonal(1, j, mixed_ref)
        sq.give_diagonal(2, j, feed(sq.d, j))
    for store in stores:
        store.start()
    for j in range(blocks):
        sq.relay_sum(2, j)
    for j in range(blocks):
        total = sq.total(2, j, r2_ref[local(j), :])
        r2_ref[local(j), :] = total
        result = (norm_parts(total)[0] * v_ref[6:7, :] + v_ref[7:8, :]).astype(BF16)
        if last:
            out_ref[local(j), :] = result
        else:
            out_ref[sq.rows(me, j), :] = result
            sq.share(3, j, out_ref)
    if not last:
        for j in range(blocks):
            sq.relay_share(3, j, out_ref)
        for j in range(blocks):
            sq.have_all(3, j, out_ref)
    sq.close()
    for store in stores:
        store.wait()


def pad_heads(rows_ref, padded_ref):
    for h in range(rows_ref.shape[0] // HW):
        at = h * 2 * HW
        padded_ref[at : at + HW, :] = jnp.zeros((HW, rows_ref.shape[1]), rows_ref.dtype)
        padded_ref[at + HW : at + 2 * HW, :] = rows_ref[h * HW : (h + 1) * HW, :]


def dense(att, x, wout, win, wffn, vall, layer, collective_id):
    tok, width = x.shape
    own = tok // 4
    wide = att.shape[1]
    last = layer == 1
    out_rows = own if last else tok
    return pl.pallas_call(
        functools.partial(dense_kernel, last, layer),
        out_shape=[jax.ShapeDtypeStruct((tok, width), BF16)] * 3
        + [jax.ShapeDtypeStruct((own, width), F32)] * 2
        + [jax.ShapeDtypeStruct((out_rows, width), BF16)],
        grid=(1,),
        in_specs=[whole(tok, wide), whole(tok, width)]
        + [of_layer(a, layer) for a in (wout, vall)]
        + [anywhere()] * 2,
        out_specs=[anywhere()] * 3 + [whole(own, width)] * 2 + [whole(out_rows, width)],
        scratch_shapes=[
            pltpu.VMEM((wide, width), BF16),
            pltpu.VMEM((width, width), BF16),
            pltpu.VMEM((width, width), BF16),
            pltpu.VMEM((tok, width), BF16),
            pltpu.VMEM((tok, width), BF16),
            pltpu.VMEM((tok, width), BF16),
            pltpu.SemaphoreType.DMA((5,)),
        ]
        + square_scratch(2, 4, own, width),
        compiler_params=params(collective_id),
        name="dense",
    )(att, x, wout, vall, win, wffn)


def norm_back(values, grad, gain):
    n, rstd = norm_parts(values)
    f = grad * gain
    back = (
        f - jnp.mean(f, axis=-1, keepdims=True) - n * jnp.mean(f * n, axis=-1, keepdims=True)
    ) * rstd
    return back, n


def dense_back_kernel(
    count,
    with_chain,
    g_ref,
    weight_ref,
    r2_ref,
    r1_ref,
    wout_ref,
    v_ref,
    *refs,
):
    late_any, refs = refs[:6], refs[6:]
    if with_chain:
        old_any, gqkv_ref, refs = refs[0], refs[1], refs[2:]
    gw_ref, gv_ref, do_ref, dr1_ref = refs[:4]
    refs = refs[4:]
    if with_chain:
        up_ref, gqkv_sum, refs = refs[0], refs[1], refs[2:]
    late, late_sems = refs[:6], refs[6]
    wffn_ref, slope_ref, win_ref, active_ref, mixed_ref, att_ref = late
    refs = refs[7:]
    layer = 0 if with_chain else 1
    loads = [
        pltpu.make_async_copy(src.at[layer] if i in (0, 2) else src, dst, late_sems.at[i])
        for i, (src, dst) in enumerate(zip(late_any, late))
    ]
    for load in loads:
        load.start()
    db2, dh, db1, wout_pad, g_buf, g_sem = refs[:6]
    refs = refs[3:]
    me = lax.axis_index("tensor")
    wide_at = lax.axis_index("wide")
    section = lax.axis_index("section")
    own, width = r1_ref.shape
    wide = att_ref.shape[1]
    blocks = sub_blocks(own)
    barrier = square_barrier(me)
    sq = Square(me, own, width, blocks, *refs[3:8])
    sq.scatters = (1,)
    refs = refs[8:]
    if with_chain:
        old, old_sem, sems, landed, hand_sems, ready = refs
        line = Line(count)
        rows = old.shape[0]
        half = gqkv_sum.shape[0]

        def half_of(core):
            return pl.ds(pl.multiple_of(core * half, 16), half)

        def swap():
            return remote(
                gqkv_ref.at[half_of(1 - section)],
                landed,
                hand_sems.at[0],
                hand_sems.at[1],
                {"section": 1 - section},
            )

        load_old = pltpu.make_async_copy(
            old_any.at[pl.ds(pl.multiple_of(section * rows, 16), rows)], old, old_sem
        )
        load_old.start()
        for side in (1, count - 1):
            pl.semaphore_signal(
                barrier,
                inc=1,
                device_id={"wide": lax.rem(wide_at + side, count)},
                device_id_type=MESH,
            )

        def inwards(source):
            return remote(source, up_ref, sems.at[0], sems.at[1], line.inward)

    def down(values):
        return jnp.sum(values, axis=0, keepdims=True)

    def local(j):
        return slice(j * sq.sub, (j + 1) * sq.sub)

    if with_chain:

        def gradient(j):
            return g_ref[local(j), :].astype(F32)

    else:
        load = pltpu.make_async_copy(g_ref.at[section, 0, sq.rows(me, 0, own)], g_buf, g_sem)
        load.start()
        weight = weight_ref[section]
        count_all = jnp.sum(jnp.sum(weight, axis=1, keepdims=True), axis=0, keepdims=True)
        factor = (weight.shape[0] * weight.shape[1]) / count_all
        here = weight_ref[section, pl.ds(wide_at * 4 + me, 1), :]
        equal = lax.broadcasted_iota(jnp.int32, (own, own), 0) == lax.broadcasted_iota(
            jnp.int32, (own, own), 1
        )
        column = jnp.sum(jnp.where(equal, here, 0.0), axis=1, keepdims=True) * factor
        load.wait()

        def gradient(j):
            return g_buf[local(j), :].astype(F32) * column[local(j), :]

    pad_heads(wout_ref, wout_pad)
    d_gain, d_shift, d_bias = 0.0, 0.0, 0.0
    for j in range(blocks):
        grad = gradient(j)
        d_two, n_two = norm_back(r2_ref[local(j), :], grad, v_ref[6:7, :])
        db2[sq.rows(me, j), :] = d_two.astype(BF16)
        dr1_ref[local(j), :] = d_two
        if j == 0:
            if with_chain:
                greet(barrier, section, 4)
                tell_ready(ready, section)
            else:
                pl.semaphore_wait(barrier, 2)
        sq.share(0, j, db2)
        d_gain += down(grad * n_two)
        d_shift += down(grad)
        d_bias += down(d_two)
    gv_ref[6:7, :] = d_gain
    gv_ref[7:8, :] = d_shift
    gv_ref[5:6, :] = d_bias

    def feed(index, j):
        here = sq.rows(index, j)
        back = dot_nt(db2[here, :], wffn_ref[...]) * slope_ref[here, :].astype(F32)
        low = back.astype(BF16)
        dh[here, :] = low
        return dot_nt(low, win_ref[...])

    if with_chain:
        load_old.wait()

        @pl.when(line.no_outer)
        def _():
            inwards(old).start()

        @pl.when(section == 1)
        def _():
            swap().start()

    for load in loads[:3]:
        load.wait()
    for j in range(blocks):
        dr1_ref[local(j), :] += feed(me, j)
        sq.relay_share(0, j, db2)
    for j in range(blocks):
        sq.have_x(0, j, db2)
        sq.give_x(1, j, feed(sq.x, j))
        sq.have_y(0, j, db2)
        sq.give_y(1, j, feed(sq.y, j))
        sq.have_diagonal(0, j, db2)
        sq.give_diagonal(1, j, feed(sq.d, j))
    for j in range(blocks):
        sq.relay_sum(1, j)
    for load in loads[3:]:
        load.wait()
    step = 256
    for i in range(width // step):
        cols = slice(i * step, (i + 1) * step)
        gw_ref[width + i * step : width + (i + 1) * step, :] = dot_tn(
            active_ref[:, cols], db2[...]
        ).astype(BF16)
        gw_ref[cols, :] = dot_tn(mixed_ref[:, cols], dh[...]).astype(BF16)
    gv_ref[4:5, :] = down(dh[...].astype(F32))
    d_gain, d_shift, d_bias = 0.0, 0.0, 0.0
    for j in range(blocks):
        total = sq.total(1, j, dr1_ref[local(j), :])
        d_one, n_one = norm_back(r1_ref[local(j), :], total, v_ref[2:3, :])
        db1[sq.rows(me, j), :] = d_one.astype(BF16)
        sq.share(2, j, db1)
        dr1_ref[local(j), :] = d_one
        d_gain += down(total * n_one)
        d_shift += down(total)
        d_bias += down(d_one)
    gv_ref[2:3, :] = d_gain
    gv_ref[3:4, :] = d_shift
    gv_ref[1:2, :] = d_bias
    gv_ref[0:1, :] = jnp.zeros((1, width), F32)

    def attended_back(index, j):
        here = sq.rows(index, j)
        do_ref[here, :] = dot_nt(db1[here, :], wout_pad[...]).astype(BF16)

    for j in range(blocks):
        attended_back(me, j)
        sq.relay_share(2, j, db1)
    for j in range(blocks):
        sq.have_x(2, j, db1)
        attended_back(sq.x, j)
        sq.have_y(2, j, db1)
        attended_back(sq.y, j)
        sq.have_diagonal(2, j, db1)
        attended_back(sq.d, j)
    for h in range(wide // (2 * HW)):
        cols = slice(h * 2 * HW, (h + 1) * 2 * HW)
        gw_ref[2 * width + h * HW : 2 * width + (h + 1) * HW, :] = dot_tn(
            att_ref[:, cols], db1[...]
        )[HW:].astype(BF16)
    sq.close()
    if with_chain:
        await_ready(ready, section)

        @pl.when(section == 0)
        def _():
            swap().start()

        @pl.when(line.has_outer)
        def _():
            inwards(old).wait_recv()

            def add(i, carry):
                span = pl.ds(pl.multiple_of(i * PIECE, 16), PIECE)
                up_ref[span, :] = (up_ref[span, :].astype(F32) + old[span, :].astype(F32)).astype(BF16)
                return carry

            lax.fori_loop(0, rows // PIECE, add, 0)

        @pl.when(line.has_outer & line.not_middle)
        def _():
            inwards(up_ref).start()

        @pl.when(line.not_middle)
        def _():
            inwards(old).wait_send()

        swap().wait()
        gqkv_sum[...] = (
            gqkv_ref[half_of(section), :].astype(F32) + landed[...].astype(F32)
        ).astype(BF16)


def dense_back(
    g, weight, r2, r1, slope, active, mixed, att, wout, win, wffn, vall, layer, count, collective_id, old
):
    own, width = r1.shape
    tok, wide = att.shape
    gw_rows = 2 * width + wide // 2
    extra_out, extra_scratch = [], []
    if old:
        half = (old[0].shape[0] // 2, width)
        small = (old[1].shape[0] // 2, width)
        extra_out = [half, small]
        extra_scratch = [
            pltpu.VMEM(half, BF16),
            pltpu.SemaphoreType.DMA,
            pltpu.SemaphoreType.DMA((2,)),
            pltpu.VMEM(small, BF16),
            pltpu.SemaphoreType.DMA((2,)),
            pltpu.SemaphoreType.REGULAR,
        ]
    return pl.pallas_call(
        functools.partial(dense_back_kernel, count, bool(old)),
        out_shape=[
            jax.ShapeDtypeStruct((gw_rows, width), BF16),
            jax.ShapeDtypeStruct((8, width), F32),
            jax.ShapeDtypeStruct((tok, wide), BF16),
            jax.ShapeDtypeStruct((own, width), F32),
        ]
        + [jax.ShapeDtypeStruct(shape, BF16) for shape in extra_out],
        grid=(1,),
        in_specs=[whole(own, width) if old else anywhere(), whole(*weight.shape)]
        + [whole(own, width)] * 2
        + [of_layer(a, layer) for a in (wout, vall)]
        + [anywhere()] * 6
        + ([anywhere(), whole(*old[1].shape)] if old else []),
        out_specs=[
            whole(gw_rows, width),
            whole(8, width),
            whole(tok, wide),
            whole(own, width),
        ]
        + [whole(*shape) for shape in extra_out],
        scratch_shapes=[
            pltpu.VMEM((width, width), BF16),
            pltpu.VMEM((tok, width), BF16),
            pltpu.VMEM((width, width), BF16),
            pltpu.VMEM((tok, width), BF16),
            pltpu.VMEM((tok, width), BF16),
            pltpu.VMEM((tok, wide), BF16),
            pltpu.SemaphoreType.DMA((6,)),
            pltpu.VMEM((tok, width), BF16),
            pltpu.VMEM((tok, width), BF16),
            pltpu.VMEM((tok, width), BF16),
            pltpu.VMEM((wide, width), BF16),
            pltpu.VMEM((own, width), BF16),
            pltpu.SemaphoreType.DMA,
        ]
        + square_scratch(1, 3, own, width)
        + extra_scratch,
        compiler_params=params(collective_id),
        name="dense_back",
    )(g, weight, r2, r1, wout, vall, wffn, slope, win, active, mixed, att, *old)


def attend_back(h, layer, total, scalars_, refs, hook):
    ids_ref, len_ref, perm_ref, start_ref = scalars_
    q_ref, kv_ref, do_ref, lse_ref, top_ref, joined, dkv, acc, rand, sums = refs
    me = lax.axis_index("wide")
    pair = 2 * HW
    rows_here = q_ref.shape[0] // BLK
    unit = grouping(rows_here)
    cols = slice(h * pair, (h + 1) * pair)
    length = len_ref[0]
    first = me * rows_here
    acc[...] = jnp.zeros_like(acc)

    def group(g, carry):
        for u in range(unit):
            row = g * unit + u
            b = first + row
            here = pl.ds(pl.multiple_of(row * BLK, BLK), BLK)
            blocks, allowed = back_blocks(ids_ref, layer, h, b, total)
            keys = jnp.concatenate([kv_ref[h, k] for k in blocks], axis=0)
            keep = jnp.where((me == 0) & (row < 2), 0.0, 1.0).astype(BF16)
            do_here = do_ref[here, cols] * keep
            both = jnp.concatenate([q_ref[here, cols], do_here], axis=0)
            s_dp = dot_nt(both, keys)
            p = jnp.exp(s_dp[:BLK] + key_bias(blocks, allowed, length) - lse_ref[h, here, :])
            p_dp = p * s_dp[BLK:]
            ds = (p_dp - p * jnp.sum(p_dp, axis=-1, keepdims=True)).astype(BF16)
            joined[here, cols] = dot(ds, keys).astype(BF16)
            d_keys = dot_tn(jnp.concatenate([ds, p.astype(BF16)], axis=0), both)
            d_keys = d_keys.reshape(8, BLK, pair)
            acc[pl.ds(b, 3)] += d_keys[:3]
            acc[1:3] += d_keys[3:5]
            rand[pl.ds(row * 3, 3)] = d_keys[5:]
        hook(g)
        return carry

    lax.fori_loop(0, rows_here // unit, group, 0)

    @pl.when(me == 0)
    def _():
        top = slice(0, 2 * BLK)
        q_here, do_here = q_ref[top, cols], do_ref[top, cols]
        both = jnp.concatenate([q_here, do_here], axis=0)
        lse = lse_ref[h, top, :]
        delta = jnp.sum(do_here.astype(F32) * top_ref[h], axis=-1, keepdims=True)
        span = max(d for d in (16, 12, 8, 2) if total % d == 0)
        step = span * BLK

        def part(i, dq):
            keys = kv_ref[h, pl.ds(i * span, span)].reshape(step, pair)
            s_dp = dot_nt(both, keys)
            token = i * step + lax.broadcasted_iota(jnp.int32, (1, step), 1)
            p = jnp.exp(s_dp[: 2 * BLK] + jnp.where(token < length, 0.0, NEG) - lse)
            ds = (p * (s_dp[2 * BLK :] - delta)).astype(BF16)
            d_keys = dot_tn(jnp.concatenate([ds, p.astype(BF16)], axis=0), both)
            acc[pl.ds(1 + i * span, span)] += d_keys.reshape(span, BLK, pair)
            return dq + dot(ds, keys)

        dq = lax.fori_loop(0, total // span, part, jnp.zeros((2 * BLK, pair), F32))
        joined[top, cols] = dq.astype(BF16)

    sums[0] = jnp.zeros((BLK, pair), F32)

    def prefix(k, carry):
        carry = carry + rand[perm_ref[layer, h, k]]
        sums[k + 1] = carry
        return carry

    lax.fori_loop(0, rows_here * 3, prefix, jnp.zeros((BLK, pair), F32))
    several = 4 if total % 4 == 0 else 1

    def settle(i, carry):
        for u in range(several):
            j = i * several + u
            low, high = start_ref[layer, h, j], start_ref[layer, h, j + 1]
            dkv[h, j] = (acc[j + 1] + (sums[high] - sums[low])).astype(BF16)
        return carry

    lax.fori_loop(0, total // several, settle, 0)


def project_back_kernel(
    count,
    heads,
    owner,
    ids_ref,
    len_ref,
    perm_ref,
    start_ref,
    q_ref,
    kv_ref,
    do_ref,
    lse_ref,
    top_ref,
    dr1_ref,
    x_any,
    w_any,
    dense_any,
    extra_ref,
    *refs,
):
    if owner == 0:
        small_ref, refs = refs[0], refs[1:]
    gw_ref, gv_ref, dx_ref, both_ref, out_ref = refs[:5]
    refs = refs[5:]
    if owner == 0:
        small_done, refs = refs[0], refs[1:]
    result_ref, all_ref, part_any, done_ref = extra_ref, out_ref, extra_ref, out_ref
    x_ref, w_ref, dense_ref, load_sems, dkv, acc, rand, sums = refs[:8]
    handed, slots, joined, send_wide, recv_wide = refs[8:13]
    sq_send, sq_recv, sq_hold, sq_send_sem, sq_recv_sem, hand_sems, ready = refs[13:20]
    me = lax.axis_index("wide")
    mine = lax.axis_index("tensor")
    section = lax.axis_index("section")
    tok, width = x_ref.shape
    own = tok // 4
    pair = 2 * HW
    wide = heads * pair
    total = dkv.shape[1]
    rows_here = tok // BLK
    right, left = {"wide": lax.rem(me + 1, count)}, {"wide": lax.rem(me + count - 1, count)}
    loads = [
        pltpu.make_async_copy(src, dst, load_sems.at[i])
        for i, (src, dst) in enumerate(
            ((dense_any, dense_ref), (w_any.at[owner], w_ref), (x_any, x_ref))
        )
    ]
    for load in loads:
        load.start()
    barrier = wide_barrier(me, count)
    for offset in (1, 2):
        pl.semaphore_signal(
            barrier, inc=1, device_id={"tensor": tensor_peer(mine, offset)}, device_id_type=MESH
        )
    greet(barrier, section, 4)
    blocks = sub_blocks(own)
    sq = Square(mine, own, width, blocks, sq_send, sq_recv, sq_hold, sq_send_sem, sq_recv_sem)
    sq.scatters = (0,)
    split = dense_ref.shape[0] // 2 if owner == 1 else dense_ref.shape[0]
    low, high = pl.ds(0, split), pl.ds(split, dense_ref.shape[0] - split)

    def hand_over(rows, to):
        return remote(
            dense_ref.at[rows], handed.at[rows], hand_sems.at[0], hand_sems.at[1], {"section": to}
        )

    if owner == 0:
        part, cross, small_up, small_cross, part_sems, small_sems = refs[20:]
        line = Line(count)

        def small_in(source):
            return remote(source, small_up, small_sems.at[0], small_sems.at[1], line.inward)

        def small_across():
            return remote(small_up, small_cross, small_sems.at[2], small_sems.at[3], line.inward)

        def small_out():
            return remote(small_done, small_done, small_sems.at[4], small_sems.at[5], line.outward)

        load_part = pltpu.make_async_copy(part_any, part, part_sems.at[0])
        load_part.start()

        def across():
            return remote(part, cross, part_sems.at[1], part_sems.at[2], line.inward)

        def outwards():
            return remote(done_ref, done_ref, part_sems.at[3], part_sems.at[4], line.outward)

        load_part.wait()

        @pl.when(line.is_middle)
        def _():
            across().start()

        @pl.when(line.no_outer)
        def _():
            small_in(small_ref).start()

    loads[0].wait()

    @pl.when(section == 1)
    def _():
        hand_over(low, 0).start()

    if owner == 1:
        tell_ready(ready, section)
        for j in range(blocks):
            all_ref[sq.rows(mine, j), :] = result_ref[j * sq.sub : (j + 1) * sq.sub, :]
            sq.share(1, j, all_ref)
    has_right, has_left = me < count - 1, me > 0

    def keys(shard):
        return pl.ds(shard * rows_here, rows_here)

    def hop(side, shard, h):
        return remote(
            slots.at[side, shard, h],
            slots.at[side, shard, h],
            send_wide.at[side, shard, h],
            recv_wide.at[side, shard, h],
            right if side == 0 else left,
        )

    def pass_on(side, shard, h, more):
        @pl.when(more)
        def _():
            hop(side, shard, h).wait_recv()
            slots[side, shard, h] = (
                slots[side, shard, h].astype(F32) + dkv[h, keys(shard)].astype(F32)
            ).astype(BF16)

        @pl.when(jnp.logical_not(more))
        def _():
            slots[side, shard, h] = dkv[h, keys(shard)]

        hop(side, shard, h).start()

    def step(h, k):
        shard_r, shard_l = count - 1 - k, k

        def rightwards():
            @pl.when(shard_r > me)
            def _():
                pass_on(0, shard_r, h, has_left)

        def leftwards():
            @pl.when(shard_l < me)
            def _():
                pass_on(1, shard_l, h, has_right)

        @pl.when(me < count // 2)
        def _():
            rightwards()
            leftwards()

        @pl.when(me >= count // 2)
        def _():
            leftwards()
            rightwards()

    def steps(h, first):
        def one(k, carry):
            step(h, k)
            return carry

        lax.fori_loop(first, count - 1, one, 0)

    groups = rows_here // grouping(rows_here)
    state = (q_ref, kv_ref, do_ref, lse_ref, top_ref, joined, dkv, acc, rand, sums)
    for h in range(heads):

        def hook(g):
            if h > 0:

                @pl.when(g < count - 1)
                def _():
                    step(h - 1, g)

        attend_back(h, owner, total, (ids_ref, len_ref, perm_ref, start_ref), state, hook)
        if h > 0:
            steps(h - 1, groups)
        if owner == 0 and h == 0:

            @pl.when(line.has_outer)
            def _():
                small_in(small_ref).wait_recv()
                small_up[...] = (
                    small_up[...].astype(F32) + small_ref[...].astype(F32)
                ).astype(BF16)

            @pl.when(line.has_outer & line.is_middle)
            def _():
                small_across().start()

            @pl.when(line.has_outer & line.not_middle)
            def _():
                small_in(small_up).start()

        if owner == 0 and h == heads - 2:

            @pl.when(line.is_middle)
            def _():
                small_across().wait_recv()
                small_done[...] = (
                    small_up[...].astype(F32) + small_cross[...].astype(F32)
                ).astype(BF16)
                across().wait_recv()

                def add(i, carry):
                    span = pl.ds(pl.multiple_of(i * PIECE, 16), PIECE)
                    done_ref[span, :] = (
                        part[span, :].astype(F32) + cross[span, :].astype(F32)
                    ).astype(BF16)
                    return carry

                lax.fori_loop(0, part.shape[0] // PIECE, add, 0)

            @pl.when(line.is_middle & line.has_outer)
            def _():
                small_out().start()
                outwards().start()

    if owner == 1:

        @pl.when(section == 0)
        def _():
            pl.semaphore_wait(ready, 1)
            hand_over(high, 1).start()

    steps(heads - 1, 0)
    for load in loads[1:]:
        load.wait()

    def add_up(first, last):
        def add(i, carry):
            span = pl.ds(pl.multiple_of(i * PIECE, 16), PIECE)
            both_ref[span, :] = (
                dense_ref[span, :].astype(F32) + handed[span, :].astype(F32)
            ).astype(BF16)
            return carry

        lax.fori_loop(first, last, add, 0)

    @pl.when(section == 0)
    def _():
        hand_over(low, 0).wait_recv()
        add_up(0, split // PIECE)

    if owner == 1:

        @pl.when(section == 1)
        def _():
            hand_over(high, 1).wait_recv()
            add_up(split // PIECE, dense_ref.shape[0] // PIECE)

    for h in range(heads):
        cols = slice(wide + h * pair, wide + (h + 1) * pair)

        @pl.when(has_left)
        def _():
            hop(0, me, h).wait_recv()

        @pl.when(has_right)
        def _():
            hop(1, me, h).wait_recv()

        here = dkv[h, keys(me)].astype(F32)
        from_left = jnp.where(has_left, slots[0, me, h].astype(F32), 0.0)
        from_right = jnp.where(has_right, slots[1, me, h].astype(F32), 0.0)
        joined[:, cols] = (here + from_left + from_right).astype(BF16).reshape(tok, pair)

    if owner == 1:
        for j in range(blocks):
            sq.relay_share(1, j, all_ref)

    def back(index, j):
        return dot(joined[sq.rows(index, j), :], w_ref[...])

    for j in range(blocks):
        sq.give_diagonal(0, j, back(sq.d, j))
    for j in range(blocks):
        sq.give_x(0, j, back(sq.x, j))
        sq.give_y(0, j, back(sq.y, j))
    for j in range(blocks):
        sq.relay_sum(0, j)
    for h in range(heads):
        at = h * 2 * HW
        gw_ref[h * HW : (h + 1) * HW, :] = dot_tn(joined[:, at : at + 2 * HW], x_ref[...])[
            :HW
        ].astype(BF16)
        gw_ref[heads * HW + at : heads * HW + at + 2 * HW, :] = dot_tn(
            joined[:, wide + at : wide + at + 2 * HW], x_ref[...]
        ).astype(BF16)
    gv_ref[...] = jnp.sum(joined[...].astype(F32), axis=0, keepdims=True)
    for j in range(blocks):
        rows = slice(j * sq.sub, (j + 1) * sq.sub)
        total = sq.total(0, j, back(mine, j) + dr1_ref[rows, :]).astype(BF16)
        dx_ref[rows, :] = total
    if owner == 1:
        for j in range(blocks):
            sq.have_all(1, j, all_ref)
    sq.close()

    @pl.when(section == 1)
    def _():
        hand_over(low, 0).wait_send()

    if owner == 1:

        @pl.when(section == 0)
        def _():
            hand_over(high, 1).wait_send()

    if owner == 0:

        @pl.when(line.is_middle)
        def _():
            small_across().wait_send()
            across().wait_send()

        @pl.when(line.not_middle)
        def _():
            small_in(small_ref).wait_send()
            small_out().wait_recv()
            outwards().wait_recv()

        @pl.when(line.not_middle & line.has_outer)
        def _():
            small_out().start()
            outwards().start()

        @pl.when(line.has_outer)
        def _():
            small_out().wait_send()
            outwards().wait_send()

    def drain(k, carry):
        shard_r, shard_l = count - 1 - k, k
        for h in range(heads):

            @pl.when(shard_r > me)
            def _():
                hop(0, shard_r, h).wait_send()

            @pl.when(shard_l < me)
            def _():
                hop(1, shard_l, h).wait_send()

        return carry

    lax.fori_loop(0, count - 1, drain, 0)


def project_back(
    scalars_, q, kv, do, lse, top, x, dr1, wt, gw, extra, small, layer, count, collective_id
):
    tok, width = x.shape
    heads, total, _, pair = kv.shape
    own = tok // 4
    wide = heads * pair
    rows_here = tok // BLK
    operands = [q, kv, do, lse, top, dr1]
    out = (tok, width) if layer == 1 else extra.shape
    parts = []
    if layer == 0:
        parts = [pltpu.VMEM(out, BF16)] * 2 + [pltpu.VMEM(small[0].shape, BF16)] * 2
        parts += [pltpu.SemaphoreType.DMA((5,)), pltpu.SemaphoreType.DMA((6,))]
    return pl.pallas_call(
        functools.partial(project_back_kernel, count, heads, layer),
        out_shape=[
            jax.ShapeDtypeStruct((wide + wide // 2, width), BF16),
            jax.ShapeDtypeStruct((1, 2 * wide), F32),
            jax.ShapeDtypeStruct((own, width), BF16),
            jax.ShapeDtypeStruct(gw.shape, BF16),
        ]
        + [jax.ShapeDtypeStruct(out, BF16)]
        + [jax.ShapeDtypeStruct(a.shape, BF16) for a in small],
        grid=(1,),
        in_specs=[scalars()] * 4
        + [whole(*a.shape) for a in operands]
        + [anywhere()] * 3
        + [whole(own, width) if layer == 1 else anywhere()]
        + [whole(*a.shape) for a in small],
        out_specs=[
            whole(wide + wide // 2, width),
            whole(1, 2 * wide),
            whole(own, width),
            whole(*gw.shape),
        ]
        + [whole(*out)]
        + [whole(*a.shape) for a in small],
        scratch_shapes=[
            pltpu.VMEM((tok, width), BF16),
            pltpu.VMEM((2 * wide, width), BF16),
            pltpu.VMEM(gw.shape, BF16),
            pltpu.SemaphoreType.DMA((3,)),
            pltpu.VMEM((heads, total, BLK, pair), BF16),
            pltpu.VMEM((total + 2, BLK, pair), F32),
            pltpu.VMEM((rows_here * 3, BLK, pair), F32),
            pltpu.VMEM((rows_here * 3 + 1, BLK, pair), F32),
            pltpu.VMEM(gw.shape, BF16),
            pltpu.VMEM((2, count, heads, rows_here, BLK, pair), BF16),
            pltpu.VMEM((tok, 2 * wide), BF16),
            pltpu.SemaphoreType.DMA((2, count, heads)),
            pltpu.SemaphoreType.DMA((2, count, heads)),
        ]
        + square_scratch(1, 2, own, width)
        + [pltpu.SemaphoreType.DMA((2,)), pltpu.SemaphoreType.REGULAR]
        + parts,
        compiler_params=params(collective_id),
        name="project_back",
    )(*scalars_, *operands, x, wt, gw, extra, *small)


def greet(barrier, section, expected):
    @pl.when(section == 0)
    def _():
        pl.semaphore_signal(barrier, inc=1, device_id={"section": 1}, device_id_type=MESH)

    pl.semaphore_wait(barrier, expected + section)


def tell_ready(ready, section):
    @pl.when(section == 1)
    def _():
        pl.semaphore_signal(ready, inc=1, device_id={"section": 0}, device_id_type=MESH)


def await_ready(ready, section):
    @pl.when(section == 0)
    def _():
        pl.semaphore_wait(ready, 1)


class Line:
    def __init__(self, count):
        w = lax.axis_index("wide")
        middle = count // 2
        low = w < middle
        self.inward = {"wide": jnp.where(low, w + 1, w - 1)}
        self.outward = {"wide": lax.rem(jnp.where(low, w + count - 1, w + 1), count)}
        self.has_outer = (w > 0) & (w < count - 1)
        self.no_outer = (w == 0) | (w == count - 1)
        self.is_middle = (w == middle - 1) | (w == middle)
        self.not_middle = (w < middle - 1) | (w > middle)


class Chain:
    def __init__(self, count, section, owner, sect, up, done, sems, segments):
        self.sect, self.up, self.done = sect, up, done
        self.r_sect, self.s_in, self.r_up, self.r_done, self.s_out, self.s_sect = sems
        self.segments = segments
        w = lax.axis_index("wide")
        middle = count // 2
        low = w < middle
        self.inward = {"wide": jnp.where(low, w + 1, w - 1)}
        self.outward = {"wide": lax.rem(jnp.where(low, w + count - 1, w + 1), count)}
        self.has_outer = (w > 0) & (w < count - 1)
        self.no_outer = (w == 0) | (w == count - 1)
        self.is_middle = (w == middle - 1) | (w == middle)
        self.not_middle = (w < middle - 1) | (w > middle)
        self.owner, self.mine = owner, section == owner
        self.other = {"section": 1 - section}

    def span(self, i, base):
        return pl.ds(pl.multiple_of((i - base) * PIECE, 16), PIECE)

    def size(self):
        return sum(size for _, _, _, size, _ in self.segments)

    def first(self):
        return min(start for _, _, start, _, _ in self.segments)

    def handed(self, ref, i, base):
        return remote(
            ref.at[self.span(i, base)],
            self.sect.at[i],
            self.s_sect.at[i],
            self.r_sect.at[i],
            self.other,
        )

    def to_up(self, i):
        return remote(self.sect.at[i], self.up.at[i], self.s_in.at[i], self.r_up.at[i], self.inward)

    def to_middle(self, i):
        return remote(
            self.sect.at[i], self.done.at[i], self.s_in.at[i], self.r_done.at[i], self.inward
        )

    def to_outer(self, i):
        return remote(
            self.done.at[i], self.done.at[i], self.s_out.at[i], self.r_done.at[i], self.outward
        )

    def pieces(self, lo, hi, body):
        for ref, base, start, size, shared in self.segments:
            first, last = max(lo, start), min(hi, start + size)
            if first < last:

                def step(i, carry, ref=ref, base=base, shared=shared):
                    body(i, ref, base, shared)
                    return carry

                lax.fori_loop(first, last, step, 0)

    def hand_over(self):
        @pl.when(jnp.logical_not(self.mine))
        def _():
            def step(i, ref, base, shared):
                if shared:
                    self.handed(ref, i, base).start()

            self.pieces(0, 1 << 20, step)

    def add(self, i, ref, base, shared):
        value = ref[self.span(i, base), :].astype(F32)
        if shared:
            self.handed(ref, i, base).wait_recv()
            value += self.sect[i].astype(F32)
        return value

    def send_in(self, i):
        @pl.when(self.is_middle)
        def _():
            self.to_middle(i).start()

        @pl.when(self.not_middle)
        def _():
            self.to_up(i).start()

    def give(self, i, ref, base, shared):
        self.sect[i] = self.add(i, ref, base, shared).astype(BF16)
        self.send_in(i)

    def relay(self, i, ref, base, shared):
        value = self.add(i, ref, base, shared)
        self.to_up(i).wait_recv()
        self.sect[i] = (value + self.up[i].astype(F32)).astype(BF16)
        self.send_in(i)

    def settle(self, i, ref, base, shared):
        self.to_middle(i).wait_recv()

        @pl.when(self.is_middle)
        def _():
            self.done[i] = (self.sect[i].astype(F32) + self.done[i].astype(F32)).astype(BF16)

        @pl.when(self.has_outer)
        def _():
            self.to_outer(i).start()

    def inwards(self, lo, hi):
        @pl.when(self.mine & self.no_outer)
        def _():
            self.pieces(lo, hi, self.give)

        @pl.when(self.mine & self.has_outer)
        def _():
            for i in range(lo, hi):
                self.pieces(i, i + 1, self.relay)
                self.pieces(i - LAG, i - LAG + 1, self.settle)

    def rest(self):
        end = self.first() + self.size()

        @pl.when(self.mine & self.no_outer)
        def _():
            self.pieces(0, end, self.settle)

        @pl.when(self.mine & self.has_outer)
        def _():
            self.pieces(end - LAG, end, self.settle)

    def close(self):
        @pl.when(self.mine)
        def _():
            self.pieces(0, 1 << 20, lambda i, ref, base, shared: self.to_up(i).wait_send())

        @pl.when(self.mine & self.has_outer)
        def _():
            self.pieces(0, 1 << 20, lambda i, ref, base, shared: self.to_outer(i).wait_send())

        @pl.when(jnp.logical_not(self.mine))
        def _():
            def step(i, ref, base, shared):
                if shared:
                    self.handed(ref, i, base).wait_send()

            self.pieces(0, 1 << 20, step)


def chain_scratch(pieces, width):
    return [pltpu.VMEM((pieces, PIECE, width), BF16)] * 2 + [
        pltpu.SemaphoreType.DMA((pieces,))
    ] * 6


def finish_kernel(
    count,
    gqkv_ref,
    gw_ref,
    gvq0_ref,
    gv0_ref,
    gvq1_ref,
    gv1_ref,
    result_ref,
    dx_ref,
    old_ref,
    small_ref,
    done_ref,
    vout_ref,
    far_ref,
    all_ref,
    got_ref,
    got_small,
    vec_ref,
    sect,
    up,
    c0,
    c1,
    c2,
    c3,
    c4,
    c5,
    vsect,
    vtens,
    vup,
    vpart,
    vfin_in,
    vfin,
    vs,
    vr,
    ts,
    tr,
    far_sems,
    ready,
    *square,
):
    section = lax.axis_index("section")
    w = lax.axis_index("wide")
    t = lax.axis_index("tensor")
    barrier = wide_barrier(w, count)
    for offset in (1, 2, 3):
        pl.semaphore_signal(
            barrier, inc=1, device_id={"tensor": tensor_peer(t, offset)}, device_id_type=MESH
        )
    greet(barrier, section, 5)
    tell_ready(ready, section)
    own, width = dx_ref.shape
    blocks = sub_blocks(own)
    sq = Square(t, own, width, blocks, *square)
    sq.scatters = ()
    for at, gvq, gv in ((0, gvq0_ref, gv0_ref), (8, gvq1_ref, gv1_ref)):
        vec_ref[at : at + 1, :] = gvq[...]
        vec_ref[at + 1 : at + 8, :] = gv[1:8, :]
    gw_pieces = gw_ref.shape[0] // PIECE
    qkv_pieces = gqkv_ref.shape[0] // PIECE
    total = gw_pieces + qkv_pieces
    sems = (c0, c1, c2, c3, c4, c5)
    chain = Chain(
        count,
        section,
        0,
        sect,
        up,
        done_ref,
        sems,
        [(gw_ref, 0, 0, gw_pieces, False), (gqkv_ref, gw_pieces, gw_pieces, qkv_pieces, True)],
    )
    inward, outward, other = chain.inward, chain.outward, chain.other
    mine = pl.ds(pl.multiple_of(section * 8, 8), 8)
    theirs = pl.ds(pl.multiple_of(8 - section * 8, 8), 8)

    def v_other():
        return remote(vec_ref.at[theirs], vsect, vs.at[0], vr.at[0], other)

    def v_peer(offset, slot):
        return remote(
            vtens.at[t],
            vtens.at[slot],
            ts.at[offset - 1],
            tr.at[offset - 1],
            {"tensor": tensor_peer(t, offset)},
        )

    def v_up():
        return remote(vpart, vup, vs.at[1], vr.at[1], inward)

    def v_middle():
        return remote(vpart, vfin_in, vs.at[1], vr.at[2], inward)

    def v_outer():
        return remote(vfin, vfin_in, vs.at[2], vr.at[2], outward)

    chain.hand_over()

    def far(ref):
        return remote(ref, far_ref, far_sems.at[0], far_sems.at[1], other)

    def hand_small():
        return remote(small_ref, got_small, far_sems.at[4], far_sems.at[5], other)

    def hand_done():
        return remote(
            old_ref, got_ref, far_sems.at[2], far_sems.at[3], other
        )

    for j in range(blocks):
        all_ref[sq.rows(t, j), :] = dx_ref[j * sq.sub : (j + 1) * sq.sub, :]
        sq.share(0, j, all_ref)
    for j in range(blocks):
        sq.relay_share(0, j, all_ref)
    chain.inwards(0, gw_pieces)
    await_ready(ready, section)
    v_other().start()

    @pl.when(section == 0)
    def _():
        far(result_ref).start()
        hand_small().start()
        hand_done().start()

    v_other().wait_recv()
    vtens[t] = vec_ref[mine, :] + vsect[...]
    for offset in (1, 2, 3):
        v_peer(offset, t).start()
    chain.inwards(gw_pieces, total)
    for j in range(blocks):
        sq.have_all(0, j, all_ref)

    @pl.when(section == 1)
    def _():
        far(all_ref).start()

    for offset in (1, 2, 3):
        v_peer(offset, tensor_peer(t, offset)).wait_recv()
    shared = vtens[0] + vtens[1] + vtens[2] + vtens[3]
    row = lax.broadcasted_iota(jnp.int32, shared.shape, 0)
    value = jnp.where((row == 0) | (row == 4), vtens[t], shared)

    @pl.when(chain.has_outer)
    def _():
        v_up().wait_recv()
        vpart[...] = value + vup[...]

    @pl.when(chain.no_outer)
    def _():
        vpart[...] = value

    @pl.when(chain.is_middle)
    def _():
        v_middle().start()

    @pl.when(chain.not_middle)
    def _():
        v_up().start()

    chain.rest()
    v_middle().wait_recv()

    @pl.when(chain.is_middle)
    def _():
        vfin[...] = vpart[...] + vfin_in[...]

    @pl.when(chain.not_middle)
    def _():
        vfin[...] = vfin_in[...]

    @pl.when(chain.has_outer)
    def _():
        v_outer().start()

    vout_ref[...] = vfin[...]
    chain.close()
    sq.close()
    far(all_ref).wait()

    @pl.when(section == 0)
    def _():
        hand_small().wait_send()
        hand_done().wait_send()

    @pl.when(section == 1)
    def _():
        hand_small().wait_recv()
        hand_done().wait_recv()

    v_other().wait_send()
    v_up().wait_send()
    for offset in (1, 2, 3):
        v_peer(offset, t).wait_send()

    @pl.when(chain.has_outer)
    def _():
        v_outer().wait_send()


def finish(gqkv, gw, vectors, result, dx, old, small_old, count, collective_id):
    own, width = dx.shape
    tok = own * 4
    pieces = (gqkv.shape[0] + gw.shape[0]) // PIECE
    small = pltpu.VMEM((8, width), F32)
    operands = [gqkv, gw, *vectors, result, dx, old, small_old]
    return pl.pallas_call(
        functools.partial(finish_kernel, count),
        out_shape=[
            jax.ShapeDtypeStruct((pieces, PIECE, width), BF16),
            jax.ShapeDtypeStruct((8, width), F32),
            jax.ShapeDtypeStruct((tok, width), BF16),
            jax.ShapeDtypeStruct((tok, width), BF16),
            jax.ShapeDtypeStruct(old.shape, BF16),
            jax.ShapeDtypeStruct(small_old.shape, BF16),
        ],
        grid=(1,),
        in_specs=[whole(*a.shape) for a in operands],
        out_specs=[whole(pieces, PIECE, width), whole(8, width)]
        + [whole(tok, width)] * 2
        + [whole(*old.shape), whole(*small_old.shape)],
        scratch_shapes=[pltpu.VMEM((16, width), F32)]
        + chain_scratch(pieces, width)
        + [small, pltpu.VMEM((4, 8, width), F32)]
        + [small] * 4
        + [pltpu.SemaphoreType.DMA((3,))] * 4
        + [pltpu.SemaphoreType.DMA((6,)), pltpu.SemaphoreType.REGULAR]
        + square_scratch(1, 1, own, width),
        compiler_params=params(collective_id),
        name="finish",
    )(*operands)


def unpack_kernel(
    heads,
    sums_ref,
    low_ref,
    high_ref,
    low_small,
    high_small,
    dx_ref,
    result_ref,
    far_ref,
    vec_ref,
    ends_ref,
    gq_ref,
    gbq_ref,
    gk_ref,
    gv_ref,
    gbv_ref,
    go_ref,
    gbo_ref,
    g1_ref,
    b1_ref,
    gi_ref,
    gbi_ref,
    gf_ref,
    gbf_ref,
    g2_ref,
    b2_ref,
    buf,
    sems,
):
    section = lax.axis_index("section")
    width = gi_ref.shape[1]
    narrow = heads * HW
    wide = heads * 2 * HW
    half = low_ref.shape[0]
    low, high = pl.ds(0, half), pl.ds(half, half)
    few = low_small.shape[0]
    spans = (low, high, pl.ds(2 * half, few), pl.ds(2 * half + few, few))
    targets = tuple(buf.at[span] for span in spans)
    targets += (ends_ref.at[0, 0, 0], ends_ref.at[0, 1, 0])

    def copy(i, source):
        return pltpu.make_async_copy(source, targets[i], sems.at[i])

    @pl.when(section == 0)
    def _():
        for i, source in enumerate(
            tuple(sums_ref.at[span] for span in spans) + (dx_ref, far_ref)
        ):
            copy(i, source).start()

    @pl.when(section != 0)
    def _():
        for i, source in enumerate(
            (low_ref, high_ref, low_small, high_small, far_ref, result_ref)
        ):
            copy(i, source).start()

    for i, ref in (
        (1, gbo_ref),
        (2, g1_ref),
        (3, b1_ref),
        (4, gbi_ref),
        (5, gbf_ref),
        (6, g2_ref),
        (7, b2_ref),
    ):
        ref[...] = vec_ref[i : i + 1, :]
    row = vec_ref[0:1, :]
    cuts = [(h * 2 * HW, wide + h * 2 * HW + HW) for h in range(heads)]
    gbq_ref[...] = 0.125 * jnp.concatenate([row[:, q : q + HW] for q, _ in cuts], axis=1)
    gbv_ref[...] = jnp.concatenate([row[:, v : v + HW] for _, v in cuts], axis=1)
    for i, source in enumerate((low_ref, high_ref, low_small, high_small)):
        copy(i, source).wait()

    def take(out, scale, source, size):
        value = buf[source : source + size, :].astype(F32)
        out(0, size, value if scale is None else scale * value)

    def into(ref, first=0):
        def put(at, span, value):
            ref[0, first + at : first + at + span, :] = value

        return put

    take(into(gi_ref), None, 0, width)
    take(into(gf_ref), None, width, width)
    take(into(go_ref), None, 2 * width, narrow)
    take(into(gq_ref), 0.125, 2 * width + narrow, narrow)
    for h in range(heads):
        source = 2 * width + 2 * narrow + h * 2 * HW
        take(into(gk_ref, h * HW), None, source, HW)
        take(into(gv_ref, h * HW), None, source + HW, HW)
    for i in (4, 5):
        copy(i, far_ref).wait()


def unpack(sums, low, high, low_small, high_small, dx, result, far, vec, heads):
    rows, width = sums.shape
    narrow = heads * HW
    ends = jax.ShapeDtypeStruct((1, 2, 1) + dx.shape, BF16)
    slim = jax.ShapeDtypeStruct((1, narrow, width), F32)
    full = jax.ShapeDtypeStruct((1, width, width), F32)
    line = jax.ShapeDtypeStruct((1, width), F32)
    short = jax.ShapeDtypeStruct((1, narrow), F32)
    shapes = [ends, slim, short, slim, slim, short, slim, line, line, line]
    shapes += [full, line, full, line, line, line]
    return pl.pallas_call(
        functools.partial(unpack_kernel, heads),
        out_shape=shapes,
        grid=(1,),
        in_specs=[anywhere()] * 8 + [whole(*vec.shape)],
        out_specs=[whole(*a.shape) for a in shapes],
        scratch_shapes=[pltpu.VMEM((rows, width), BF16), pltpu.SemaphoreType.DMA((6,))],
        compiler_params=params(),
        name="unpack",
    )(sums, low, high, low_small, high_small, dx, result, far, vec)


def body(
    inputs,
    target,
    pad_mask,
    loss_mask,
    rand_blocks,
    w_query,
    b_query,
    w_key,
    w_value,
    b_value,
    w_out,
    b_out,
    ln1_gain,
    ln1_bias,
    w_in,
    b_in,
    w_ffn,
    b_ffn,
    ln2_gain,
    ln2_bias,
):
    section = lax.axis_index("section")
    count = lax.axis_size("wide")
    micro, _, tok, width = inputs.shape
    total = pad_mask.shape[2] // BLK
    heads = w_query.shape[2] // HW
    wide = heads * 2 * HW

    rand = rand_blocks[0].reshape(heads, -1)
    far_rand = lax.ppermute(rand, "section", [(0, 1), (1, 0)])
    ids = jnp.where(section == 0, jnp.stack([rand, far_rand]), jnp.stack([far_rand, rand]))
    here = lax.dynamic_slice_in_dim(ids, lax.axis_index("wide") * (tok // BLK * 3), tok // BLK * 3, 2)
    slot = jnp.arange(here.shape[2], dtype=jnp.int32)
    order = here * here.shape[2] + slot
    rank = jnp.sum((order[..., None, :] < order[..., :, None]).astype(jnp.int32), axis=-1)
    perm = jnp.sum(jnp.where(rank[..., None, :] == slot[:, None], slot, 0), axis=-1)
    block = jnp.arange(total + 1, dtype=jnp.int32)
    starts = jnp.sum((here[..., None, :] < block[:, None]).astype(jnp.int32), axis=-1)
    weight = (loss_mask * pad_mask).astype(F32).reshape(micro, -1, tok // 4)
    length = jnp.sum(lax.dynamic_index_in_dim(pad_mask, section, 0), axis=(0, 1, 2))[None]
    matrices = [jnp.swapaxes(m, 1, 2)[0] for m in (w_query, w_key, w_value)]
    matrices += [w_in[0], w_ffn[0], w_out[0]]
    vectors = [b_query, b_value, b_out, ln1_gain, ln1_bias, b_in, b_ffn, ln2_gain, ln2_bias]
    x, q, kv, att, lse, top, wt, vall, win, wffn, wout = begin(
        ids, length, inputs, matrices, vectors, count, heads, 2
    )

    saved = []
    for layer in range(2):
        if layer == 1:
            q, kv, att, lse, top = project(ids, length, x, wt, vall, layer, count, heads, 3)
        mixed, active, slope, r1, r2, x_next = dense(
            att, x, wout, win, wffn, vall, layer, 4 + layer
        )
        saved.append((x, q, kv, att, lse, top, mixed, active, slope, r1, r2))
        x = x_next
    result, grad, handed, vector_grads = x, target, (), [None, None]
    for layer in (1, 0):
        x, q, kv, att, lse, top, mixed, active, slope, r1, r2 = saved[layer]
        gw, gv, do, dr1, *middle = dense_back(
            grad,
            weight,
            r2,
            r1,
            slope,
            active,
            mixed,
            att,
            wout,
            win,
            wffn,
            vall,
            layer,
            count,
            6 + layer,
            handed,
        )
        scalars_ = (ids, length, perm, starts)
        extra, small = (result, []) if layer == 1 else (middle[0], [middle[1]])
        gqkv, gvq, grad, gw_both, out, *small_done = project_back(
            scalars_, q, kv, do, lse, top, x, dr1, wt, gw, extra, small, layer, count, 8 + layer
        )
        vector_grads[layer] = [gvq, gv]
        if layer == 1:
            handed, result = (gw_both, gqkv), out

    vectors = vector_grads[0] + vector_grads[1]
    sums, vec, far, dx, low, low_small = finish(
        gqkv, gw_both, vectors, result, grad, out, small_done[0], count, 10
    )
    ends, gq, gbq, gk, gvalue, gbv, gout, *rest = unpack(
        sums.reshape(-1, width), low, out, low_small, small_done[0], dx, result, far, vec, heads
    )
    return (
        ends,
        jnp.swapaxes(gq, 1, 2),
        gbq,
        jnp.swapaxes(gk, 1, 2),
        jnp.swapaxes(gvalue, 1, 2),
        gbv,
        gout,
        *rest,
    )


def solution(mesh):
    matrix = P("section", None, "tensor")
    rowwise = P("section", "tensor", None)
    cut = P("section", "tensor")
    plain = P("section", None)
    return jax.shard_map(
        body,
        mesh=mesh,
        in_specs=(
            P(None, None, "wide", None),
            P(None, None, "wide", None),
            P(),
            P(),
            P("section", "tensor", None, None),
            matrix,
            cut,
            matrix,
            matrix,
            cut,
            rowwise,
            plain,
            plain,
            plain,
            matrix,
            cut,
            rowwise,
            plain,
            plain,
            plain,
        ),
        out_specs=(
            P("section", None, None, "wide", None),
            matrix,
            cut,
            matrix,
            matrix,
            cut,
            rowwise,
            plain,
            plain,
            plain,
            matrix,
            cut,
            rowwise,
            plain,
            plain,
            plain,
        ),
        check_vma=False,
    )
```

```python
import functools

import jax
import jax.numpy as jnp
from jax import lax
from jax.experimental import pallas as pl
from jax.experimental.pallas import tpu as pltpu
from jax.sharding import PartitionSpec as P

HW = 64
BLK = 64
EPS = 1e-06
NEG = -1e30
MESH = pl.DeviceIdType.MESH
F32 = jnp.float32
BF16 = jnp.bfloat16
VMEM_BYTES = 56 * 1024 * 1024
GELU_C = 0.7978845608
GELU_A = 0.044715
NT_DIMS = (((1,), (1,)), ((), ()))
TN_DIMS = (((0,), (0,)), ((), ()))
ORDER = (3, 1, 2)
PIECE = 144
LAG = 2


def dot(a, b):
    return jnp.dot(a, b, preferred_element_type=F32)


def dot_nt(a, b):
    return lax.dot_general(a, b, NT_DIMS, preferred_element_type=F32)


def dot_tn(a, b):
    return lax.dot_general(a, b, TN_DIMS, preferred_element_type=F32)


def vmem():
    return pl.BlockSpec(memory_space=pltpu.VMEM)


def anywhere():
    return pl.BlockSpec(memory_space=pl.ANY)


def whole(*shape):
    return pl.BlockSpec(shape, lambda i: (0,) * len(shape))


def of_layer(array, layer):
    return pl.BlockSpec((None,) + array.shape[1:], lambda i: (layer,) + (0,) * (array.ndim - 1))


def remote(src, dst, send_sem, recv_sem, device):
    return pltpu.make_async_remote_copy(
        src_ref=src,
        dst_ref=dst,
        send_sem=send_sem,
        recv_sem=recv_sem,
        device_id=device,
        device_id_type=MESH,
    )


def tensor_peer(me, offset):
    if offset == 1:
        return me + 1 - 2 * lax.rem(me, 2)
    if offset == 2:
        return lax.rem(me + 2, 4)
    return 3 - me


def tensor_barrier(me):
    barrier = pltpu.get_barrier_semaphore()
    for offset in (1, 2, 3):
        pl.semaphore_signal(
            barrier, inc=1, device_id={"tensor": tensor_peer(me, offset)}, device_id_type=MESH
        )
    return barrier


def params(collective_id=None):
    if collective_id is None:
        return pltpu.CompilerParams(vmem_limit_bytes=VMEM_BYTES)
    return pltpu.CompilerParams(
        vmem_limit_bytes=VMEM_BYTES, collective_id=collective_id, has_side_effects=True
    )


def key_blocks(ids_ref, layer, head, row, first, total):
    b = first + row
    start = jnp.clip(b - 1, 0, total - 3)
    window = [start, start + 1, start + 2]
    r = [ids_ref[layer, head, b * 3 + k] for k in range(3)]

    def far(block):
        return (block < b - 1) | (block > b + 1)

    fresh = [far(k) & (k >= 2) for k in r]
    allowed = [jnp.logical_not(far(k)) for k in window]
    allowed += [far(jnp.int32(0)), far(jnp.int32(1))]
    allowed += [fresh[0], fresh[1] & (r[1] != r[0]), fresh[2] & (r[2] != r[0]) & (r[2] != r[1])]
    return window + [jnp.int32(0), jnp.int32(1)] + r, allowed


def back_blocks(ids_ref, layer, head, b, total):
    blocks, allowed = key_blocks(ids_ref, layer, head, 0, b, total)
    window = [jnp.maximum(b - 1, 0), b, jnp.minimum(b + 1, total - 1)]
    return window + blocks[3:], [b >= 1, b >= 0, b + 1 < total] + allowed[3:]


def key_bias(blocks, allowed, length):
    lane = lax.broadcasted_iota(jnp.int32, (1, 8 * BLK), 1)
    slot = lane // BLK
    limit = jnp.zeros((1, 8 * BLK), jnp.int32)
    for s in range(8):
        tokens = jnp.where(allowed[s], jnp.clip(length - blocks[s] * BLK, 0, BLK), 0)
        limit = jnp.where(slot == s, tokens, limit)
    return jnp.where(lane - slot * BLK < limit, 0.0, NEG)


def gathered(kv_ref, blocks):
    window = kv_ref[pl.ds(blocks[0], 3)].reshape(3 * BLK, -1)
    ends = kv_ref[0:2].reshape(2 * BLK, -1)
    return jnp.concatenate([window, ends] + [kv_ref[k] for k in blocks[5:]], axis=0)


def grouping(rows_here):
    return max(u for u in (4, 3, 2, 1) if rows_here % u == 0)


def wide_barrier(me, count):
    barrier = pltpu.get_barrier_semaphore()
    for side in (1, count - 1):
        pl.semaphore_signal(
            barrier,
            inc=1,
            device_id={"wide": lax.rem(me + side, count)},
            device_id_type=MESH,
        )
    return barrier


def softmax_values(s, keys):
    peak = jnp.max(s, axis=-1, keepdims=True)
    e = jnp.exp(s - peak)
    mass = jnp.sum(e, axis=-1, keepdims=True)
    return dot(e.astype(BF16), keys) / mass, peak + jnp.log(mass)


def gather_attend(
    count, heads, layer, x_ref, wt_ref, bias, ids_ref, len_ref, outs, scratch, ready, finished
):
    q_ref, kv_ref, att_ref, lse_ref, top_ref = outs
    held, (save, send_r, recv_r, send_l, recv_l) = scratch[:heads], scratch[heads:]
    me = lax.axis_index("wide")
    tok = x_ref.shape[0]
    right, left = {"wide": lax.rem(me + 1, count)}, {"wide": lax.rem(me + count - 1, count)}
    pair = 2 * HW
    wide = heads * pair
    has_right, has_left = me < count - 1, me > 0
    length = len_ref[0]
    rows_here = tok // BLK
    total = held[0].shape[0]
    unit = grouping(rows_here)
    groups = rows_here // unit

    def rows(shard):
        return pl.ds(shard * rows_here, rows_here)

    kv = dot_nt(x_ref[...], wt_ref[wide:, :]) + bias[:, wide:]
    for h in range(heads):
        own = kv[:, h * pair : (h + 1) * pair].astype(BF16)
        held[h][rows(me)] = own.reshape(rows_here, BLK, pair)
    ready()

    def copy_r(h, shard, step):
        part = held[h].at[rows(shard)]
        return remote(part, part, send_r.at[h, step], recv_r.at[h, shard], right)

    def copy_l(h, shard, step):
        part = held[h].at[rows(shard)]
        return remote(part, part, send_l.at[h, step], recv_l.at[h, shard], left)

    for h in range(heads):

        @pl.when(has_right)
        def _():
            copy_r(h, me, 0).start()

        @pl.when(has_left)
        def _():
            copy_l(h, me, 0).start()

    q = dot_nt(x_ref[...], wt_ref[:wide, :]) + bias[:, :wide]
    q_ref[...] = q.astype(BF16)

    def forward(h, step):
        shard_r, shard_l = me - step, me + step

        @pl.when(shard_r >= 0)
        def _():
            copy_r(h, shard_r, step).wait_recv()

            @pl.when(has_right)
            def _():
                copy_r(h, shard_r, step).start()

        @pl.when(shard_l < count)
        def _():
            copy_l(h, shard_l, step).wait_recv()

            @pl.when(has_left)
            def _():
                copy_l(h, shard_l, step).start()

    def forward_from(h, first):
        def step(k, carry):
            forward(h, k)
            return carry

        lax.fori_loop(first, count, step, 0)

    forward_from(0, 1)
    for h in range(heads):
        pltpu.make_async_copy(held[h], kv_ref.at[h], save.at[h]).start()
        cols = slice(h * pair, (h + 1) * pair)

        def group(g, carry):
            for u in range(unit):
                row = g * unit + u
                here = pl.ds(pl.multiple_of(row * BLK, BLK), BLK)
                blocks, allowed = key_blocks(ids_ref, layer, h, row, me * rows_here, total)
                keys = gathered(held[h], blocks)
                s = dot_nt(q_ref[here, cols], keys) + key_bias(blocks, allowed, length)
                o, lse = softmax_values(s, keys)
                att_ref[here, cols] = o.astype(BF16)
                lse_ref[h, here, :] = lse
            if h + 1 < heads:

                @pl.when(g + 1 < count)
                def _():
                    forward(h + 1, g + 1)

            return carry

        lax.fori_loop(0, groups, group, 0)
        if h + 1 < heads:
            forward_from(h + 1, groups + 1)

        @pl.when(me == 0)
        def _():
            keys = held[h][...].reshape(total * BLK, pair)
            token = lax.broadcasted_iota(jnp.int32, (1, keys.shape[0]), 1)
            s = dot_nt(q_ref[0 : 2 * BLK, cols], keys) + jnp.where(token < length, 0.0, NEG)
            o, lse = softmax_values(s, keys)
            att_ref[0 : 2 * BLK, cols] = o.astype(BF16)
            lse_ref[h, 0 : 2 * BLK, :] = lse
            top_ref[h] = o

        @pl.when(me != 0)
        def _():
            top_ref[h] = jnp.zeros((2 * BLK, pair), F32)

    finished()

    def drain(step, carry):
        shard_r, shard_l = me - step, me + step
        for h in range(heads):

            @pl.when((shard_r >= 0) & has_right)
            def _():
                copy_r(h, shard_r, step).wait_send()

            @pl.when((shard_l < count) & has_left)
            def _():
                copy_l(h, shard_l, step).wait_send()

        return carry

    lax.fori_loop(0, count, drain, 0)
    for h in range(heads):
        pltpu.make_async_copy(held[h], kv_ref.at[h], save.at[h]).wait()


def attend_outs(count, heads, tok):
    pair = 2 * HW
    shapes = [
        jax.ShapeDtypeStruct((tok, heads * pair), BF16),
        jax.ShapeDtypeStruct((heads, count * tok // BLK, BLK, pair), BF16),
        jax.ShapeDtypeStruct((tok, heads * pair), BF16),
        jax.ShapeDtypeStruct((heads, tok, 1), F32),
        jax.ShapeDtypeStruct((heads, 2 * BLK, pair), F32),
    ]
    specs = [anywhere() if i == 1 else whole(*a.shape) for i, a in enumerate(shapes)]
    return shapes, specs


def gather_scratch(count, heads, tok):
    return (
        [pltpu.VMEM((count * tok // BLK, BLK, 2 * HW), BF16)] * heads
        + [pltpu.SemaphoreType.DMA((heads,))]
        + [pltpu.SemaphoreType.DMA((heads, count))] * 4
    )


def scalars():
    return pl.BlockSpec(memory_space=pltpu.SMEM)


def begin_kernel(
    count,
    heads,
    ids_ref,
    len_ref,
    inputs_ref,
    wq_ref,
    wk_ref,
    wv_ref,
    win_ref,
    wffn_ref,
    wout_ref,
    bq_ref,
    bv_ref,
    bout_ref,
    g1_ref,
    b1_ref,
    bin_ref,
    bffn_ref,
    g2_ref,
    b2_ref,
    x_ref,
    q_ref,
    kv_ref,
    att_ref,
    lse_ref,
    top_ref,
    wt_ref,
    vall_ref,
    win_all_ref,
    wffn_all_ref,
    wout_all_ref,
    turn,
    x_sem,
    keep,
    send,
    recv,
    *scratch,
):
    section = lax.axis_index("section")
    other = {"section": 1 - section}
    barrier = wide_barrier(lax.axis_index("wide"), count)
    pl.semaphore_signal(barrier, inc=1, device_id=other, device_id_type=MESH)
    load = pltpu.make_async_copy(inputs_ref.at[section, 0], x_ref, x_sem)
    load.start()
    wide = heads * 2 * HW
    scale = jnp.asarray(0.125, BF16)
    none = jnp.zeros((HW, x_ref.shape[1]), BF16)
    row = []
    for h in range(heads):
        at, cut = h * 2 * HW, slice(h * HW, (h + 1) * HW)
        wt_ref[section, at : at + HW, :] = wq_ref[cut, :] * scale
        wt_ref[section, at + HW : at + 2 * HW, :] = none
        wt_ref[section, wide + at : wide + at + HW, :] = wk_ref[cut, :]
        wt_ref[section, wide + at + HW : wide + at + 2 * HW, :] = wv_ref[cut, :]
        row += [bq_ref[:, cut].astype(F32) * 0.125, jnp.zeros((1, HW), F32)]
    for h in range(heads):
        row += [jnp.zeros((1, HW), F32), bv_ref[:, h * HW : (h + 1) * HW].astype(F32)]
    vall_ref[section, 0:1, :] = jnp.concatenate(row, axis=1)
    for i, ref in enumerate((bout_ref, g1_ref, b1_ref, bin_ref, bffn_ref, g2_ref, b2_ref)):
        vall_ref[section, i + 1 : i + 2, :] = ref[...].astype(F32)
    pl.semaphore_wait(barrier, 3)

    pairs = [
        (wt_ref.at[section], wt_ref.at[section]),
        (vall_ref.at[section], vall_ref.at[section]),
        (win_ref, win_all_ref.at[section]),
        (wffn_ref, wffn_all_ref.at[section]),
        (wout_ref, wout_all_ref.at[section]),
    ]
    swaps = [remote(src, dst, send.at[i], recv.at[i], other) for i, (src, dst) in enumerate(pairs)]
    keeps = [
        pltpu.make_async_copy(src, dst, keep.at[i]) for i, (src, dst) in enumerate(pairs[2:])
    ]
    for copy in swaps + keeps:
        copy.start()
    load.wait()

    @pl.when(section == 1)
    def _():
        swaps[0].wait_recv()
        swaps[1].wait_recv()

    def ready():
        @pl.when(section == 1)
        def _():
            pl.semaphore_wait(turn, 1)

    def finished():
        @pl.when(section == 0)
        def _():
            pl.semaphore_signal(turn, inc=1, device_id={"section": 1}, device_id_type=MESH)

    gather_attend(
        count,
        heads,
        0,
        x_ref,
        wt_ref.at[0],
        vall_ref[0, 0:1, :],
        ids_ref,
        len_ref,
        (q_ref, kv_ref, att_ref, lse_ref, top_ref),
        scratch,
        ready,
        finished,
    )

    @pl.when(section == 0)
    def _():
        swaps[0].wait_recv()
        swaps[1].wait_recv()

    for copy in swaps[2:]:
        copy.wait_recv()
    for copy in swaps:
        copy.wait_send()
    for copy in keeps:
        copy.wait()


def begin(ids, length, inputs, matrices, vectors, count, heads, collective_id):
    _, _, tok, width = inputs.shape
    wide = heads * 2 * HW
    narrow = heads * HW
    both = [(2, width, width), (2, width, width), (2, narrow, width)]
    shapes, specs = attend_outs(count, heads, tok)
    return pl.pallas_call(
        functools.partial(begin_kernel, count, heads),
        grid=(1,),
        out_shape=[jax.ShapeDtypeStruct((tok, width), BF16)]
        + shapes
        + [
            jax.ShapeDtypeStruct((2, 2 * wide, width), BF16),
            jax.ShapeDtypeStruct((2, 8, width), F32),
        ]
        + [jax.ShapeDtypeStruct(shape, BF16) for shape in both],
        in_specs=[scalars(), scalars(), anywhere()]
        + [whole(*m.shape) for m in matrices]
        + [whole(*v.shape) for v in vectors],
        out_specs=[whole(tok, width)]
        + specs
        + [whole(2, 2 * wide, width), whole(2, 8, width)]
        + [anywhere()] * 3,
        scratch_shapes=[
            pltpu.SemaphoreType.REGULAR,
            pltpu.SemaphoreType.DMA,
            pltpu.SemaphoreType.DMA((3,)),
            pltpu.SemaphoreType.DMA((5,)),
            pltpu.SemaphoreType.DMA((5,)),
        ]
        + gather_scratch(count, heads, tok),
        compiler_params=params(collective_id),
        name="begin",
    )(ids, length, inputs, *matrices, *vectors)


def project_kernel(count, heads, layer, ids_ref, len_ref, x_ref, wt_ref, v_ref, *refs):
    barrier = wide_barrier(lax.axis_index("wide"), count)
    gather_attend(
        count,
        heads,
        layer,
        x_ref,
        wt_ref,
        v_ref[0:1, :],
        ids_ref,
        len_ref,
        refs[:5],
        refs[5:],
        lambda: pl.semaphore_wait(barrier, 2),
        lambda: None,
    )


def project(ids, length, x, wt, vall, layer, count, heads, collective_id):
    tok, width = x.shape
    shapes, specs = attend_outs(count, heads, tok)
    return pl.pallas_call(
        functools.partial(project_kernel, count, heads, layer),
        grid=(1,),
        out_shape=shapes,
        in_specs=[scalars(), scalars(), whole(tok, width), of_layer(wt, layer), of_layer(vall, layer)],
        out_specs=specs,
        scratch_shapes=gather_scratch(count, heads, tok),
        compiler_params=params(collective_id),
        name="project",
    )(ids, length, x, wt, vall)


class Square:
    def __init__(self, me, own, width, blocks, send_buf, recv_buf, hold, send_sem, recv_sem):
        self.me = me
        self.x, self.y, self.d = (tensor_peer(me, k) for k in (1, 2, 3))
        self.own, self.sub, self.half = own, own // blocks, width // 2
        self.blocks = blocks
        self.send_buf, self.recv_buf, self.hold = send_buf, recv_buf, hold
        self.send_sem, self.recv_sem = send_sem, recv_sem
        self.used = []

    def rows(self, index, j, size=None):
        return pl.ds(pl.multiple_of(index * self.own + j * self.sub, 16), size or self.sub)

    def to(self, m):
        return {"tensor": self.x if m < 3 else self.y}

    def scatter(self, stage, j, m):
        slot = self.scatters.index(stage)
        return remote(
            self.send_buf.at[slot, j, m],
            self.recv_buf.at[slot, j, m],
            self.send_sem.at[stage, j, m],
            self.recv_sem.at[stage, j, m],
            self.to(m),
        )

    def put(self, stage, j, m, value):
        self.send_buf[self.scatters.index(stage), j, m] = value.astype(BF16)
        self.scatter(stage, j, m).start()
        self.used.append(self.scatter(stage, j, m))

    def got(self, stage, j, m):
        self.scatter(stage, j, m).wait_recv()
        return self.recv_buf[self.scatters.index(stage), j, m].astype(F32)

    def give_diagonal(self, stage, j, part):
        self.put(stage, j, 0, part[:, self.half :])
        self.put(stage, j, 3, part[:, : self.half])

    def give_x(self, stage, j, part):
        self.put(stage, j, 1, part[:, self.half :])
        self.hold[j, 0] = part[:, : self.half]

    def give_y(self, stage, j, part):
        self.put(stage, j, 4, part[:, : self.half])
        self.hold[j, 1] = part[:, self.half :]

    def relay_sum(self, stage, j):
        self.put(stage, j, 2, self.hold[j, 0] + self.got(stage, j, 3))
        self.put(stage, j, 5, self.hold[j, 1] + self.got(stage, j, 0))

    def total(self, stage, j, own):
        left = own[:, : self.half] + self.got(stage, j, 4) + self.got(stage, j, 2)
        right = own[:, self.half :] + self.got(stage, j, 1) + self.got(stage, j, 5)
        return jnp.concatenate([left, right], axis=1)

    def gather(self, stage, j, m, ref, index, first):
        cols = pl.ds(0 if first else self.half, self.half)
        return remote(
            ref.at[self.rows(index, j), cols],
            ref.at[self.rows(index, j), cols],
            self.send_sem.at[stage, j, m],
            self.recv_sem.at[stage, j, m],
            self.to(m),
        )

    def send(self, copy):
        copy.start()
        self.used.append(copy)

    def share(self, stage, j, ref):
        for m, first in ((0, True), (3, False), (1, False), (4, True)):
            self.send(self.gather(stage, j, m, ref, self.me, first))

    def relay_share(self, stage, j, ref):
        self.gather(stage, j, 0, ref, self.x, True).wait_recv()
        self.send(self.gather(stage, j, 5, ref, self.x, True))
        self.gather(stage, j, 3, ref, self.y, False).wait_recv()
        self.send(self.gather(stage, j, 2, ref, self.y, False))

    def have_x(self, stage, j, ref):
        self.gather(stage, j, 1, ref, self.x, False).wait_recv()

    def have_y(self, stage, j, ref):
        self.gather(stage, j, 4, ref, self.y, True).wait_recv()

    def have_diagonal(self, stage, j, ref):
        self.gather(stage, j, 5, ref, self.d, True).wait_recv()
        self.gather(stage, j, 2, ref, self.d, False).wait_recv()

    def have_all(self, stage, j, ref):
        self.have_x(stage, j, ref)
        self.have_y(stage, j, ref)
        self.have_diagonal(stage, j, ref)

    def close(self):
        for copy in self.used:
            copy.wait_send()


def square_barrier(me):
    barrier = pltpu.get_barrier_semaphore()
    for offset in (1, 2):
        pl.semaphore_signal(
            barrier, inc=1, device_id={"tensor": tensor_peer(me, offset)}, device_id_type=MESH
        )
    return barrier


def sub_blocks(own):
    return 2 if own % 32 == 0 else 1


def square_scratch(scatters, stages, own, width):
    blocks = sub_blocks(own)
    buf = pltpu.VMEM((scatters, blocks, 6, own // blocks, width // 2), BF16)
    return [
        buf,
        buf,
        pltpu.VMEM((blocks, 2, own // blocks, width // 2), F32),
        pltpu.SemaphoreType.DMA((stages, blocks, 6)),
        pltpu.SemaphoreType.DMA((stages, blocks, 6)),
    ]


def norm_parts(values):
    center = values - jnp.mean(values, axis=-1, keepdims=True)
    rstd = lax.rsqrt(jnp.mean(center * center, axis=-1, keepdims=True) + EPS)
    return center * rstd, rstd


def dense_kernel(
    last,
    layer,
    att_ref,
    x_ref,
    wout_ref,
    v_ref,
    win_any,
    wffn_any,
    mixed_any,
    active_any,
    slope_any,
    r1_ref,
    r2_ref,
    out_ref,
    wout_pad,
    win_ref,
    wffn_ref,
    mixed_ref,
    active_ref,
    slope_ref,
    sems,
    *scratch,
):
    me = lax.axis_index("tensor")
    own, width = x_ref.shape[0] // 4, x_ref.shape[1]
    blocks = sub_blocks(own)
    barrier = square_barrier(me)
    sq = Square(me, own, width, blocks, *scratch)
    pad_heads(wout_ref, wout_pad)
    sq.scatters = (0, 2)
    loads = [
        pltpu.make_async_copy(src.at[layer], dst, sems.at[i])
        for i, (src, dst) in enumerate(((win_any, win_ref), (wffn_any, wffn_ref)))
    ]
    for load in loads:
        load.start()
    stores = [
        pltpu.make_async_copy(src, dst, sems.at[2 + i])
        for i, (src, dst) in enumerate(
            ((mixed_ref, mixed_any), (active_ref, active_any), (slope_ref, slope_any))
        )
    ]

    def local(j):
        return slice(j * sq.sub, (j + 1) * sq.sub)

    def branch(index, j):
        return dot(att_ref[sq.rows(index, j), :], wout_pad[...])

    for j in range(blocks):
        part = branch(sq.d, j)
        if j == 0:
            pl.semaphore_wait(barrier, 2)
        sq.give_diagonal(0, j, part)
    for j in range(blocks):
        sq.give_x(0, j, branch(sq.x, j))
        sq.give_y(0, j, branch(sq.y, j))
    for j in range(blocks):
        r1_ref[local(j), :] = (
            branch(me, j) + x_ref[sq.rows(me, j), :].astype(F32) + v_ref[1:2, :]
        )
        sq.relay_sum(0, j)
    for j in range(blocks):
        total = sq.total(0, j, r1_ref[local(j), :])
        r1_ref[local(j), :] = total
        mixed = (norm_parts(total)[0] * v_ref[2:3, :] + v_ref[3:4, :]).astype(BF16)
        mixed_ref[sq.rows(me, j), :] = mixed
        sq.share(1, j, mixed_ref)

    for load in loads:
        load.wait()

    def feed(index, j):
        here = sq.rows(index, j)
        u = dot(mixed_ref[here, :], win_ref[...]) + v_ref[4:5, :]
        th = jnp.tanh(GELU_C * (u + GELU_A * u * u * u))
        half = 0.5 * (1.0 + th)
        slope = half + 0.5 * u * (1.0 - th * th) * (GELU_C * (1.0 + 3.0 * GELU_A * u * u))
        slope_ref[here, :] = slope.astype(BF16)
        active = (u * half).astype(BF16)
        active_ref[here, :] = active
        return dot(active, wffn_ref[...])

    for j in range(blocks):
        r2_ref[local(j), :] = (
            feed(me, j) + mixed_ref[sq.rows(me, j), :].astype(F32) + v_ref[5:6, :]
        )
        sq.relay_share(1, j, mixed_ref)
    for j in range(blocks):
        sq.have_x(1, j, mixed_ref)
        sq.give_x(2, j, feed(sq.x, j))
        sq.have_y(1, j, mixed_ref)
        sq.give_y(2, j, feed(sq.y, j))
        sq.have_diagonal(1, j, mixed_ref)
        sq.give_diagonal(2, j, feed(sq.d, j))
    for store in stores:
        store.start()
    for j in range(blocks):
        sq.relay_sum(2, j)
    for j in range(blocks):
        total = sq.total(2, j, r2_ref[local(j), :])
        r2_ref[local(j), :] = total
        result = (norm_parts(total)[0] * v_ref[6:7, :] + v_ref[7:8, :]).astype(BF16)
        if last:
            out_ref[local(j), :] = result
        else:
            out_ref[sq.rows(me, j), :] = result
            sq.share(3, j, out_ref)
    if not last:
        for j in range(blocks):
            sq.relay_share(3, j, out_ref)
        for j in range(blocks):
            sq.have_all(3, j, out_ref)
    sq.close()
    for store in stores:
        store.wait()


def pad_heads(rows_ref, padded_ref):
    for h in range(rows_ref.shape[0] // HW):
        at = h * 2 * HW
        padded_ref[at : at + HW, :] = jnp.zeros((HW, rows_ref.shape[1]), rows_ref.dtype)
        padded_ref[at + HW : at + 2 * HW, :] = rows_ref[h * HW : (h + 1) * HW, :]


def dense(att, x, wout, win, wffn, vall, layer, collective_id):
    tok, width = x.shape
    own = tok // 4
    wide = att.shape[1]
    last = layer == 1
    out_rows = own if last else tok
    return pl.pallas_call(
        functools.partial(dense_kernel, last, layer),
        out_shape=[jax.ShapeDtypeStruct((tok, width), BF16)] * 3
        + [jax.ShapeDtypeStruct((own, width), F32)] * 2
        + [jax.ShapeDtypeStruct((out_rows, width), BF16)],
        grid=(1,),
        in_specs=[whole(tok, wide), whole(tok, width)]
        + [of_layer(a, layer) for a in (wout, vall)]
        + [anywhere()] * 2,
        out_specs=[anywhere()] * 3 + [whole(own, width)] * 2 + [whole(out_rows, width)],
        scratch_shapes=[
            pltpu.VMEM((wide, width), BF16),
            pltpu.VMEM((width, width), BF16),
            pltpu.VMEM((width, width), BF16),
            pltpu.VMEM((tok, width), BF16),
            pltpu.VMEM((tok, width), BF16),
            pltpu.VMEM((tok, width), BF16),
            pltpu.SemaphoreType.DMA((5,)),
        ]
        + square_scratch(2, 4, own, width),
        compiler_params=params(collective_id),
        name="dense",
    )(att, x, wout, vall, win, wffn)


def norm_back(values, grad, gain):
    n, rstd = norm_parts(values)
    f = grad * gain
    back = (
        f - jnp.mean(f, axis=-1, keepdims=True) - n * jnp.mean(f * n, axis=-1, keepdims=True)
    ) * rstd
    return back, n


def dense_back_kernel(
    count,
    with_chain,
    g_ref,
    weight_ref,
    r2_ref,
    r1_ref,
    wout_ref,
    v_ref,
    *refs,
):
    late_any, refs = refs[:6], refs[6:]
    if with_chain:
        old_any, gqkv_ref, refs = refs[0], refs[1], refs[2:]
    gw_ref, gv_ref, do_ref, dr1_ref = refs[:4]
    refs = refs[4:]
    if with_chain:
        up_ref, gqkv_sum, refs = refs[0], refs[1], refs[2:]
    late, late_sems = refs[:6], refs[6]
    wffn_ref, slope_ref, win_ref, active_ref, mixed_ref, att_ref = late
    refs = refs[7:]
    layer = 0 if with_chain else 1
    loads = [
        pltpu.make_async_copy(src.at[layer] if i in (0, 2) else src, dst, late_sems.at[i])
        for i, (src, dst) in enumerate(zip(late_any, late))
    ]
    for load in loads:
        load.start()
    db2, dh, db1, wout_pad, g_buf, g_sem = refs[:6]
    refs = refs[3:]
    me = lax.axis_index("tensor")
    wide_at = lax.axis_index("wide")
    section = lax.axis_index("section")
    own, width = r1_ref.shape
    wide = att_ref.shape[1]
    blocks = sub_blocks(own)
    barrier = square_barrier(me)
    sq = Square(me, own, width, blocks, *refs[3:8])
    sq.scatters = (1,)
    refs = refs[8:]
    if with_chain:
        old, old_sem, sems, landed, hand_sems, ready = refs
        line = Line(count)
        rows = old.shape[0]
        half = gqkv_sum.shape[0]

        def half_of(core):
            return pl.ds(pl.multiple_of(core * half, 16), half)

        def swap():
            return remote(
                gqkv_ref.at[half_of(1 - section)],
                landed,
                hand_sems.at[0],
                hand_sems.at[1],
                {"section": 1 - section},
            )

        load_old = pltpu.make_async_copy(
            old_any.at[pl.ds(pl.multiple_of(section * rows, 16), rows)], old, old_sem
        )
        load_old.start()
        for side in (1, count - 1):
            pl.semaphore_signal(
                barrier,
                inc=1,
                device_id={"wide": lax.rem(wide_at + side, count)},
                device_id_type=MESH,
            )

        def inwards(source):
            return remote(source, up_ref, sems.at[0], sems.at[1], line.inward)

    def down(values):
        return jnp.sum(values, axis=0, keepdims=True)

    def local(j):
        return slice(j * sq.sub, (j + 1) * sq.sub)

    if with_chain:

        def gradient(j):
            return g_ref[local(j), :].astype(F32)

    else:
        load = pltpu.make_async_copy(g_ref.at[section, 0, sq.rows(me, 0, own)], g_buf, g_sem)
        load.start()
        weight = weight_ref[section]
        count_all = jnp.sum(jnp.sum(weight, axis=1, keepdims=True), axis=0, keepdims=True)
        factor = (weight.shape[0] * weight.shape[1]) / count_all
        here = weight_ref[section, pl.ds(wide_at * 4 + me, 1), :]
        equal = lax.broadcasted_iota(jnp.int32, (own, own), 0) == lax.broadcasted_iota(
            jnp.int32, (own, own), 1
        )
        column = jnp.sum(jnp.where(equal, here, 0.0), axis=1, keepdims=True) * factor
        load.wait()

        def gradient(j):
            return g_buf[local(j), :].astype(F32) * column[local(j), :]

    pad_heads(wout_ref, wout_pad)
    d_gain, d_shift, d_bias = 0.0, 0.0, 0.0
    for j in range(blocks):
        grad = gradient(j)
        d_two, n_two = norm_back(r2_ref[local(j), :], grad, v_ref[6:7, :])
        db2[sq.rows(me, j), :] = d_two.astype(BF16)
        dr1_ref[local(j), :] = d_two
        if j == 0:
            if with_chain:
                greet(barrier, section, 4)
                tell_ready(ready, section)
            else:
                pl.semaphore_wait(barrier, 2)
        sq.share(0, j, db2)
        d_gain += down(grad * n_two)
        d_shift += down(grad)
        d_bias += down(d_two)
    gv_ref[6:7, :] = d_gain
    gv_ref[7:8, :] = d_shift
    gv_ref[5:6, :] = d_bias

    def feed(index, j):
        here = sq.rows(index, j)
        back = dot_nt(db2[here, :], wffn_ref[...]) * slope_ref[here, :].astype(F32)
        low = back.astype(BF16)
        dh[here, :] = low
        return dot_nt(low, win_ref[...])

    if with_chain:
        load_old.wait()

        @pl.when(line.no_outer)
        def _():
            inwards(old).start()

        @pl.when(section == 1)
        def _():
            swap().start()

    for load in loads[:3]:
        load.wait()
    for j in range(blocks):
        dr1_ref[local(j), :] += feed(me, j)
        sq.relay_share(0, j, db2)
    for j in range(blocks):
        sq.have_x(0, j, db2)
        sq.give_x(1, j, feed(sq.x, j))
        sq.have_y(0, j, db2)
        sq.give_y(1, j, feed(sq.y, j))
        sq.have_diagonal(0, j, db2)
        sq.give_diagonal(1, j, feed(sq.d, j))
    for j in range(blocks):
        sq.relay_sum(1, j)
    for load in loads[3:]:
        load.wait()
    step = 256
    for i in range(width // step):
        cols = slice(i * step, (i + 1) * step)
        gw_ref[width + i * step : width + (i + 1) * step, :] = dot_tn(
            active_ref[:, cols], db2[...]
        ).astype(BF16)
        gw_ref[cols, :] = dot_tn(mixed_ref[:, cols], dh[...]).astype(BF16)
    gv_ref[4:5, :] = down(dh[...].astype(F32))
    d_gain, d_shift, d_bias = 0.0, 0.0, 0.0
    for j in range(blocks):
        total = sq.total(1, j, dr1_ref[local(j), :])
        d_one, n_one = norm_back(r1_ref[local(j), :], total, v_ref[2:3, :])
        db1[sq.rows(me, j), :] = d_one.astype(BF16)
        sq.share(2, j, db1)
        dr1_ref[local(j), :] = d_one
        d_gain += down(total * n_one)
        d_shift += down(total)
        d_bias += down(d_one)
    gv_ref[2:3, :] = d_gain
    gv_ref[3:4, :] = d_shift
    gv_ref[1:2, :] = d_bias
    gv_ref[0:1, :] = jnp.zeros((1, width), F32)

    def attended_back(index, j):
        here = sq.rows(index, j)
        do_ref[here, :] = dot_nt(db1[here, :], wout_pad[...]).astype(BF16)

    for j in range(blocks):
        attended_back(me, j)
        sq.relay_share(2, j, db1)
    for j in range(blocks):
        sq.have_x(2, j, db1)
        attended_back(sq.x, j)
        sq.have_y(2, j, db1)
        attended_back(sq.y, j)
        sq.have_diagonal(2, j, db1)
        attended_back(sq.d, j)
    for h in range(wide // (2 * HW)):
        cols = slice(h * 2 * HW, (h + 1) * 2 * HW)
        gw_ref[2 * width + h * HW : 2 * width + (h + 1) * HW, :] = dot_tn(
            att_ref[:, cols], db1[...]
        )[HW:].astype(BF16)
    sq.close()
    if with_chain:
        await_ready(ready, section)

        @pl.when(section == 0)
        def _():
            swap().start()

        @pl.when(line.has_outer)
        def _():
            inwards(old).wait_recv()

            def add(i, carry):
                span = pl.ds(pl.multiple_of(i * PIECE, 16), PIECE)
                up_ref[span, :] = (up_ref[span, :].astype(F32) + old[span, :].astype(F32)).astype(BF16)
                return carry

            lax.fori_loop(0, rows // PIECE, add, 0)

        @pl.when(line.has_outer & line.not_middle)
        def _():
            inwards(up_ref).start()

        @pl.when(line.not_middle)
        def _():
            inwards(old).wait_send()

        swap().wait()
        gqkv_sum[...] = (
            gqkv_ref[half_of(section), :].astype(F32) + landed[...].astype(F32)
        ).astype(BF16)


def dense_back(
    g, weight, r2, r1, slope, active, mixed, att, wout, win, wffn, vall, layer, count, collective_id, old
):
    own, width = r1.shape
    tok, wide = att.shape
    gw_rows = 2 * width + wide // 2
    extra_out, extra_scratch = [], []
    if old:
        half = (old[0].shape[0] // 2, width)
        small = (old[1].shape[0] // 2, width)
        extra_out = [half, small]
        extra_scratch = [
            pltpu.VMEM(half, BF16),
            pltpu.SemaphoreType.DMA,
            pltpu.SemaphoreType.DMA((2,)),
            pltpu.VMEM(small, BF16),
            pltpu.SemaphoreType.DMA((2,)),
            pltpu.SemaphoreType.REGULAR,
        ]
    return pl.pallas_call(
        functools.partial(dense_back_kernel, count, bool(old)),
        out_shape=[
            jax.ShapeDtypeStruct((gw_rows, width), BF16),
            jax.ShapeDtypeStruct((8, width), F32),
            jax.ShapeDtypeStruct((tok, wide), BF16),
            jax.ShapeDtypeStruct((own, width), F32),
        ]
        + [jax.ShapeDtypeStruct(shape, BF16) for shape in extra_out],
        grid=(1,),
        in_specs=[whole(own, width) if old else anywhere(), whole(*weight.shape)]
        + [whole(own, width)] * 2
        + [of_layer(a, layer) for a in (wout, vall)]
        + [anywhere()] * 6
        + ([anywhere(), whole(*old[1].shape)] if old else []),
        out_specs=[
            whole(gw_rows, width),
            whole(8, width),
            whole(tok, wide),
            whole(own, width),
        ]
        + [whole(*shape) for shape in extra_out],
        scratch_shapes=[
            pltpu.VMEM((width, width), BF16),
            pltpu.VMEM((tok, width), BF16),
            pltpu.VMEM((width, width), BF16),
            pltpu.VMEM((tok, width), BF16),
            pltpu.VMEM((tok, width), BF16),
            pltpu.VMEM((tok, wide), BF16),
            pltpu.SemaphoreType.DMA((6,)),
            pltpu.VMEM((tok, width), BF16),
            pltpu.VMEM((tok, width), BF16),
            pltpu.VMEM((tok, width), BF16),
            pltpu.VMEM((wide, width), BF16),
            pltpu.VMEM((own, width), BF16),
            pltpu.SemaphoreType.DMA,
        ]
        + square_scratch(1, 3, own, width)
        + extra_scratch,
        compiler_params=params(collective_id),
        name="dense_back",
    )(g, weight, r2, r1, wout, vall, wffn, slope, win, active, mixed, att, *old)


def attend_back(h, layer, total, scalars_, refs, hook):
    ids_ref, len_ref, perm_ref, start_ref = scalars_
    q_ref, kv_ref, do_ref, lse_ref, top_ref, joined, dkv, acc, rand, sums = refs
    me = lax.axis_index("wide")
    pair = 2 * HW
    rows_here = q_ref.shape[0] // BLK
    unit = grouping(rows_here)
    cols = slice(h * pair, (h + 1) * pair)
    length = len_ref[0]
    first = me * rows_here
    acc[...] = jnp.zeros_like(acc)

    def group(g, carry):
        for u in range(unit):
            row = g * unit + u
            b = first + row
            here = pl.ds(pl.multiple_of(row * BLK, BLK), BLK)
            blocks, allowed = back_blocks(ids_ref, layer, h, b, total)
            keys = jnp.concatenate([kv_ref[h, k] for k in blocks], axis=0)
            keep = jnp.where((me == 0) & (row < 2), 0.0, 1.0).astype(BF16)
            do_here = do_ref[here, cols] * keep
            both = jnp.concatenate([q_ref[here, cols], do_here], axis=0)
            s_dp = dot_nt(both, keys)
            p = jnp.exp(s_dp[:BLK] + key_bias(blocks, allowed, length) - lse_ref[h, here, :])
            p_dp = p * s_dp[BLK:]
            ds = (p_dp - p * jnp.sum(p_dp, axis=-1, keepdims=True)).astype(BF16)
            joined[here, cols] = dot(ds, keys).astype(BF16)
            d_keys = dot_tn(jnp.concatenate([ds, p.astype(BF16)], axis=0), both)
            d_keys = d_keys.reshape(8, BLK, pair)
            acc[pl.ds(b, 3)] += d_keys[:3]
            acc[1:3] += d_keys[3:5]
            rand[pl.ds(row * 3, 3)] = d_keys[5:]
        hook(g)
        return carry

    lax.fori_loop(0, rows_here // unit, group, 0)

    @pl.when(me == 0)
    def _():
        top = slice(0, 2 * BLK)
        q_here, do_here = q_ref[top, cols], do_ref[top, cols]
        both = jnp.concatenate([q_here, do_here], axis=0)
        lse = lse_ref[h, top, :]
        delta = jnp.sum(do_here.astype(F32) * top_ref[h], axis=-1, keepdims=True)
        span = max(d for d in (16, 12, 8, 2) if total % d == 0)
        step = span * BLK

        def part(i, dq):
            keys = kv_ref[h, pl.ds(i * span, span)].reshape(step, pair)
            s_dp = dot_nt(both, keys)
            token = i * step + lax.broadcasted_iota(jnp.int32, (1, step), 1)
            p = jnp.exp(s_dp[: 2 * BLK] + jnp.where(token < length, 0.0, NEG) - lse)
            ds = (p * (s_dp[2 * BLK :] - delta)).astype(BF16)
            d_keys = dot_tn(jnp.concatenate([ds, p.astype(BF16)], axis=0), both)
            acc[pl.ds(1 + i * span, span)] += d_keys.reshape(span, BLK, pair)
            return dq + dot(ds, keys)

        dq = lax.fori_loop(0, total // span, part, jnp.zeros((2 * BLK, pair), F32))
        joined[top, cols] = dq.astype(BF16)

    sums[0] = jnp.zeros((BLK, pair), F32)

    def prefix(k, carry):
        carry = carry + rand[perm_ref[layer, h, k]]
        sums[k + 1] = carry
        return carry

    lax.fori_loop(0, rows_here * 3, prefix, jnp.zeros((BLK, pair), F32))
    several = 4 if total % 4 == 0 else 1

    def settle(i, carry):
        for u in range(several):
            j = i * several + u
            low, high = start_ref[layer, h, j], start_ref[layer, h, j + 1]
            dkv[h, j] = (acc[j + 1] + (sums[high] - sums[low])).astype(BF16)
        return carry

    lax.fori_loop(0, total // several, settle, 0)


def project_back_kernel(
    count,
    heads,
    owner,
    ids_ref,
    len_ref,
    perm_ref,
    start_ref,
    q_ref,
    kv_ref,
    do_ref,
    lse_ref,
    top_ref,
    dr1_ref,
    x_any,
    w_any,
    dense_any,
    extra_ref,
    *refs,
):
    if owner == 0:
        small_ref, refs = refs[0], refs[1:]
    gw_ref, gv_ref, dx_ref, both_ref, out_ref = refs[:5]
    refs = refs[5:]
    if owner == 0:
        small_done, refs = refs[0], refs[1:]
    result_ref, all_ref, part_any, done_ref = extra_ref, out_ref, extra_ref, out_ref
    x_ref, w_ref, dense_ref, load_sems, dkv, acc, rand, sums = refs[:8]
    handed, slots, joined, send_wide, recv_wide = refs[8:13]
    sq_send, sq_recv, sq_hold, sq_send_sem, sq_recv_sem, hand_sems, ready = refs[13:20]
    me = lax.axis_index("wide")
    mine = lax.axis_index("tensor")
    section = lax.axis_index("section")
    tok, width = x_ref.shape
    own = tok // 4
    pair = 2 * HW
    wide = heads * pair
    total = dkv.shape[1]
    rows_here = tok // BLK
    right, left = {"wide": lax.rem(me + 1, count)}, {"wide": lax.rem(me + count - 1, count)}
    loads = [
        pltpu.make_async_copy(src, dst, load_sems.at[i])
        for i, (src, dst) in enumerate(
            ((dense_any, dense_ref), (w_any.at[owner], w_ref), (x_any, x_ref))
        )
    ]
    for load in loads:
        load.start()
    barrier = wide_barrier(me, count)
    for offset in (1, 2):
        pl.semaphore_signal(
            barrier, inc=1, device_id={"tensor": tensor_peer(mine, offset)}, device_id_type=MESH
        )
    greet(barrier, section, 4)
    blocks = sub_blocks(own)
    sq = Square(mine, own, width, blocks, sq_send, sq_recv, sq_hold, sq_send_sem, sq_recv_sem)
    sq.scatters = (0,)
    split = dense_ref.shape[0] // 2 if owner == 1 else dense_ref.shape[0]
    low, high = pl.ds(0, split), pl.ds(split, dense_ref.shape[0] - split)

    def hand_over(rows, to):
        return remote(
            dense_ref.at[rows], handed.at[rows], hand_sems.at[0], hand_sems.at[1], {"section": to}
        )

    if owner == 0:
        part, cross, small_up, small_cross, part_sems, small_sems = refs[20:]
        line = Line(count)

        def small_in(source):
            return remote(source, small_up, small_sems.at[0], small_sems.at[1], line.inward)

        def small_across():
            return remote(small_up, small_cross, small_sems.at[2], small_sems.at[3], line.inward)

        def small_out():
            return remote(small_done, small_done, small_sems.at[4], small_sems.at[5], line.outward)

        load_part = pltpu.make_async_copy(part_any, part, part_sems.at[0])
        load_part.start()

        def across():
            return remote(part, cross, part_sems.at[1], part_sems.at[2], line.inward)

        def outwards():
            return remote(done_ref, done_ref, part_sems.at[3], part_sems.at[4], line.outward)

        load_part.wait()

        @pl.when(line.is_middle)
        def _():
            across().start()

        @pl.when(line.no_outer)
        def _():
            small_in(small_ref).start()

    loads[0].wait()

    @pl.when(section == 1)
    def _():
        hand_over(low, 0).start()

    if owner == 1:
        tell_ready(ready, section)
        for j in range(blocks):
            all_ref[sq.rows(mine, j), :] = result_ref[j * sq.sub : (j + 1) * sq.sub, :]
            sq.share(1, j, all_ref)
    has_right, has_left = me < count - 1, me > 0

    def keys(shard):
        return pl.ds(shard * rows_here, rows_here)

    def hop(side, shard, h):
        return remote(
            slots.at[side, shard, h],
            slots.at[side, shard, h],
            send_wide.at[side, shard, h],
            recv_wide.at[side, shard, h],
            right if side == 0 else left,
        )

    def pass_on(side, shard, h, more):
        @pl.when(more)
        def _():
            hop(side, shard, h).wait_recv()
            slots[side, shard, h] = (
                slots[side, shard, h].astype(F32) + dkv[h, keys(shard)].astype(F32)
            ).astype(BF16)

        @pl.when(jnp.logical_not(more))
        def _():
            slots[side, shard, h] = dkv[h, keys(shard)]

        hop(side, shard, h).start()

    def step(h, k):
        shard_r, shard_l = count - 1 - k, k

        def rightwards():
            @pl.when(shard_r > me)
            def _():
                pass_on(0, shard_r, h, has_left)

        def leftwards():
            @pl.when(shard_l < me)
            def _():
                pass_on(1, shard_l, h, has_right)

        @pl.when(me < count // 2)
        def _():
            rightwards()
            leftwards()

        @pl.when(me >= count // 2)
        def _():
            leftwards()
            rightwards()

    def steps(h, first):
        def one(k, carry):
            step(h, k)
            return carry

        lax.fori_loop(first, count - 1, one, 0)

    groups = rows_here // grouping(rows_here)
    state = (q_ref, kv_ref, do_ref, lse_ref, top_ref, joined, dkv, acc, rand, sums)
    for h in range(heads):

        def hook(g):
            if h > 0:

                @pl.when(g < count - 1)
                def _():
                    step(h - 1, g)

        attend_back(h, owner, total, (ids_ref, len_ref, perm_ref, start_ref), state, hook)
        if h > 0:
            steps(h - 1, groups)
        if owner == 0 and h == 0:

            @pl.when(line.has_outer)
            def _():
                small_in(small_ref).wait_recv()
                small_up[...] = (
                    small_up[...].astype(F32) + small_ref[...].astype(F32)
                ).astype(BF16)

            @pl.when(line.has_outer & line.is_middle)
            def _():
                small_across().start()

            @pl.when(line.has_outer & line.not_middle)
            def _():
                small_in(small_up).start()

        if owner == 0 and h == heads - 2:

            @pl.when(line.is_middle)
            def _():
                small_across().wait_recv()
                small_done[...] = (
                    small_up[...].astype(F32) + small_cross[...].astype(F32)
                ).astype(BF16)
                across().wait_recv()

                def add(i, carry):
                    span = pl.ds(pl.multiple_of(i * PIECE, 16), PIECE)
                    done_ref[span, :] = (
                        part[span, :].astype(F32) + cross[span, :].astype(F32)
                    ).astype(BF16)
                    return carry

                lax.fori_loop(0, part.shape[0] // PIECE, add, 0)

            @pl.when(line.is_middle & line.has_outer)
            def _():
                small_out().start()
                outwards().start()

    if owner == 1:

        @pl.when(section == 0)
        def _():
            pl.semaphore_wait(ready, 1)
            hand_over(high, 1).start()

    steps(heads - 1, 0)
    for load in loads[1:]:
        load.wait()

    def add_up(first, last):
        def add(i, carry):
            span = pl.ds(pl.multiple_of(i * PIECE, 16), PIECE)
            both_ref[span, :] = (
                dense_ref[span, :].astype(F32) + handed[span, :].astype(F32)
            ).astype(BF16)
            return carry

        lax.fori_loop(first, last, add, 0)

    @pl.when(section == 0)
    def _():
        hand_over(low, 0).wait_recv()
        add_up(0, split // PIECE)

    if owner == 1:

        @pl.when(section == 1)
        def _():
            hand_over(high, 1).wait_recv()
            add_up(split // PIECE, dense_ref.shape[0] // PIECE)

    for h in range(heads):
        cols = slice(wide + h * pair, wide + (h + 1) * pair)

        @pl.when(has_left)
        def _():
            hop(0, me, h).wait_recv()

        @pl.when(has_right)
        def _():
            hop(1, me, h).wait_recv()

        here = dkv[h, keys(me)].astype(F32)
        from_left = jnp.where(has_left, slots[0, me, h].astype(F32), 0.0)
        from_right = jnp.where(has_right, slots[1, me, h].astype(F32), 0.0)
        joined[:, cols] = (here + from_left + from_right).astype(BF16).reshape(tok, pair)

    if owner == 1:
        for j in range(blocks):
            sq.relay_share(1, j, all_ref)

    def back(index, j):
        return dot(joined[sq.rows(index, j), :], w_ref[...])

    for j in range(blocks):
        sq.give_diagonal(0, j, back(sq.d, j))
    for j in range(blocks):
        sq.give_x(0, j, back(sq.x, j))
        sq.give_y(0, j, back(sq.y, j))
    for j in range(blocks):
        sq.relay_sum(0, j)
    for h in range(heads):
        at = h * 2 * HW
        gw_ref[h * HW : (h + 1) * HW, :] = dot_tn(joined[:, at : at + 2 * HW], x_ref[...])[
            :HW
        ].astype(BF16)
        gw_ref[heads * HW + at : heads * HW + at + 2 * HW, :] = dot_tn(
            joined[:, wide + at : wide + at + 2 * HW], x_ref[...]
        ).astype(BF16)
    gv_ref[...] = jnp.sum(joined[...].astype(F32), axis=0, keepdims=True)
    for j in range(blocks):
        rows = slice(j * sq.sub, (j + 1) * sq.sub)
        total = sq.total(0, j, back(mine, j) + dr1_ref[rows, :]).astype(BF16)
        dx_ref[rows, :] = total
    if owner == 1:
        for j in range(blocks):
            sq.have_all(1, j, all_ref)
    sq.close()

    @pl.when(section == 1)
    def _():
        hand_over(low, 0).wait_send()

    if owner == 1:

        @pl.when(section == 0)
        def _():
            hand_over(high, 1).wait_send()

    if owner == 0:

        @pl.when(line.is_middle)
        def _():
            small_across().wait_send()
            across().wait_send()

        @pl.when(line.not_middle)
        def _():
            small_in(small_ref).wait_send()
            small_out().wait_recv()
            outwards().wait_recv()

        @pl.when(line.not_middle & line.has_outer)
        def _():
            small_out().start()
            outwards().start()

        @pl.when(line.has_outer)
        def _():
            small_out().wait_send()
            outwards().wait_send()

    def drain(k, carry):
        shard_r, shard_l = count - 1 - k, k
        for h in range(heads):

            @pl.when(shard_r > me)
            def _():
                hop(0, shard_r, h).wait_send()

            @pl.when(shard_l < me)
            def _():
                hop(1, shard_l, h).wait_send()

        return carry

    lax.fori_loop(0, count - 1, drain, 0)


def project_back(
    scalars_, q, kv, do, lse, top, x, dr1, wt, gw, extra, small, layer, count, collective_id
):
    tok, width = x.shape
    heads, total, _, pair = kv.shape
    own = tok // 4
    wide = heads * pair
    rows_here = tok // BLK
    operands = [q, kv, do, lse, top, dr1]
    out = (tok, width) if layer == 1 else extra.shape
    parts = []
    if layer == 0:
        parts = [pltpu.VMEM(out, BF16)] * 2 + [pltpu.VMEM(small[0].shape, BF16)] * 2
        parts += [pltpu.SemaphoreType.DMA((5,)), pltpu.SemaphoreType.DMA((6,))]
    return pl.pallas_call(
        functools.partial(project_back_kernel, count, heads, layer),
        out_shape=[
            jax.ShapeDtypeStruct((wide + wide // 2, width), BF16),
            jax.ShapeDtypeStruct((1, 2 * wide), F32),
            jax.ShapeDtypeStruct((own, width), BF16),
            jax.ShapeDtypeStruct(gw.shape, BF16),
        ]
        + [jax.ShapeDtypeStruct(out, BF16)]
        + [jax.ShapeDtypeStruct(a.shape, BF16) for a in small],
        grid=(1,),
        in_specs=[scalars()] * 4
        + [whole(*a.shape) for a in operands]
        + [anywhere()] * 3
        + [whole(own, width) if layer == 1 else anywhere()]
        + [whole(*a.shape) for a in small],
        out_specs=[
            whole(wide + wide // 2, width),
            whole(1, 2 * wide),
            whole(own, width),
            whole(*gw.shape),
        ]
        + [whole(*out)]
        + [whole(*a.shape) for a in small],
        scratch_shapes=[
            pltpu.VMEM((tok, width), BF16),
            pltpu.VMEM((2 * wide, width), BF16),
            pltpu.VMEM(gw.shape, BF16),
            pltpu.SemaphoreType.DMA((3,)),
            pltpu.VMEM((heads, total, BLK, pair), BF16),
            pltpu.VMEM((total + 2, BLK, pair), F32),
            pltpu.VMEM((rows_here * 3, BLK, pair), F32),
            pltpu.VMEM((rows_here * 3 + 1, BLK, pair), F32),
            pltpu.VMEM(gw.shape, BF16),
            pltpu.VMEM((2, count, heads, rows_here, BLK, pair), BF16),
            pltpu.VMEM((tok, 2 * wide), BF16),
            pltpu.SemaphoreType.DMA((2, count, heads)),
            pltpu.SemaphoreType.DMA((2, count, heads)),
        ]
        + square_scratch(1, 2, own, width)
        + [pltpu.SemaphoreType.DMA((2,)), pltpu.SemaphoreType.REGULAR]
        + parts,
        compiler_params=params(collective_id),
        name="project_back",
    )(*scalars_, *operands, x, wt, gw, extra, *small)


def greet(barrier, section, expected):
    @pl.when(section == 0)
    def _():
        pl.semaphore_signal(barrier, inc=1, device_id={"section": 1}, device_id_type=MESH)

    pl.semaphore_wait(barrier, expected + section)


def tell_ready(ready, section):
    @pl.when(section == 1)
    def _():
        pl.semaphore_signal(ready, inc=1, device_id={"section": 0}, device_id_type=MESH)


def await_ready(ready, section):
    @pl.when(section == 0)
    def _():
        pl.semaphore_wait(ready, 1)


class Line:
    def __init__(self, count):
        w = lax.axis_index("wide")
        middle = count // 2
        low = w < middle
        self.inward = {"wide": jnp.where(low, w + 1, w - 1)}
        self.outward = {"wide": lax.rem(jnp.where(low, w + count - 1, w + 1), count)}
        self.has_outer = (w > 0) & (w < count - 1)
        self.no_outer = (w == 0) | (w == count - 1)
        self.is_middle = (w == middle - 1) | (w == middle)
        self.not_middle = (w < middle - 1) | (w > middle)


class Chain:
    def __init__(self, count, section, owner, sect, up, done, sems, segments):
        self.sect, self.up, self.done = sect, up, done
        self.r_sect, self.s_in, self.r_up, self.r_done, self.s_out, self.s_sect = sems
        self.segments = segments
        w = lax.axis_index("wide")
        middle = count // 2
        low = w < middle
        self.inward = {"wide": jnp.where(low, w + 1, w - 1)}
        self.outward = {"wide": lax.rem(jnp.where(low, w + count - 1, w + 1), count)}
        self.has_outer = (w > 0) & (w < count - 1)
        self.no_outer = (w == 0) | (w == count - 1)
        self.is_middle = (w == middle - 1) | (w == middle)
        self.not_middle = (w < middle - 1) | (w > middle)
        self.owner, self.mine = owner, section == owner
        self.other = {"section": 1 - section}

    def span(self, i, base):
        return pl.ds(pl.multiple_of((i - base) * PIECE, 16), PIECE)

    def size(self):
        return sum(size for _, _, _, size, _ in self.segments)

    def first(self):
        return min(start for _, _, start, _, _ in self.segments)

    def handed(self, ref, i, base):
        return remote(
            ref.at[self.span(i, base)],
            self.sect.at[i],
            self.s_sect.at[i],
            self.r_sect.at[i],
            self.other,
        )

    def to_up(self, i):
        return remote(self.sect.at[i], self.up.at[i], self.s_in.at[i], self.r_up.at[i], self.inward)

    def to_middle(self, i):
        return remote(
            self.sect.at[i], self.done.at[i], self.s_in.at[i], self.r_done.at[i], self.inward
        )

    def to_outer(self, i):
        return remote(
            self.done.at[i], self.done.at[i], self.s_out.at[i], self.r_done.at[i], self.outward
        )

    def pieces(self, lo, hi, body):
        for ref, base, start, size, shared in self.segments:
            first, last = max(lo, start), min(hi, start + size)
            if first < last:

                def step(i, carry, ref=ref, base=base, shared=shared):
                    body(i, ref, base, shared)
                    return carry

                lax.fori_loop(first, last, step, 0)

    def hand_over(self):
        @pl.when(jnp.logical_not(self.mine))
        def _():
            def step(i, ref, base, shared):
                if shared:
                    self.handed(ref, i, base).start()

            self.pieces(0, 1 << 20, step)

    def add(self, i, ref, base, shared):
        value = ref[self.span(i, base), :].astype(F32)
        if shared:
            self.handed(ref, i, base).wait_recv()
            value += self.sect[i].astype(F32)
        return value

    def send_in(self, i):
        @pl.when(self.is_middle)
        def _():
            self.to_middle(i).start()

        @pl.when(self.not_middle)
        def _():
            self.to_up(i).start()

    def give(self, i, ref, base, shared):
        self.sect[i] = self.add(i, ref, base, shared).astype(BF16)
        self.send_in(i)

    def relay(self, i, ref, base, shared):
        value = self.add(i, ref, base, shared)
        self.to_up(i).wait_recv()
        self.sect[i] = (value + self.up[i].astype(F32)).astype(BF16)
        self.send_in(i)

    def settle(self, i, ref, base, shared):
        self.to_middle(i).wait_recv()

        @pl.when(self.is_middle)
        def _():
            self.done[i] = (self.sect[i].astype(F32) + self.done[i].astype(F32)).astype(BF16)

        @pl.when(self.has_outer)
        def _():
            self.to_outer(i).start()

    def inwards(self, lo, hi):
        @pl.when(self.mine & self.no_outer)
        def _():
            self.pieces(lo, hi, self.give)

        @pl.when(self.mine & self.has_outer)
        def _():
            for i in range(lo, hi):
                self.pieces(i, i + 1, self.relay)
                self.pieces(i - LAG, i - LAG + 1, self.settle)

    def rest(self):
        end = self.first() + self.size()

        @pl.when(self.mine & self.no_outer)
        def _():
            self.pieces(0, end, self.settle)

        @pl.when(self.mine & self.has_outer)
        def _():
            self.pieces(end - LAG, end, self.settle)

    def close(self):
        @pl.when(self.mine)
        def _():
            self.pieces(0, 1 << 20, lambda i, ref, base, shared: self.to_up(i).wait_send())

        @pl.when(self.mine & self.has_outer)
        def _():
            self.pieces(0, 1 << 20, lambda i, ref, base, shared: self.to_outer(i).wait_send())

        @pl.when(jnp.logical_not(self.mine))
        def _():
            def step(i, ref, base, shared):
                if shared:
                    self.handed(ref, i, base).wait_send()

            self.pieces(0, 1 << 20, step)


def chain_scratch(pieces, width):
    return [pltpu.VMEM((pieces, PIECE, width), BF16)] * 2 + [
        pltpu.SemaphoreType.DMA((pieces,))
    ] * 6


def finish_kernel(
    count,
    gqkv_ref,
    gw_ref,
    gvq0_ref,
    gv0_ref,
    gvq1_ref,
    gv1_ref,
    result_ref,
    dx_ref,
    old_ref,
    small_ref,
    done_ref,
    vout_ref,
    far_ref,
    all_ref,
    got_ref,
    got_small,
    vec_ref,
    sect,
    up,
    c0,
    c1,
    c2,
    c3,
    c4,
    c5,
    vsect,
    vtens,
    vup,
    vpart,
    vfin_in,
    vfin,
    vs,
    vr,
    ts,
    tr,
    far_sems,
    ready,
    *square,
):
    section = lax.axis_index("section")
    w = lax.axis_index("wide")
    t = lax.axis_index("tensor")
    barrier = wide_barrier(w, count)
    for offset in (1, 2, 3):
        pl.semaphore_signal(
            barrier, inc=1, device_id={"tensor": tensor_peer(t, offset)}, device_id_type=MESH
        )
    greet(barrier, section, 5)
    tell_ready(ready, section)
    own, width = dx_ref.shape
    blocks = sub_blocks(own)
    sq = Square(t, own, width, blocks, *square)
    sq.scatters = ()
    for at, gvq, gv in ((0, gvq0_ref, gv0_ref), (8, gvq1_ref, gv1_ref)):
        vec_ref[at : at + 1, :] = gvq[...]
        vec_ref[at + 1 : at + 8, :] = gv[1:8, :]
    gw_pieces = gw_ref.shape[0] // PIECE
    qkv_pieces = gqkv_ref.shape[0] // PIECE
    total = gw_pieces + qkv_pieces
    sems = (c0, c1, c2, c3, c4, c5)
    chain = Chain(
        count,
        section,
        0,
        sect,
        up,
        done_ref,
        sems,
        [(gw_ref, 0, 0, gw_pieces, False), (gqkv_ref, gw_pieces, gw_pieces, qkv_pieces, True)],
    )
    inward, outward, other = chain.inward, chain.outward, chain.other
    mine = pl.ds(pl.multiple_of(section * 8, 8), 8)
    theirs = pl.ds(pl.multiple_of(8 - section * 8, 8), 8)

    def v_other():
        return remote(vec_ref.at[theirs], vsect, vs.at[0], vr.at[0], other)

    def v_peer(offset, slot):
        return remote(
            vtens.at[t],
            vtens.at[slot],
            ts.at[offset - 1],
            tr.at[offset - 1],
            {"tensor": tensor_peer(t, offset)},
        )

    def v_up():
        return remote(vpart, vup, vs.at[1], vr.at[1], inward)

    def v_middle():
        return remote(vpart, vfin_in, vs.at[1], vr.at[2], inward)

    def v_outer():
        return remote(vfin, vfin_in, vs.at[2], vr.at[2], outward)

    chain.hand_over()

    def far(ref):
        return remote(ref, far_ref, far_sems.at[0], far_sems.at[1], other)

    def hand_small():
        return remote(small_ref, got_small, far_sems.at[4], far_sems.at[5], other)

    def hand_done():
        return remote(
            old_ref, got_ref, far_sems.at[2], far_sems.at[3], other
        )

    for j in range(blocks):
        all_ref[sq.rows(t, j), :] = dx_ref[j * sq.sub : (j + 1) * sq.sub, :]
        sq.share(0, j, all_ref)
    for j in range(blocks):
        sq.relay_share(0, j, all_ref)
    chain.inwards(0, gw_pieces)
    await_ready(ready, section)
    v_other().start()

    @pl.when(section == 0)
    def _():
        far(result_ref).start()
        hand_small().start()
        hand_done().start()

    v_other().wait_recv()
    vtens[t] = vec_ref[mine, :] + vsect[...]
    for offset in (1, 2, 3):
        v_peer(offset, t).start()
    chain.inwards(gw_pieces, total)
    for j in range(blocks):
        sq.have_all(0, j, all_ref)

    @pl.when(section == 1)
    def _():
        far(all_ref).start()

    for offset in (1, 2, 3):
        v_peer(offset, tensor_peer(t, offset)).wait_recv()
    shared = vtens[0] + vtens[1] + vtens[2] + vtens[3]
    row = lax.broadcasted_iota(jnp.int32, shared.shape, 0)
    value = jnp.where((row == 0) | (row == 4), vtens[t], shared)

    @pl.when(chain.has_outer)
    def _():
        v_up().wait_recv()
        vpart[...] = value + vup[...]

    @pl.when(chain.no_outer)
    def _():
        vpart[...] = value

    @pl.when(chain.is_middle)
    def _():
        v_middle().start()

    @pl.when(chain.not_middle)
    def _():
        v_up().start()

    chain.rest()
    v_middle().wait_recv()

    @pl.when(chain.is_middle)
    def _():
        vfin[...] = vpart[...] + vfin_in[...]

    @pl.when(chain.not_middle)
    def _():
        vfin[...] = vfin_in[...]

    @pl.when(chain.has_outer)
    def _():
        v_outer().start()

    vout_ref[...] = vfin[...]
    chain.close()
    sq.close()
    far(all_ref).wait()

    @pl.when(section == 0)
    def _():
        hand_small().wait_send()
        hand_done().wait_send()

    @pl.when(section == 1)
    def _():
        hand_small().wait_recv()
        hand_done().wait_recv()

    v_other().wait_send()
    v_up().wait_send()
    for offset in (1, 2, 3):
        v_peer(offset, t).wait_send()

    @pl.when(chain.has_outer)
    def _():
        v_outer().wait_send()


def finish(gqkv, gw, vectors, result, dx, old, small_old, count, collective_id):
    own, width = dx.shape
    tok = own * 4
    pieces = (gqkv.shape[0] + gw.shape[0]) // PIECE
    small = pltpu.VMEM((8, width), F32)
    operands = [gqkv, gw, *vectors, result, dx, old, small_old]
    return pl.pallas_call(
        functools.partial(finish_kernel, count),
        out_shape=[
            jax.ShapeDtypeStruct((pieces, PIECE, width), BF16),
            jax.ShapeDtypeStruct((8, width), F32),
            jax.ShapeDtypeStruct((tok, width), BF16),
            jax.ShapeDtypeStruct((tok, width), BF16),
            jax.ShapeDtypeStruct(old.shape, BF16),
            jax.ShapeDtypeStruct(small_old.shape, BF16),
        ],
        grid=(1,),
        in_specs=[whole(*a.shape) for a in operands],
        out_specs=[whole(pieces, PIECE, width), whole(8, width)]
        + [whole(tok, width)] * 2
        + [whole(*old.shape), whole(*small_old.shape)],
        scratch_shapes=[pltpu.VMEM((16, width), F32)]
        + chain_scratch(pieces, width)
        + [small, pltpu.VMEM((4, 8, width), F32)]
        + [small] * 4
        + [pltpu.SemaphoreType.DMA((3,))] * 4
        + [pltpu.SemaphoreType.DMA((6,)), pltpu.SemaphoreType.REGULAR]
        + square_scratch(1, 1, own, width),
        compiler_params=params(collective_id),
        name="finish",
    )(*operands)


def unpack_kernel(
    heads,
    sums_ref,
    low_ref,
    high_ref,
    low_small,
    high_small,
    dx_ref,
    result_ref,
    far_ref,
    vec_ref,
    ends_ref,
    gq_ref,
    gbq_ref,
    gk_ref,
    gv_ref,
    gbv_ref,
    go_ref,
    gbo_ref,
    g1_ref,
    b1_ref,
    gi_ref,
    gbi_ref,
    gf_ref,
    gbf_ref,
    g2_ref,
    b2_ref,
    buf,
    sems,
):
    section = lax.axis_index("section")
    width = gi_ref.shape[1]
    narrow = heads * HW
    wide = heads * 2 * HW
    half = low_ref.shape[0]
    low, high = pl.ds(0, half), pl.ds(half, half)
    few = low_small.shape[0]
    spans = (low, high, pl.ds(2 * half, few), pl.ds(2 * half + few, few))
    targets = tuple(buf.at[span] for span in spans)
    targets += (ends_ref.at[0, 0, 0], ends_ref.at[0, 1, 0])

    def copy(i, source):
        return pltpu.make_async_copy(source, targets[i], sems.at[i])

    @pl.when(section == 0)
    def _():
        for i, source in enumerate(
            tuple(sums_ref.at[span] for span in spans) + (dx_ref, far_ref)
        ):
            copy(i, source).start()

    @pl.when(section != 0)
    def _():
        for i, source in enumerate(
            (low_ref, high_ref, low_small, high_small, far_ref, result_ref)
        ):
            copy(i, source).start()

    for i, ref in (
        (1, gbo_ref),
        (2, g1_ref),
        (3, b1_ref),
        (4, gbi_ref),
        (5, gbf_ref),
        (6, g2_ref),
        (7, b2_ref),
    ):
        ref[...] = vec_ref[i : i + 1, :]
    row = vec_ref[0:1, :]
    cuts = [(h * 2 * HW, wide + h * 2 * HW + HW) for h in range(heads)]
    gbq_ref[...] = 0.125 * jnp.concatenate([row[:, q : q + HW] for q, _ in cuts], axis=1)
    gbv_ref[...] = jnp.concatenate([row[:, v : v + HW] for _, v in cuts], axis=1)
    for i, source in enumerate((low_ref, high_ref, low_small, high_small)):
        copy(i, source).wait()

    def take(out, scale, source, size):
        value = buf[source : source + size, :].astype(F32)
        out(0, size, value if scale is None else scale * value)

    def into(ref, first=0):
        def put(at, span, value):
            ref[0, first + at : first + at + span, :] = value

        return put

    take(into(gi_ref), None, 0, width)
    take(into(gf_ref), None, width, width)
    take(into(go_ref), None, 2 * width, narrow)
    take(into(gq_ref), 0.125, 2 * width + narrow, narrow)
    for h in range(heads):
        source = 2 * width + 2 * narrow + h * 2 * HW
        take(into(gk_ref, h * HW), None, source, HW)
        take(into(gv_ref, h * HW), None, source + HW, HW)
    for i in (4, 5):
        copy(i, far_ref).wait()


def unpack(sums, low, high, low_small, high_small, dx, result, far, vec, heads):
    rows, width = sums.shape
    narrow = heads * HW
    ends = jax.ShapeDtypeStruct((1, 2, 1) + dx.shape, BF16)
    slim = jax.ShapeDtypeStruct((1, narrow, width), F32)
    full = jax.ShapeDtypeStruct((1, width, width), F32)
    line = jax.ShapeDtypeStruct((1, width), F32)
    short = jax.ShapeDtypeStruct((1, narrow), F32)
    shapes = [ends, slim, short, slim, slim, short, slim, line, line, line]
    shapes += [full, line, full, line, line, line]
    return pl.pallas_call(
        functools.partial(unpack_kernel, heads),
        out_shape=shapes,
        grid=(1,),
        in_specs=[anywhere()] * 8 + [whole(*vec.shape)],
        out_specs=[whole(*a.shape) for a in shapes],
        scratch_shapes=[pltpu.VMEM((rows, width), BF16), pltpu.SemaphoreType.DMA((6,))],
        compiler_params=params(),
        name="unpack",
    )(sums, low, high, low_small, high_small, dx, result, far, vec)


def body(
    inputs,
    target,
    pad_mask,
    loss_mask,
    rand_blocks,
    w_query,
    b_query,
    w_key,
    w_value,
    b_value,
    w_out,
    b_out,
    ln1_gain,
    ln1_bias,
    w_in,
    b_in,
    w_ffn,
    b_ffn,
    ln2_gain,
    ln2_bias,
):
    section = lax.axis_index("section")
    count = lax.axis_size("wide")
    micro, _, tok, width = inputs.shape
    total = pad_mask.shape[2] // BLK
    heads = w_query.shape[2] // HW
    wide = heads * 2 * HW

    rand = rand_blocks[0].reshape(heads, -1)
    far_rand = lax.ppermute(rand, "section", [(0, 1), (1, 0)])
    ids = jnp.where(section == 0, jnp.stack([rand, far_rand]), jnp.stack([far_rand, rand]))
    here = lax.dynamic_slice_in_dim(ids, lax.axis_index("wide") * (tok // BLK * 3), tok // BLK * 3, 2)
    slot = jnp.arange(here.shape[2], dtype=jnp.int32)
    order = here * here.shape[2] + slot
    rank = jnp.sum((order[..., None, :] < order[..., :, None]).astype(jnp.int32), axis=-1)
    perm = jnp.sum(jnp.where(rank[..., None, :] == slot[:, None], slot, 0), axis=-1)
    block = jnp.arange(total + 1, dtype=jnp.int32)
    starts = jnp.sum((here[..., None, :] < block[:, None]).astype(jnp.int32), axis=-1)
    weight = (loss_mask * pad_mask).astype(F32).reshape(micro, -1, tok // 4)
    length = jnp.sum(lax.dynamic_index_in_dim(pad_mask, section, 0), axis=(0, 1, 2))[None]
    matrices = [jnp.swapaxes(m, 1, 2)[0] for m in (w_query, w_key, w_value)]
    matrices += [w_in[0], w_ffn[0], w_out[0]]
    vectors = [b_query, b_value, b_out, ln1_gain, ln1_bias, b_in, b_ffn, ln2_gain, ln2_bias]
    x, q, kv, att, lse, top, wt, vall, win, wffn, wout = begin(
        ids, length, inputs, matrices, vectors, count, heads, 2
    )

    saved = []
    for layer in range(2):
        if layer == 1:
            q, kv, att, lse, top = project(ids, length, x, wt, vall, layer, count, heads, 3)
        mixed, active, slope, r1, r2, x_next = dense(
            att, x, wout, win, wffn, vall, layer, 4 + layer
        )
        saved.append((x, q, kv, att, lse, top, mixed, active, slope, r1, r2))
        x = x_next
    result, grad, handed, vector_grads = x, target, (), [None, None]
    for layer in (1, 0):
        x, q, kv, att, lse, top, mixed, active, slope, r1, r2 = saved[layer]
        gw, gv, do, dr1, *middle = dense_back(
            grad,
            weight,
            r2,
            r1,
            slope,
            active,
            mixed,
            att,
            wout,
            win,
            wffn,
            vall,
            layer,
            count,
            6 + layer,
            handed,
        )
        scalars_ = (ids, length, perm, starts)
        extra, small = (result, []) if layer == 1 else (middle[0], [middle[1]])
        gqkv, gvq, grad, gw_both, out, *small_done = project_back(
            scalars_, q, kv, do, lse, top, x, dr1, wt, gw, extra, small, layer, count, 8 + layer
        )
        vector_grads[layer] = [gvq, gv]
        if layer == 1:
            handed, result = (gw_both, gqkv), out

    vectors = vector_grads[0] + vector_grads[1]
    sums, vec, far, dx, low, low_small = finish(
        gqkv, gw_both, vectors, result, grad, out, small_done[0], count, 10
    )
    ends, gq, gbq, gk, gvalue, gbv, gout, *rest = unpack(
        sums.reshape(-1, width), low, out, low_small, small_done[0], dx, result, far, vec, heads
    )
    return (
        ends,
        jnp.swapaxes(gq, 1, 2),
        gbq,
        jnp.swapaxes(gk, 1, 2),
        jnp.swapaxes(gvalue, 1, 2),
        gbv,
        gout,
        *rest,
    )


def solution(mesh):
    matrix = P("section", None, "tensor")
    rowwise = P("section", "tensor", None)
    cut = P("section", "tensor")
    plain = P("section", None)
    return jax.shard_map(
        body,
        mesh=mesh,
        in_specs=(
            P(None, None, "wide", None),
            P(None, None, "wide", None),
            P(),
            P(),
            P("section", "tensor", None, None),
            matrix,
            cut,
            matrix,
            matrix,
            cut,
            rowwise,
            plain,
            plain,
            plain,
            matrix,
            cut,
            rowwise,
            plain,
            plain,
            plain,
        ),
        out_specs=(
            P("section", None, None, "wide", None),
            matrix,
            cut,
            matrix,
            matrix,
            cut,
            rowwise,
            plain,
            plain,
            plain,
            matrix,
            cut,
            rowwise,
            plain,
            plain,
            plain,
        ),
        check_vma=False,
    )
```
